32 devices in a mesh: seq: 2 (over x), head: 4 (over z), dp: 4 (over y, core).
Axes of the slice: x: 2, y: 2, z: 4, core: 2. Of those that a mesh axis runs over, the one named last changes fastest.
Arguments:
- layer_input: bfloat16 [4, 1024, 2048], P('dp', 'seq'), may hold values from -6 to 6
- w_query: bfloat16 [2048, 2048], P(None, 'head'), may hold values from -0.125 to 0.125
- w_key: bfloat16 [2048, 2048], P(None, 'head'), may hold values from -0.125 to 0.125
- w_value: bfloat16 [2048, 2048], P(None, 'head'), may hold values from -0.125 to 0.125
- w_out: bfloat16 [2048, 2048], P('head'), may hold values from -0.125 to 0.125
- out_grad: bfloat16 [4, 1024, 2048], P('dp', 'seq'), may hold values from -6 to 6
Outputs:
- input_grad: bfloat16 [4, 1024, 2048], P('dp', 'seq', 'head')
- grad_query: float32 [2048, 2048], P(('seq', 'dp'), 'head')
- grad_key: float32 [2048, 2048], P(('seq', 'dp'), 'head')
- grad_value: float32 [2048, 2048], P(('seq', 'dp'), 'head')
- grad_out: float32 [2048, 2048], P('head', ('seq', 'dp'))
The draws below stay inside these ranges and needn't reach their ends.
All inputs are finite; a program needn't handle non-finite values.
Results may differ from the reference program's by a relative error of at most 0.0073.
Values sent between devices are 32-bit elements; how exact they have to be, the bound alone decides.
No kernel may reach another device: no remote copies, remote signals or barrier semaphores. Data moves between devices by JAX's collectives and lax.ppermute only.
A program may use at most 128 MiB of HBM per device.

```python
import jax
import jax.numpy as jnp
from jax import lax

D = 2048
HEADS = 16
HEAD_DIM = 128
TOK_DEV = 512
SEQS = 4
LENGTH = 1024
HD = 2048
N_SEQ = 2


def raised(entries, rng, source, target, shards_of, factor):
    def block_of(axis_at):
        return (jnp.arange(entries.shape[axis_at]) // (entries.shape[axis_at] // shards_of)).reshape((-1,) + (1,) * (entries.ndim - 1 - axis_at))

    near = jax.random.permutation(rng, shards_of)[block_of(target)]
    other_side = (block_of(target) + shards_of // 2) % shards_of
    return jnp.where((block_of(source) == near) | (block_of(source) == other_side), factor * entries, entries)


def block_levels(key, dims, cuts, low, high):
    def one(axis_at, parts):
        draws = jax.random.uniform(jax.random.fold_in(jax.random.fold_in(key, 6), axis_at), (parts,), jnp.float32, low / len(cuts), high / len(cuts))
        return jnp.repeat(jnp.exp(draws), dims[axis_at] // parts).reshape((-1,) + (1,) * (len(dims) - axis_at - 1))

    factor_of = one(*cuts[0])
    for cut in cuts[1:]:
        factor_of = factor_of * one(*cut)
    return factor_of


def gaussian(key, extent, width, bound, pieces=(), held_as=jnp.bfloat16):
    factor_of = block_levels(key, extent, pieces, -0.22, 0.18) if pieces else 1.0
    drawn = jax.random.normal(key, extent, jnp.float32) * width * factor_of
    return jnp.minimum(jnp.maximum(drawn, -bound), bound).astype(held_as)


def noise_with(key, shape, width, reach, shards, heavy, kind=jnp.bfloat16):
    drawn = width * jax.random.normal(key, shape, jnp.float32)
    if shards:
        drawn = drawn * block_levels(key, shape, shards, -0.22, 0.18)
    return jnp.clip(raised(drawn, jax.random.fold_in(key, 3), *heavy), -reach, reach).astype(kind)


def setup_inputs(seed: int = 0) -> dict:
    key_of = jax.random.split(jax.random.key(seed), 7)
    layer_input = noise_with(key_of[0], (SEQS, LENGTH, D), 1.0, 6.0, ((0, 4), (1, 2)), (1, 2, 2, 2.0))
    w_query = gaussian(key_of[1], (D, HD), D ** -0.5, 0.125, ((1, 4),))
    w_key = gaussian(key_of[2], (D, HD), D ** -0.5, 0.125, ((1, 4),))
    w_value = gaussian(key_of[3], (D, HD), D ** -0.5, 0.125, ((1, 4),))
    w_out = gaussian(key_of[4], (HD, D), HD ** -0.5, 0.125, ((0, 4),))
    out_grad = noise_with(key_of[5], (SEQS, LENGTH, D), 1.0, 6.0, ((0, 4), (1, 2)), (1, 2, 2, 2.0))
    return dict(layer_input=layer_input, w_query=w_query, w_key=w_key, w_value=w_value, w_out=w_out, out_grad=out_grad)


def widen_float(array_in):
    return array_in.astype(jnp.float32)

def reference(layer_input, w_query, w_key, w_value, w_out, out_grad):
    precise = lax.Precision.HIGHEST
    num_blocks = N_SEQ
    block_len = TOK_DEV
    in_rows = layer_input.reshape(-1, D)
    grad_rows = out_grad.reshape(-1, D)

    def project(weight):
        result = jnp.dot(in_rows, weight, preferred_element_type=jnp.float32).astype(jnp.bfloat16)
        return result.reshape(SEQS, num_blocks, block_len, HEADS, HEAD_DIM)
    queries = project(w_query)
    key_rows = project(w_key)
    value_rows = project(w_value)
    positions = jnp.arange(LENGTH, dtype=jnp.float32)
    pos_scale = (1.0 / jnp.sqrt(HEAD_DIM * (positions + 1.0))).reshape(num_blocks, block_len)
    backward = jnp.dot(grad_rows, w_out.T, preferred_element_type=jnp.float32).reshape(SEQS, num_blocks, block_len, HEADS, HEAD_DIM)
    grad_in = (backward * pos_scale[None, :, :, None, None]).astype(jnp.bfloat16)
    kv_state = jnp.einsum('bntkd,bntke->bnkde', widen_float(key_rows), widen_float(value_rows), precision=precise)
    qg_state = jnp.einsum('bntkd,bntke->bnkde', widen_float(queries), widen_float(grad_in), precision=precise)
    prefix = (jnp.cumsum(kv_state, axis=1) - kv_state).astype(jnp.bfloat16)
    suffix = (lax.optimization_barrier(jnp.sum(qg_state, axis=1, keepdims=True)) - jnp.cumsum(qg_state, axis=1)).astype(jnp.bfloat16)
    causal = jnp.arange(block_len)[:, None] >= jnp.arange(block_len)[None, :]

    def one_block(block_item):
        q_block, k_block, v_block, g_block, p_block, r_block, s_block = block_item
        scores = jnp.einsum('thd,shd->hts', widen_float(q_block), widen_float(k_block), precision=precise)
        scores_qk = jnp.where(causal[None], scores, 0.0).astype(jnp.bfloat16)
        scores_g = jnp.einsum('thd,shd->hts', widen_float(g_block), widen_float(v_block), precision=precise)
        scores_gv = jnp.where(causal[None], scores_g, 0.0).astype(jnp.bfloat16)
        inner_sum = jnp.einsum('hts,she->the', widen_float(scores_qk), widen_float(v_block), precision=precise)
        cross_sum = jnp.einsum('thd,hde->the', widen_float(q_block), widen_float(p_block), precision=precise)
        attention = ((inner_sum + cross_sum) * s_block[:, None, None]).astype(jnp.bfloat16)
        d_query = jnp.einsum('hts,shd->thd', widen_float(scores_gv), widen_float(k_block), precision=precise) + jnp.einsum('the,hde->thd', widen_float(g_block), widen_float(p_block), precision=precise)
        d_keys = jnp.einsum('hts,thd->shd', widen_float(scores_gv), widen_float(q_block), precision=precise) + jnp.einsum('she,hde->shd', widen_float(v_block), widen_float(r_block), precision=precise)
        d_values = jnp.einsum('hts,the->she', widen_float(scores_qk), widen_float(g_block), precision=precise) + jnp.einsum('shd,hde->she', widen_float(k_block), widen_float(r_block), precision=precise)
        return (attention, d_query.astype(jnp.bfloat16), d_keys.astype(jnp.bfloat16), d_values.astype(jnp.bfloat16))
    item_count = SEQS * num_blocks
    all_scales = jnp.broadcast_to(pos_scale[None], (SEQS, num_blocks, block_len)).reshape(item_count, block_len)
    block_items = (queries.reshape(item_count, block_len, HEADS, HEAD_DIM), key_rows.reshape(item_count, block_len, HEADS, HEAD_DIM), value_rows.reshape(item_count, block_len, HEADS, HEAD_DIM), grad_in.reshape(item_count, block_len, HEADS, HEAD_DIM), prefix.reshape(item_count, HEADS, HEAD_DIM, HEAD_DIM), suffix.reshape(item_count, HEADS, HEAD_DIM, HEAD_DIM), all_scales)
    attention, d_query, d_keys, d_values = lax.map(one_block, block_items)
    attention = attention.reshape(-1, HD)
    d_query = d_query.reshape(-1, HD)
    d_keys = d_keys.reshape(-1, HD)
    d_values = d_values.reshape(-1, HD)
    summed_in = jnp.dot(d_query, w_query.T, preferred_element_type=jnp.float32)
    summed_in = summed_in + jnp.dot(d_keys, w_key.T, preferred_element_type=jnp.float32)
    summed_in = summed_in + jnp.dot(d_values, w_value.T, preferred_element_type=jnp.float32)
    input_grad = summed_in.astype(jnp.bfloat16).reshape(SEQS, LENGTH, D)
    grad_scale = jnp.float32(1.0) / jnp.sqrt(jnp.float32(SEQS * LENGTH))
    in_rows_t = in_rows.T
    grad_query = jnp.dot(in_rows_t, d_query, preferred_element_type=jnp.float32) * grad_scale
    grad_key = jnp.dot(in_rows_t, d_keys, preferred_element_type=jnp.float32) * grad_scale
    grad_value = jnp.dot(in_rows_t, d_values, preferred_element_type=jnp.float32) * grad_scale
    grad_out = jnp.dot(attention.T, grad_rows, preferred_element_type=jnp.float32) * grad_scale
    return (input_grad, grad_query, grad_key, grad_value, grad_out)
```

```python
import functools

import jax
import jax.numpy as jnp
from jax import lax
from jax.experimental import pallas as pl
from jax.experimental.pallas import tpu as pltpu
from jax.sharding import PartitionSpec as P

HEAD_DIM = 128
BF16 = jnp.bfloat16
F32 = jnp.float32
VMEM_LIMIT = 48 * 1024 * 1024
NN = ((1,), (0,))
NT = ((1,), (1,))
TN = ((0,), (0,))


def dot(a, b, dims):
    return lax.dot_general(a, b, (dims, ((), ())), preferred_element_type=F32)


def shaped(shape, dtype):
    return jax.ShapeDtypeStruct(shape, dtype)


def position_scale(start, rows):
    positions = (start + lax.broadcasted_iota(jnp.int32, (rows, 1), 0)).astype(F32)
    return 1.0 / jnp.sqrt(HEAD_DIM * (positions + 1.0))


def project_kernel(
    seq_ref, x_hbm, o_hbm, wq_hbm, wk_hbm, wv_hbm, wo_hbm,
    q_ref, k_ref, v_ref, g_ref, *rest, one_state,
):
    states, (x_ref, o_ref, wq_ref, wk_ref, wv_ref, wo_ref, sems) = rest[:-7], rest[-7:]
    rows, hd = q_ref.shape
    pairs = (
        (x_hbm, x_ref), (wk_hbm, wk_ref), (wv_hbm, wv_ref),
        (wq_hbm, wq_ref), (o_hbm, o_ref), (wo_hbm, wo_ref),
    )
    copies = [pltpu.make_async_copy(a, b, sems.at[i]) for i, (a, b) in enumerate(pairs)]
    for c in copies[:3]:
        c.start()
    copies[0].wait()
    copies[1].wait()
    for c in copies[3:]:
        c.start()
    k_ref[...] = dot(x_ref[...], wk_ref[...], NN).astype(BF16)
    copies[2].wait()
    v_ref[...] = dot(x_ref[...], wv_ref[...], NN).astype(BF16)
    copies[3].wait()
    q_ref[...] = dot(x_ref[...], wq_ref[...], NN).astype(BF16)
    copies[4].wait()
    copies[5].wait()
    scale = position_scale(seq_ref[0] * rows, rows)
    g_ref[...] = (dot(o_ref[...], wo_ref[...], NT) * scale).astype(BF16)

    def state(a_ref, b_ref, out_ref):
        for h in range(hd // HEAD_DIM):
            at = pl.ds(h * HEAD_DIM, HEAD_DIM)
            out_ref[h] = dot(a_ref[:, at], b_ref[:, at], TN)

    if one_state:

        @pl.when(seq_ref[0] == 0)
        def _():
            state(k_ref, v_ref, states[0])

        @pl.when(seq_ref[0] != 0)
        def _():
            state(q_ref, g_ref, states[0])

    else:
        state(k_ref, v_ref, states[0])
        state(q_ref, g_ref, states[1])


def project(seq_at, in_rows, grad_rows, w_query, w_key, w_value, w_out, one_state):
    rows, width = in_rows.shape
    hd = w_query.shape[1]
    n_states = 1 if one_state else 2
    anywhere = pl.BlockSpec(memory_space=pl.ANY)
    return pl.pallas_call(
        functools.partial(project_kernel, one_state=one_state),
        out_shape=[shaped((rows, hd), BF16)] * 4
        + [shaped((hd // HEAD_DIM, HEAD_DIM, HEAD_DIM), F32)] * n_states,
        in_specs=[pl.BlockSpec(memory_space=pltpu.SMEM)] + [anywhere] * 6,
        out_specs=[pl.BlockSpec(memory_space=pltpu.VMEM)] * (4 + n_states),
        scratch_shapes=[
            pltpu.VMEM((rows, width), BF16),
            pltpu.VMEM((rows, width), BF16),
            pltpu.VMEM((width, hd), BF16),
            pltpu.VMEM((width, hd), BF16),
            pltpu.VMEM((width, hd), BF16),
            pltpu.VMEM((hd, width), BF16),
            pltpu.SemaphoreType.DMA((6,)),
        ],
        compiler_params=pltpu.CompilerParams(vmem_limit_bytes=VMEM_LIMIT),
        cost_estimate=pl.CostEstimate(
            flops=8 * rows * width * hd, bytes_accessed=12 * 2**20, transcendentals=0
        ),
        name="project",
    )(seq_at.reshape(1), in_rows, grad_rows, w_query, w_key, w_value, w_out)


def attend_kernel(
    flags_ref, q_ref, k_ref, v_ref, g_ref, pre_ref, suf_ref,
    first_ref, second_ref, first16_ref, second16_ref,
):
    q, k, v, g = q_ref[...], k_ref[...], v_ref[...], g_ref[...]
    rows = q.shape[0]
    half = rows // 2
    top, low = slice(0, half), slice(half, rows)
    prefix = jnp.where(flags_ref[1] != 0, pre_ref[0], 0.0).astype(BF16)
    suffix = jnp.where(flags_ref[2] != 0, suf_ref[0], 0.0).astype(BF16)

    def causal(a, b):
        r = lax.broadcasted_iota(jnp.int32, (half, half), 0)
        c = lax.broadcasted_iota(jnp.int32, (half, half), 1)
        diagonal = r >= c
        s00 = jnp.where(diagonal, dot(a[top], b[top], NT), 0.0).astype(BF16)
        s10 = dot(a[low], b[top], NT).astype(BF16)
        s11 = jnp.where(diagonal, dot(a[low], b[low], NT), 0.0).astype(BF16)
        return s00, s10, s11

    def forward(s, b):
        s00, s10, s11 = s
        return (dot(s00, b[top], NN), dot(s10, b[top], NN) + dot(s11, b[low], NN))

    def backward(s, a):
        s00, s10, s11 = s
        return (dot(s00, a[top], TN) + dot(s10, a[low], TN), dot(s11, a[low], TN))

    def put(out_ref, out16_ref, at, halves, cross, scale=None):
        for rows_at, inner in zip((top, low), halves):
            value = inner + cross[rows_at]
            if scale is not None:
                value = value * scale[rows_at]
            rounded = value.astype(BF16)
            out16_ref[at, rows_at, :] = rounded
            out_ref[at, rows_at, :] = rounded.astype(F32)

    s_qk = causal(q, k)
    scale = position_scale(flags_ref[0] * rows, rows)
    put(first_ref, first16_ref, 0, forward(s_qk, v), dot(q, prefix, NN), scale)
    put(first_ref, first16_ref, 1, backward(s_qk, g), dot(k, suffix, NN))
    s_gv = causal(g, v)
    put(second_ref, second16_ref, 0, forward(s_gv, k), dot(g, prefix, NT))
    put(second_ref, second16_ref, 1, backward(s_gv, q), dot(v, suffix, NT))


def attend(flags, q, k, v, g, prefix, suffix):
    rows, hd = q.shape
    head = pl.BlockSpec((rows, HEAD_DIM), lambda h: (0, h))
    state = pl.BlockSpec((1, HEAD_DIM, HEAD_DIM), lambda h: (h, 0, 0))
    out = pl.BlockSpec((2, rows, HEAD_DIM), lambda h: (0, 0, h))
    return pl.pallas_call(
        attend_kernel,
        grid=(hd // HEAD_DIM,),
        out_shape=[shaped((2, rows, hd), F32)] * 2 + [shaped((2, rows, hd), BF16)] * 2,
        in_specs=[pl.BlockSpec(memory_space=pltpu.SMEM)] + [head] * 4 + [state] * 2,
        out_specs=[out] * 4,
        compiler_params=pltpu.CompilerParams(vmem_limit_bytes=VMEM_LIMIT),
        cost_estimate=pl.CostEstimate(
            flops=14 * rows * rows * hd, bytes_accessed=8 * 2**20, transcendentals=0
        ),
        name="attend",
    )(flags, q, k, v, g, prefix, suffix)


def head_terms_kernel(d2_ref, d1_ref, wq_ref, wk_ref, wv_ref, out_ref):
    out_ref[...] = (
        dot(d2_ref[0], wq_ref[...], NT)
        + dot(d2_ref[1], wk_ref[...], NT)
        + dot(d1_ref[1], wv_ref[...], NT)
    )


def head_terms(first16, second16, w_query, w_key, w_value):
    width, hd = w_query.shape
    rows = first16.shape[1]
    step = 256
    whole = pl.BlockSpec((2, rows, hd), lambda i: (0, 0, 0))
    weight = pl.BlockSpec((step, hd), lambda i: (i, 0))
    return pl.pallas_call(
        head_terms_kernel,
        grid=(width // step,),
        out_shape=shaped((rows, width), F32),
        in_specs=[whole, whole, weight, weight, weight],
        out_specs=pl.BlockSpec((rows, step), lambda i: (0, i)),
        compiler_params=pltpu.CompilerParams(vmem_limit_bytes=VMEM_LIMIT),
        cost_estimate=pl.CostEstimate(
            flops=6 * rows * width * hd, bytes_accessed=12 * 2**20, transcendentals=0
        ),
        name="head_terms",
    )(second16, first16, w_query, w_key, w_value)


def tiles_kernel(
    at_ref, rows0a, rows0b, rows1a, rows1b, far0a, far0b, far1a, far1b, own_ref, far_ref, *rest,
    out_first, scale, added,
):
    received, outs = (rest[:2], rest[2:]) if added else (None, rest)
    half = own_ref.shape[2] // 2
    inputs = (((rows0a, far0a), (rows0b, far0b)), ((rows1a, far1a), (rows1b, far1b)))
    for side in range(2):
        features = pl.ds(side * half, half)
        for t in range(2):
            near, far = inputs[t][side]
            pair = (
                (near[...], own_ref[t, :, features]),
                (far[...].astype(BF16), far_ref[t, :, features].astype(BF16)),
            )
            if out_first[t]:
                pair = tuple((b, a) for a, b in pair)
            tile = (dot(*pair[0], TN) + dot(*pair[1], TN)) * scale
            if added:
                tile = tile + received[side][0, t]
            outs[side][0, t] = tile


def tiles(near, rows, far, own, other, blocks, out_first, scale, received=None):
    positions, hd = own.shape[1:]
    half = hd // 2
    block = far[0].shape[1] // 4
    low, high = blocks

    def near_spec(which):
        return pl.BlockSpec((positions, block), lambda i, at: (0, at[which[0] + i * (which[1] - which[0])]))

    def far_spec(which):
        return pl.BlockSpec((positions, block), lambda i, at: (0, which[0] + i * (which[1] - which[0])))

    whole = pl.BlockSpec((2, positions, hd), lambda i, at: (0, 0, 0))
    tile = pl.BlockSpec((1, 2, half, block), lambda i, at: (i, 0, 0, 0))
    in_specs = [near_spec(low), near_spec(high)] * 2 + [far_spec(low), far_spec(high)] * 2
    in_specs += [whole, whole]
    args = [rows[0], rows[0], rows[1], rows[1], far[0], far[0], far[1], far[1], own, other]
    if received is not None:
        in_specs += [tile, tile]
        args += list(received)
    return pl.pallas_call(
        functools.partial(
            tiles_kernel, out_first=out_first, scale=scale, added=received is not None
        ),
        grid_spec=pltpu.PrefetchScalarGridSpec(
            num_scalar_prefetch=1, grid=(2,), in_specs=in_specs, out_specs=[tile, tile]
        ),
        out_shape=[shaped((2, 2, half, block), F32)] * 2,
        compiler_params=pltpu.CompilerParams(vmem_limit_bytes=VMEM_LIMIT),
        cost_estimate=pl.CostEstimate(
            flops=8 * 2 * positions * hd * block * 2, bytes_accessed=12 * 2**20, transcendentals=0
        ),
        name="tiles",
    )(near, *args)


def states_before(x, axis, reverse):
    peers, here = (lax.axis_size(axis), lax.axis_index(axis))
    everything = lax.all_gather(x, axis)
    at = jnp.arange(peers)
    reached = at > here if reverse else at < here
    return jnp.sum(jnp.where(reached[:, None, None, None], everything, 0.0), axis=0)


def swap(x, axis, bit):
    return lax.ppermute(x, axis, [(i, i ^ bit) for i in range(lax.axis_size(axis))])


def after(x, done):
    return lax.optimization_barrier((x, done))[0]


def local(layer_input, w_query, w_key, w_value, w_out, out_grad):
    num_rows, width = layer_input.shape[1:]
    hd = w_query.shape[1]
    in_rows = layer_input[0]
    grad_rows = out_grad[0]
    n_seq, n_dp = (lax.axis_size(a) for a in ("seq", "dp"))
    seq_at, dp_at = (lax.axis_index(a) for a in ("seq", "dp"))
    total_rows = n_seq * n_dp * num_rows
    scale = float(total_rows) ** -0.5
    planar = n_seq == 2 and n_dp == 4

    q, k, v, g, *states = project(
        seq_at, in_rows, grad_rows, w_query, w_key, w_value, w_out, n_seq == 2
    )
    if n_seq == 2:
        prefix = suffix = swap(states[0], "seq", 1)
        flags = jnp.stack([seq_at, seq_at, 1 - seq_at]).astype(jnp.int32)
    else:
        prefix = states_before(states[0], "seq", False)
        suffix = states_before(states[1], "seq", True)
        flags = jnp.stack([seq_at, 1, 1]).astype(jnp.int32)

    if planar:
        y_at, core_at = dp_at // 2, dp_at % 2
        block = width // 8
        near = jnp.stack(
            [(seq_at ^ ds) * 4 + (y_at ^ dy) * 2 + core_at for ds in (0, 1) for dy in (0, 1)]
        ).astype(jnp.int32)

        def to_other_core(rows):
            rows = after(rows, states[0])
            parts = [
                lax.dynamic_slice_in_dim(rows, (near[i] ^ 1) * block, block, axis=1)
                for i in range(4)
            ]
            return swap(jnp.concatenate(parts, axis=1).astype(F32), "dp", 1)

        far_in = to_other_core(in_rows)
        far_grad = to_other_core(grad_rows)

    first, second, first16, second16 = attend(flags, q, k, v, g, prefix, suffix)

    if not planar:
        terms = head_terms(first16, second16, w_query, w_key, w_value)
        input_grad = lax.psum_scatter(terms, "head", scatter_dimension=1, tiled=True)

        def reduced(rows, d):
            return lax.psum_scatter(
                dot(rows, d, TN) * scale, ("seq", "dp"), scatter_dimension=0, tiled=True
            )

        return (
            input_grad.astype(BF16)[None],
            reduced(in_rows, second16[0]),
            reduced(in_rows, second16[1]),
            reduced(in_rows, first16[1]),
            reduced(grad_rows, first16[0]).T,
        )

    far_first = swap(first, "dp", 1)
    far_second = swap(second, "dp", 1)
    terms = head_terms(first16, second16, w_query, w_key, w_value)
    input_grad = lax.psum_scatter(terms, "head", scatter_dimension=1, tiled=True)

    def pair(rows, far, own, other, out_first):
        make = functools.partial(tiles, near, rows, far, own, other)
        a, b = make(((2, 3), (1, 3)), out_first, scale)
        a, b = swap(a, "seq", 1), swap(b, "dp", 2)
        a, b = make(((0, 1), (0, 2)), out_first, scale, (a, b))
        return a[0], swap(a[1], "dp", 2), b[0], swap(b[1], "seq", 1)

    a, far_a, b, far_b = pair(
        (grad_rows, in_rows), (far_grad, far_in), first16, far_first, (True, False)
    )
    grad_out = jnp.concatenate([a[0] + far_a[0], b[0] + far_b[0]], axis=0)
    grad_value = jnp.concatenate([a[1] + far_a[1], b[1] + far_b[1]], axis=1)
    a, far_a, b, far_b = pair(
        (in_rows, in_rows), (far_in, far_in), second16, far_second, (False, False)
    )
    grad_query = jnp.concatenate([a[0] + far_a[0], b[0] + far_b[0]], axis=1)
    grad_key = jnp.concatenate([a[1] + far_a[1], b[1] + far_b[1]], axis=1)
    return (input_grad.astype(BF16)[None], grad_query, grad_key, grad_value, grad_out)


def solution(mesh):
    return jax.shard_map(
        local,
        mesh=mesh,
        in_specs=(
            P("dp", "seq", None),
            P(None, "head"),
            P(None, "head"),
            P(None, "head"),
            P("head", None),
            P("dp", "seq", None),
        ),
        out_specs=(
            P("dp", "seq", "head"),
            P(("seq", "dp"), "head"),
            P(("seq", "dp"), "head"),
            P(("seq", "dp"), "head"),
            P("head", ("seq", "dp")),
        ),
        check_vma=False,
    )
```

```python
import functools

import jax
import jax.numpy as jnp
from jax import lax
from jax.experimental import pallas as pl
from jax.experimental.pallas import tpu as pltpu
from jax.sharding import PartitionSpec as P

HEAD_DIM = 128
BF16 = jnp.bfloat16
F32 = jnp.float32
MIB = 1024 * 1024
NN = ((1,), (0,))
NT = ((1,), (1,))
TN = ((0,), (0,))
ANYWHERE = pl.BlockSpec(memory_space=pl.ANY)
IN_VMEM = pl.BlockSpec(memory_space=pltpu.VMEM)
IN_SMEM = pl.BlockSpec(memory_space=pltpu.SMEM)


def dot(a, b, dims):
    return lax.dot_general(a, b, (dims, ((), ())), preferred_element_type=F32)


def shaped(shape, dtype):
    return jax.ShapeDtypeStruct(shape, dtype)


def params(mib):
    return pltpu.CompilerParams(vmem_limit_bytes=mib * MIB)


def cost(flops, size):
    return pl.CostEstimate(flops=flops, bytes_accessed=size, transcendentals=0)


def position_scale(start, rows):
    positions = (start + lax.broadcasted_iota(jnp.int32, (rows, 1), 0)).astype(F32)
    return 1.0 / jnp.sqrt(HEAD_DIM * (positions + 1.0))


def project_kernel(
    x_hbm, o_hbm, wq_hbm, wk_hbm, wv_hbm, wo_hbm,
    q_ref, k_ref, v_ref, g_ref, x_ref, o_ref, wq_ref, wk_ref, wv_ref, *rest, one_state,
):
    states, (wo_ref, sems) = rest[:-2], rest[-2:]
    rows, hd = q_ref.shape
    mid = x_ref.shape[1] // 2
    lower, upper = pl.ds(0, mid), pl.ds(mid, mid)
    parts = (
        (x_hbm.at[:, lower], x_ref.at[:, lower]),
        (wk_hbm.at[lower], wk_ref.at[lower]),
        (x_hbm.at[:, upper], x_ref.at[:, upper]),
        (wk_hbm.at[upper], wk_ref.at[upper]),
        (wv_hbm, wv_ref),
        (wq_hbm, wq_ref),
        (o_hbm, o_ref),
        (wo_hbm, wo_ref),
    )
    copies = [pltpu.make_async_copy(a, b, sems.at[i]) for i, (a, b) in enumerate(parts)]
    for c in copies[:4]:
        c.start()
    copies[0].wait()
    copies[1].wait()
    for c in copies[4:]:
        c.start()
    keys = dot(x_ref[:, lower], wk_ref[lower, :], NN)
    copies[2].wait()
    copies[3].wait()
    k_ref[...] = (keys + dot(x_ref[:, upper], wk_ref[upper, :], NN)).astype(BF16)
    copies[4].wait()
    v_ref[...] = dot(x_ref[...], wv_ref[...], NN).astype(BF16)
    copies[5].wait()
    q_ref[...] = dot(x_ref[...], wq_ref[...], NN).astype(BF16)
    copies[6].wait()
    copies[7].wait()
    seq_at = lax.axis_index("seq")
    scale = position_scale(seq_at * rows, rows)
    g_ref[...] = (dot(o_ref[...], wo_ref[...], NT) * scale).astype(BF16)

    def state(a_ref, b_ref, out_ref):
        for h in range(hd // HEAD_DIM):
            at = pl.ds(h * HEAD_DIM, HEAD_DIM)
            out_ref[h] = dot(a_ref[:, at], b_ref[:, at], TN)

    if one_state:
        pl.when(seq_at == 0)(lambda: state(k_ref, v_ref, states[0]))
        pl.when(seq_at != 0)(lambda: state(q_ref, g_ref, states[0]))
    else:
        state(k_ref, v_ref, states[0])
        state(q_ref, g_ref, states[1])


def project(in_rows, grad_rows, w_query, w_key, w_value, w_out, one_state):
    rows, width = in_rows.shape
    hd = w_query.shape[1]
    n_states = 1 if one_state else 2
    args = [
        pltpu.with_memory_space_constraint(a, pltpu.HBM)
        for a in (in_rows, grad_rows, w_query, w_key, w_value, w_out)
    ]
    outs = [(rows, hd)] * 4 + [(rows, width)] * 2 + [(width, hd)] * 3
    out_shape = [pltpu.VMEM(s, BF16) for s in outs]
    out_shape += [pltpu.VMEM((hd // HEAD_DIM, HEAD_DIM, HEAD_DIM), F32)] * n_states
    return pl.pallas_call(
        functools.partial(project_kernel, one_state=one_state),
        out_shape=out_shape,
        in_specs=[ANYWHERE] * 6,
        out_specs=[IN_VMEM] * len(out_shape),
        scratch_shapes=[pltpu.VMEM((hd, width), BF16), pltpu.SemaphoreType.DMA((8,))],
        compiler_params=params(16),
        cost_estimate=cost(8 * rows * width * hd, 14 * MIB),
        name="project",
    )(*args)


def call(kernel, name, out_shape, args, flops, after=()):
    n, n_after = len(args), len(after)

    def body(*refs):
        kernel(*refs[:n], *refs[n + n_after :])

    many = isinstance(out_shape, (list, tuple))
    return pl.pallas_call(
        body,
        out_shape=out_shape,
        in_specs=[IN_VMEM] * n + [ANYWHERE] * n_after,
        out_specs=[IN_VMEM] * len(out_shape) if many else IN_VMEM,
        compiler_params=params(16),
        cost_estimate=cost(flops, 2 * MIB),
        name=name,
    )(*args, *after)


def attend_kernel(q_all, k_all, v_all, g_all, *rest, which):
    state_ref, out_ref = rest if len(rest) == 2 else (None, rest[0])
    rows, hd = q_all.shape
    half = rows // 2
    top, low = slice(0, half), slice(half, rows)

    def causal(a, b):
        r = lax.broadcasted_iota(jnp.int32, (half, half), 0)
        c = lax.broadcasted_iota(jnp.int32, (half, half), 1)
        diagonal = r >= c
        s00 = jnp.where(diagonal, dot(a[top], b[top], NT), 0.0).astype(BF16)
        s10 = dot(a[low], b[top], NT).astype(BF16)
        s11 = jnp.where(diagonal, dot(a[low], b[low], NT), 0.0).astype(BF16)
        return s00, s10, s11

    def head(h):
        at = pl.ds(h * HEAD_DIM, HEAD_DIM)
        state = None if state_ref is None else state_ref[h].astype(BF16)

        def put(t, halves, cross, dims, scale=None):
            for rows_at, value in zip((top, low), halves):
                if state is not None:
                    value = value + dot(cross[rows_at], state, dims)
                if scale is not None:
                    value = value * scale[rows_at]
                out_ref[t, rows_at, at] = value.astype(BF16)

        return [r[:, at] for r in (q_all, k_all, v_all, g_all)], put

    def forward():
        scale = position_scale(lax.axis_index("seq") * rows, rows)
        for h in range(hd // HEAD_DIM):
            (q, k, v, g), put = head(h)
            for t, a, b, c, dims in ((0, q, k, v, NN), (1, g, v, k, NT)):
                s00, s10, s11 = causal(a, b)
                halves = (dot(s00, c[top], NN), dot(s10, c[top], NN) + dot(s11, c[low], NN))
                put(t, halves, a, dims, scale if t == 0 else None)

    def backward():
        for h in range(hd // HEAD_DIM):
            (q, k, v, g), put = head(h)
            for t, a, b, c, dims in ((0, q, k, g, NN), (1, g, v, q, NT)):
                s00, s10, s11 = causal(a, b)
                halves = (dot(s00, c[top], TN) + dot(s10, c[low], TN), dot(s11, c[low], TN))
                put(t, halves, b, dims)

    chosen = which()
    pl.when(chosen == 0)(forward)
    pl.when(chosen != 0)(backward)


def attend(which, q, k, v, g, state=None, after=()):
    rows, hd = q.shape
    return call(
        functools.partial(attend_kernel, which=which),
        "attend",
        shaped((2, rows, hd), BF16),
        [q, k, v, g] + ([] if state is None else [state]),
        128 * rows * rows * hd,
        after,
    )


def head_terms_kernel(d1_ref, d2_ref, wq_ref, wk_ref, wv_ref, out_ref, *, which, shard):
    width = out_ref.shape[1]
    step = min(width, 256)
    start = shard() * width

    def fill(d_query, d_keys, d_values):
        for i in range(width // step):
            rows = pl.ds(pl.multiple_of(start + i * step, step), step)
            out_ref[:, pl.ds(i * step, step)] = (
                dot(d_query[...], wq_ref[rows, :], NT)
                + dot(d_keys[...], wk_ref[rows, :], NT)
                + dot(d_values[...], wv_ref[rows, :], NT)
            )

    chosen = which()
    pl.when(chosen == 0)(lambda: fill(d1_ref.at[1], d2_ref.at[1], d2_ref.at[0]))
    pl.when(chosen != 0)(lambda: fill(d2_ref.at[1], d1_ref.at[1], d1_ref.at[0]))


def head_terms(which, first, second, weights, shard, shards, after=()):
    width, hd = weights[0].shape
    rows = first.shape[1]
    return call(
        functools.partial(head_terms_kernel, which=which, shard=shard),
        "head_terms",
        shaped((rows, width // shards), F32),
        [first, second, *weights],
        6 * rows * width // shards * hd,
        after,
    )


def add_kernel(*refs):
    total = refs[0][...]
    for ref in refs[1:-1]:
        total = total + ref[...]
    refs[-1][...] = total.astype(refs[-1].dtype)


def add(arrays, dtype, after=()):
    return call(add_kernel, "add", shaped(arrays[0].shape, dtype), list(arrays), 0, after)


def column_block(i):
    seq_at, dp_at = lax.axis_index("seq"), lax.axis_index("dp")
    return (seq_at ^ (i // 2 % 2)) * 4 + (dp_at ^ (i % 2 * 2 + i // 4))


def core():
    return lax.axis_index("dp") % 2


def fill_tiles(x_ref, o_ref, d_ref, pair, side, blocks, scale, added, outs):
    half = d_ref.shape[2] // 2
    block = outs[0].shape[1]
    features = pl.ds(pl.multiple_of(side * half, half), half)

    def fill(inputs):
        for i, b in enumerate(blocks):
            columns = pl.ds(pl.multiple_of(column_block(b) * block, block), block)
            for t in (0, 1):
                tile = dot(inputs[t][:, columns], d_ref[t, :, features], TN) * scale
                for ref, places in added:
                    tile = tile + ref[places[i], t]
                outs[i][t] = tile

    forward = lax.axis_index("seq") == pair
    pl.when(forward)(lambda: fill((o_ref, x_ref)))
    pl.when(jnp.logical_not(forward))(lambda: fill((x_ref, x_ref)))


def other_core_kernel(x_ref, o_ref, d_ref, out_ref, *, pair, slot, scale):
    outs = [out_ref.at[i] for i in range(4)]
    fill_tiles(x_ref, o_ref, d_ref, pair, 1 - core() ^ slot, (4, 5, 6, 7), scale, (), outs)


def first_hop_kernel(x_ref, o_ref, d_ref, far_ref, out_ref, *, pair, slot, scale):
    side = core() ^ slot
    blocks = (2 - side, 3)
    outs = [out_ref.at[i] for i in range(2)]
    fill_tiles(x_ref, o_ref, d_ref, pair, side, blocks, scale, ((far_ref, blocks),), outs)


def second_hop_kernel(
    x_ref, o_ref, d0_ref, d1_ref, far0_ref, far1_ref, over0_ref, over1_ref, keep_ref, send_ref,
    *, slot, scale,
):
    results, far, over = (d0_ref, d1_ref), (far0_ref, far1_ref), (over0_ref, over1_ref)

    def fill(side):
        blocks = (0, 1 + side)
        for p in (0, 1):
            pair = p if side else 1 - p
            added = ((far[pair], blocks), (over[p], (0, 1)))
            outs = (keep_ref.at[p], send_ref.at[p])
            fill_tiles(x_ref, o_ref, results[pair], pair, side, blocks, scale, added, outs)

    side = core() ^ slot
    pl.when(side == 0)(lambda: fill(0))
    pl.when(side != 0)(lambda: fill(1))


def collect_kernel(*refs):
    kept, moved, (out_ref, query_ref, key_ref, value_ref) = refs[:2], refs[2:4], refs[4:]
    half = query_ref.shape[1] // 2

    def put_all(forward, core_at):
        def total(pair, side, t):
            slot = side ^ core_at
            return kept[slot][pair if side else 1 - pair, t] + moved[slot][1 - pair, t]

        for side in (0, 1):
            at = pl.ds(side * half, half)
            out_ref[at, :] = total(forward, side, 0).T
            query_ref[:, at] = total(forward, side, 1)
            value_ref[:, at] = total(1 - forward, side, 0)
            key_ref[:, at] = total(1 - forward, side, 1)

    for forward in (0, 1):
        for core_at in (0, 1):
            chosen = jnp.logical_and(lax.axis_index("seq") == forward, core() == core_at)
            pl.when(chosen)(functools.partial(put_all, forward, core_at))


def collect(kept, moved, after):
    block, half = kept[0].shape[2:]
    tall, wide = shaped((block, 2 * half), F32), shaped((2 * half, block), F32)
    outs = [wide, tall, tall, tall]
    return call(collect_kernel, "collect", outs, [*kept, *moved], 0, after)


def states_before(x, axis, reverse):
    peers, here = (lax.axis_size(axis), lax.axis_index(axis))
    everything = lax.all_gather(x, axis)
    at = jnp.arange(peers)
    reached = at > here if reverse else at < here
    return jnp.sum(jnp.where(reached[:, None, None, None], everything, 0.0), axis=0)


def swap(x, axis, bit):
    return lax.ppermute(x, axis, [(i, i ^ bit) for i in range(lax.axis_size(axis))])


def local(layer_input, w_query, w_key, w_value, w_out, out_grad):
    num_rows = layer_input.shape[1]
    n_seq, n_head, n_dp = (lax.axis_size(a) for a in ("seq", "head", "dp"))
    scale = float(n_seq * n_dp * num_rows) ** -0.5

    q, k, v, g, x, o, *kept = project(
        layer_input[0], out_grad[0], w_query, w_key, w_value, w_out, n_seq == 2
    )
    weights, states = kept[:3], kept[3:]

    if (n_seq, n_head, n_dp) != (2, 4, 4):
        first = attend(lambda: 0, q, k, v, g, states_before(states[0], "seq", False))
        second = attend(lambda: 1, q, k, v, g, states_before(states[1], "seq", True))
        terms = head_terms(lambda: 0, first, second, weights, lambda: 0, 1)

        def reduced(rows, d):
            return lax.psum_scatter(
                dot(rows, d, TN) * scale, ("seq", "dp"), scatter_dimension=0, tiled=True
            )

        return (
            lax.psum_scatter(terms, "head", scatter_dimension=1, tiled=True).astype(BF16)[None],
            reduced(x, first[1]),
            reduced(x, second[1]),
            reduced(x, second[0]),
            reduced(o, first[0]).T,
        )

    def here():
        return lax.axis_index("seq")

    def term(flip, after):
        shard = functools.partial(lambda f: lax.axis_index("head") ^ f, flip)
        return head_terms(here, first, second, weights, shard, n_head, after)

    def hop(array, slot, second):
        pairs = []
        for i in range(8):
            side = i % 2 ^ slot
            pairs.append((i, i ^ (4 if side == second else 2)))
        return lax.ppermute(array, ("seq", "dp"), pairs)

    block, half = x.shape[1] // 8, q.shape[1] // 2
    tile = (2, block, half)
    flops = 4 * num_rows * block * half

    def to_core(pair, slot, after):
        kernel = functools.partial(other_core_kernel, pair=pair, slot=slot, scale=scale)
        args = [x, o, results[pair]]
        array = call(kernel, "other_core", shaped((4, *tile), F32), args, 4 * flops, after)
        return array, swap(array, "dp", 1)

    def first_hop(pair, slot, after):
        kernel = functools.partial(first_hop_kernel, pair=pair, slot=slot, scale=scale)
        args = [x, o, results[pair], far[pair][slot]]
        array = call(kernel, "first_hop", shaped((2, *tile), F32), args, 2 * flops, after)
        return array, hop(array, slot, 0)

    def second_hop(slot, over, after):
        kernel = functools.partial(second_hop_kernel, slot=slot, scale=scale)
        args = [x, o, *results, far[0][slot], far[1][slot], *over]
        outs = [shaped((2, *tile), F32)] * 2
        keep, leave = call(kernel, "second_hop", outs, args, 4 * flops, after)
        return keep, hop(leave, slot, 1)

    results, far = [], ([None, None], [None, None])
    state = swap(states[0], "seq", 1)
    first = attend(here, q, k, v, g)
    results.append(first)
    at, far[0][0] = to_core(0, 0, [first])
    at, far[0][1] = to_core(0, 1, [at])
    second = attend(lambda: 1 - here(), q, k, v, g, state, after=[at])
    results.append(second)
    at, far[1][0] = to_core(1, 0, [second])
    at, far[1][1] = to_core(1, 1, [at])
    at, over1 = first_hop(0, 0, [at])
    at, over2 = first_hop(0, 1, [at])
    t3 = term(3, [at])
    t3_in = swap(t3, "head", 1)
    at, over3 = first_hop(1, 0, [t3])
    t1 = term(1, [at])
    t1_in = swap(t1, "head", 1)
    t2 = term(2, [t1])
    t0 = term(0, [t2])
    at, over4 = first_hop(1, 1, [t0, over1])
    t2 = add([t2, t3_in], F32, [at, over2])
    t2_in = swap(t2, "head", 2)
    keep0, moved0 = second_hop(0, (over1, over3), [t2])
    keep1, moved1 = second_hop(1, (over2, over4), [keep0])
    input_grad = add([t0, t1_in, t2_in], BF16, [keep1])
    kept, moved = (keep0, keep1), (moved0, moved1)
    grad_out, grad_query, grad_key, grad_value = collect(kept, moved, [])
    return (input_grad[None], grad_query, grad_key, grad_value, grad_out)


def solution(mesh):
    return jax.shard_map(
        local,
        mesh=mesh,
        in_specs=(
            P("dp", "seq", None),
            P(None, "head"),
            P(None, "head"),
            P(None, "head"),
            P("head", None),
            P("dp", "seq", None),
        ),
        out_specs=(
            P("dp", "seq", "head"),
            P(("seq", "dp"), "head"),
            P(("seq", "dp"), "head"),
            P(("seq", "dp"), "head"),
            P("head", ("seq", "dp")),
        ),
        check_vma=False,
    )
```

```python
import functools

import jax
import jax.numpy as jnp
from jax import lax
from jax.experimental import pallas as pl
from jax.experimental.pallas import tpu as pltpu
from jax.sharding import PartitionSpec as P

HEAD_DIM = 128
BF16 = jnp.bfloat16
F32 = jnp.float32
MIB = 1024 * 1024
PLANNED = (2, 4, 4)
NN = ((1,), (0,))
NT = ((1,), (1,))
TN = ((0,), (0,))
ANYWHERE = pl.BlockSpec(memory_space=pl.ANY)
IN_VMEM = pl.BlockSpec(memory_space=pltpu.VMEM)
IN_SMEM = pl.BlockSpec(memory_space=pltpu.SMEM)


def dot(a, b, dims):
    return lax.dot_general(a, b, (dims, ((), ())), preferred_element_type=F32)


def shaped(shape, dtype):
    return jax.ShapeDtypeStruct(shape, dtype)


def params(mib):
    return pltpu.CompilerParams(vmem_limit_bytes=mib * MIB)


def cost(flops, size):
    return pl.CostEstimate(flops=flops, bytes_accessed=size, transcendentals=0)


class Place:
    def __init__(self, number, sizes):
        _, n_head, n_dp = sizes
        self.dp = lax.rem(number, n_dp)
        self.head = lax.rem(lax.div(number, n_dp), n_head)
        self.seq = lax.div(number, n_head * n_dp)
        self.core = lax.rem(self.dp, 2)


def position_scale(start, rows):
    positions = (start + lax.broadcasted_iota(jnp.int32, (rows, 1), 0)).astype(F32)
    return 1.0 / jnp.sqrt(HEAD_DIM * (positions + 1.0))


def project_kernel(
    number_ref, x_hbm, o_hbm, wq_hbm, wk_hbm, wv_hbm, wo_hbm,
    q_ref, k_ref, v_ref, g_ref, xo_ref, wq_ref, wk_ref, wv_ref, *rest, one_state, sizes,
):
    states, (wo_ref, sems) = rest[:-2], rest[-2:]
    rows, hd = q_ref.shape
    x_ref, o_ref = xo_ref.at[0], xo_ref.at[1]
    mid = x_ref.shape[1] // 2
    lower, upper = pl.ds(0, mid), pl.ds(mid, mid)
    parts = (
        (x_hbm.at[:, lower], x_ref.at[:, lower]),
        (wk_hbm.at[lower], wk_ref.at[lower]),
        (x_hbm.at[:, upper], x_ref.at[:, upper]),
        (wk_hbm.at[upper], wk_ref.at[upper]),
        (wv_hbm, wv_ref),
        (wq_hbm, wq_ref),
        (o_hbm, o_ref),
        (wo_hbm, wo_ref),
    )
    copies = [pltpu.make_async_copy(a, b, sems.at[i]) for i, (a, b) in enumerate(parts)]
    for c in copies[:4]:
        c.start()
    copies[0].wait()
    copies[1].wait()
    for c in copies[4:]:
        c.start()
    keys = dot(x_ref[:, lower], wk_ref[lower, :], NN)
    copies[2].wait()
    copies[3].wait()
    k_ref[...] = (keys + dot(x_ref[:, upper], wk_ref[upper, :], NN)).astype(BF16)
    copies[4].wait()
    v_ref[...] = dot(x_ref[...], wv_ref[...], NN).astype(BF16)
    copies[5].wait()
    q_ref[...] = dot(x_ref[...], wq_ref[...], NN).astype(BF16)
    copies[6].wait()
    copies[7].wait()
    seq_at = Place(number_ref[0], sizes).seq
    scale = position_scale(seq_at * rows, rows)
    g_ref[...] = (dot(o_ref[...], wo_ref[...], NT) * scale).astype(BF16)

    def state(a_ref, b_ref, out_ref):
        for h in range(hd // HEAD_DIM):
            at = pl.ds(h * HEAD_DIM, HEAD_DIM)
            out_ref[h] = dot(a_ref[:, at], b_ref[:, at], TN)

    if one_state:
        pl.when(seq_at == 0)(lambda: state(k_ref, v_ref, states[0]))
        pl.when(seq_at != 0)(lambda: state(q_ref, g_ref, states[0]))
    else:
        state(k_ref, v_ref, states[0])
        state(q_ref, g_ref, states[1])


def project(number, sizes, in_rows, grad_rows, w_query, w_key, w_value, w_out):
    rows, width = in_rows.shape
    hd = w_query.shape[1]
    one_state = sizes == PLANNED
    n_states = 1 if one_state else 2
    args = [
        pltpu.with_memory_space_constraint(a, pltpu.HBM)
        for a in (in_rows, grad_rows, w_query, w_key, w_value, w_out)
    ]
    outs = [(rows, hd)] * 4 + [(2, rows, width)] + [(width, hd)] * 3
    out_shape = [pltpu.VMEM(s, BF16) for s in outs]
    out_shape += [pltpu.VMEM((hd // HEAD_DIM, HEAD_DIM, HEAD_DIM), F32)] * n_states
    return pl.pallas_call(
        functools.partial(project_kernel, one_state=one_state, sizes=sizes),
        out_shape=out_shape,
        in_specs=[IN_SMEM] + [ANYWHERE] * 6,
        out_specs=[IN_VMEM] * len(out_shape),
        scratch_shapes=[pltpu.VMEM((hd, width), BF16), pltpu.SemaphoreType.DMA((8,))],
        compiler_params=params(16),
        cost_estimate=cost(8 * rows * width * hd, 14 * MIB),
        name="project",
    )(number, *args)


def call(kernel, name, out_shape, args, flops, after=(), place=None, in_place=False):
    n, n_after = len(args), len(after)
    numbers = [] if place is None else [place[0]]

    def body(*refs):
        first = [Place(refs[0][0], place[1])] if numbers else []
        refs = refs[len(numbers) :]
        kernel(*first, *refs[:n], *refs[n + n_after :])

    many = isinstance(out_shape, (list, tuple))
    return pl.pallas_call(
        body,
        out_shape=out_shape,
        in_specs=[IN_SMEM] * len(numbers) + [IN_VMEM] * n + [ANYWHERE] * n_after,
        out_specs=[IN_VMEM] * len(out_shape) if many else IN_VMEM,
        compiler_params=params(16),
        cost_estimate=cost(flops, 2 * MIB),
        input_output_aliases={len(numbers) + n - 1: 0} if in_place else {},
        name=name,
    )(*numbers, *args, *after)


def attend_kernel(place, q_all, k_all, v_all, g_all, *rest, which, with_state):
    state_ref, out_ref = rest[0] if with_state else None, rest[-1]
    rows, hd = q_all.shape
    half = rows // 2
    top, low = slice(0, half), slice(half, rows)

    def causal(a, b):
        r = lax.broadcasted_iota(jnp.int32, (half, half), 0)
        c = lax.broadcasted_iota(jnp.int32, (half, half), 1)
        diagonal = r >= c
        s00 = jnp.where(diagonal, dot(a[top], b[top], NT), 0.0).astype(BF16)
        s10 = dot(a[low], b[top], NT).astype(BF16)
        s11 = jnp.where(diagonal, dot(a[low], b[low], NT), 0.0).astype(BF16)
        return s00, s10, s11

    def per_head(body):
        def step(h, carry):
            at = pl.ds(pl.multiple_of(h * HEAD_DIM, HEAD_DIM), HEAD_DIM)
            state = state_ref[h].astype(BF16) if with_state else None

            def put(slot, halves, cross, dims, scale=None):
                for rows_at, value in zip((top, low), halves):
                    if with_state:
                        value = value + dot(cross[rows_at], state, dims)
                    if scale is not None:
                        value = value * scale[rows_at]
                    out_ref[slot, rows_at, at] = value.astype(BF16)

            body([r[:, at] for r in (q_all, k_all, v_all, g_all)], put)
            return carry

        lax.fori_loop(0, hd // HEAD_DIM, step, 0, unroll=2)

    def forward():
        scale = position_scale(place.seq * rows, rows)

        def body(heads, put):
            q, k, v, g = heads
            for slot, a, b, c, dims in ((0, q, k, v, NN), (1, g, v, k, NT)):
                s00, s10, s11 = causal(a, b)
                halves = (dot(s00, c[top], NN), dot(s10, c[top], NN) + dot(s11, c[low], NN))
                put(slot, halves, a, dims, scale if slot == 0 else None)

        per_head(body)

    def backward():
        def body(heads, put):
            q, k, v, g = heads
            for slot, a, b, c, dims in ((2, q, k, g, NN), (3, g, v, q, NT)):
                s00, s10, s11 = causal(a, b)
                halves = (dot(s00, c[top], TN) + dot(s10, c[low], TN), dot(s11, c[low], TN))
                put(slot, halves, b, dims)

        per_head(body)

    chosen = which(place)
    pl.when(chosen == 0)(forward)
    pl.when(chosen != 0)(backward)


def attend(place, which, q, k, v, g, state=None, into=None, after=()):
    rows, hd = q.shape
    args = [q, k, v, g] + [a for a in (state, into) if a is not None]
    return call(
        functools.partial(attend_kernel, which=which, with_state=state is not None),
        "attend",
        shaped((4, rows, hd), BF16),
        args,
        128 * rows * rows * hd,
        after,
        place,
        in_place=into is not None,
    )


def head_terms_kernel(place, d_ref, wq_ref, wk_ref, wv_ref, out_ref, *, shard):
    width = out_ref.shape[1]
    step = min(width, 256)
    start = shard(place) * width
    for i in range(width // step):
        rows = pl.ds(pl.multiple_of(start + i * step, step), step)
        out_ref[:, pl.ds(i * step, step)] = (
            dot(d_ref[1], wq_ref[rows, :], NT)
            + dot(d_ref[3], wk_ref[rows, :], NT)
            + dot(d_ref[2], wv_ref[rows, :], NT)
        )


def head_terms(place, results, weights, shard, shards, after=()):
    width, hd = weights[0].shape
    rows = results.shape[1]
    return call(
        functools.partial(head_terms_kernel, shard=shard),
        "head_terms",
        shaped((rows, width // shards), F32),
        [results, *weights],
        6 * rows * width // shards * hd,
        after,
        place,
    )


def add_kernel(*refs):
    total = refs[0][...]
    for ref in refs[1:-1]:
        total = total + ref[...]
    refs[-1][...] = total.astype(refs[-1].dtype)


def add(arrays, dtype, after=()):
    return call(add_kernel, "add", shaped(arrays[0].shape, dtype), list(arrays), 0, after)


def column_block(place, i):
    return (place.seq ^ (i // 2 % 2)) * 4 + (place.dp ^ (i % 2 * 2 + i // 4))


def fill_tiles(place, xo_ref, d_ref, pair, side, blocks, scale, added, outs):
    half = d_ref.shape[2] // 2
    block = outs[0].shape[1]
    features = pl.ds(pl.multiple_of(side * half, half), half)
    for i, b in enumerate(blocks):
        columns = pl.ds(pl.multiple_of(column_block(place, b) * block, block), block)
        for t, rows in enumerate((1 - pair, 0)):
            tile = dot(xo_ref[rows, :, columns], d_ref[2 * pair + t, :, features], TN) * scale
            for read in added:
                tile = tile + read(i, t)
            outs[i][t] = tile


def other_core_kernel(place, xo_ref, d_ref, out_ref, *, early, slot, scale):
    outs = [out_ref.at[i] for i in range(4)]
    pair, side = place.seq ^ early, 1 - place.core ^ slot
    fill_tiles(place, xo_ref, d_ref, pair, side, (4, 5, 6, 7), scale, (), outs)


def first_hop_kernel(place, xo_ref, d_ref, far_ref, out_ref, *, early, slot, scale):
    pair, side = place.seq ^ early, place.core ^ slot
    blocks = (2 - side, 3)
    outs = [out_ref.at[i] for i in range(2)]
    added = (lambda i, t: far_ref[blocks[i], t],)
    fill_tiles(place, xo_ref, d_ref, pair, side, blocks, scale, added, outs)


def second_hop_kernel(
    place, xo_ref, d_ref, far0_ref, far1_ref, over0_ref, over1_ref, keep_ref, send_ref, *, slot, scale
):
    far, over = (far0_ref, far1_ref), (over0_ref, over1_ref)
    side = place.core ^ slot
    blocks = (0, 1 + side)
    for p in (0, 1):
        added = (
            lambda i, t: jnp.where(side == 0, far[1 - p][blocks[i], t], far[p][blocks[i], t]),
            lambda i, t: over[p][i, t],
        )
        pair = place.seq ^ p ^ 1 - side
        outs = (keep_ref.at[p], send_ref.at[p])
        fill_tiles(place, xo_ref, d_ref, pair, side, blocks, scale, added, outs)


def collect_kernel(place, *refs):
    kept, moved, (out_ref, query_ref, key_ref, value_ref) = refs[:2], refs[2:4], refs[4:]
    half = query_ref.shape[1] // 2
    for side in (0, 1):
        at = pl.ds(side * half, half)

        def total(pair, t):
            p = place.seq ^ pair
            first = kept[side][p if side else 1 - p, t] + moved[side][1 - p, t]
            second = kept[1 - side][p if side else 1 - p, t] + moved[1 - side][1 - p, t]
            return jnp.where(place.core == 0, first, second)

        out_ref[at, :] = total(0, 0).T
        query_ref[:, at] = total(0, 1)
        value_ref[:, at] = total(1, 0)
        key_ref[:, at] = total(1, 1)


def collect(place, kept, moved, after):
    block, half = kept[0].shape[2:]
    tall, wide = shaped((block, 2 * half), F32), shaped((2 * half, block), F32)
    outs = [wide, tall, tall, tall]
    return call(collect_kernel, "collect", outs, [*kept, *moved], 0, after, place)


def states_before(x, axis, reverse):
    peers, here = (lax.axis_size(axis), lax.axis_index(axis))
    everything = lax.all_gather(x, axis)
    at = jnp.arange(peers)
    reached = at > here if reverse else at < here
    return jnp.sum(jnp.where(reached[:, None, None, None], everything, 0.0), axis=0)


def swap(x, axis, bit):
    return lax.ppermute(x, axis, [(i, i ^ bit) for i in range(lax.axis_size(axis))])


def local(layer_input, w_query, w_key, w_value, w_out, out_grad):
    num_rows = layer_input.shape[1]
    n_seq, n_head, n_dp = (lax.axis_size(a) for a in ("seq", "head", "dp"))
    scale = float(n_seq * n_dp * num_rows) ** -0.5

    sizes = (n_seq, n_head, n_dp)
    number = (lax.axis_index("seq") * n_head + lax.axis_index("head")) * n_dp + lax.axis_index("dp")
    number = number.astype(jnp.int32).reshape(1)
    place = (number, sizes)
    q, k, v, g, xo, *kept = project(
        number, sizes, layer_input[0], out_grad[0], w_query, w_key, w_value, w_out
    )
    weights, states = kept[:3], kept[3:]

    if sizes != PLANNED:
        prefix = states_before(states[0], "seq", False)
        suffix = states_before(states[1], "seq", True)
        d = attend(place, lambda at: 0, q, k, v, g, prefix)
        d = attend(place, lambda at: 1, q, k, v, g, suffix, d)
        terms = head_terms(place, d, weights, lambda at: 0, 1)

        def reduced(rows, d):
            return lax.psum_scatter(
                dot(rows, d, TN) * scale, ("seq", "dp"), scatter_dimension=0, tiled=True
            )

        return (
            lax.psum_scatter(terms, "head", scatter_dimension=1, tiled=True).astype(BF16)[None],
            reduced(xo[0], d[1]),
            reduced(xo[0], d[3]),
            reduced(xo[0], d[2]),
            reduced(xo[1], d[0]).T,
        )

    def term(flip, after):
        return head_terms(place, d, weights, lambda at: at.head ^ flip, n_head, after)

    def hop(array, slot, second):
        pairs = []
        for i in range(8):
            side = i % 2 ^ slot
            pairs.append((i, i ^ (4 if side == second else 2)))
        return lax.ppermute(array, ("seq", "dp"), pairs)

    block, half = xo.shape[2] // 8, q.shape[1] // 2
    tile = (2, block, half)
    flops = 4 * num_rows * block * half

    def to_core(d, early, slot, after):
        kernel = functools.partial(other_core_kernel, early=early, slot=slot, scale=scale)
        out = shaped((4, *tile), F32)
        array = call(kernel, "other_core", out, [xo, d], 4 * flops, after, place)
        return array, swap(array, "dp", 1)

    def first_hop(early, slot, after):
        kernel = functools.partial(first_hop_kernel, early=early, slot=slot, scale=scale)
        out = shaped((2, *tile), F32)
        args = [xo, d, far[early][slot]]
        array = call(kernel, "first_hop", out, args, 2 * flops, after, place)
        return array, hop(array, slot, 0)

    def second_hop(slot, over, after):
        kernel = functools.partial(second_hop_kernel, slot=slot, scale=scale)
        args = [xo, d, far[0][slot], far[1][slot], *over]
        outs = [shaped((2, *tile), F32)] * 2
        keep, leave = call(kernel, "second_hop", outs, args, 4 * flops, after, place)
        return keep, hop(leave, slot, 1)

    far = ([None, None], [None, None])
    state = swap(states[0], "seq", 1)
    early = attend(place, lambda at: at.seq, q, k, v, g)
    at, far[0][0] = to_core(early, 0, 0, [])
    at, far[0][1] = to_core(early, 0, 1, [at])
    d = attend(place, lambda at: 1 - at.seq, q, k, v, g, state, early, [at])
    at, far[1][0] = to_core(d, 1, 0, [])
    at, far[1][1] = to_core(d, 1, 1, [at])
    at, over1 = first_hop(0, 0, [at])
    at, over2 = first_hop(0, 1, [at])
    t3 = term(3, [at])
    t3_in = swap(t3, "head", 1)
    at, over3 = first_hop(1, 0, [t3])
    t1 = term(1, [at])
    t1_in = swap(t1, "head", 1)
    t2 = term(2, [t1])
    t0 = term(0, [t2])
    at, over4 = first_hop(1, 1, [t0, over1])
    t2 = add([t2, t3_in], F32, [at, over2])
    t2_in = swap(t2, "head", 2)
    keep0, moved0 = second_hop(0, (over1, over3), [t2])
    keep1, moved1 = second_hop(1, (over2, over4), [keep0])
    input_grad = add([t0, t1_in, t2_in], BF16, [keep1])
    kept, moved = (keep0, keep1), (moved0, moved1)
    grad_out, grad_query, grad_key, grad_value = collect(place, kept, moved, [])
    return (input_grad[None], grad_query, grad_key, grad_value, grad_out)


def solution(mesh):
    return jax.shard_map(
        local,
        mesh=mesh,
        in_specs=(
            P("dp", "seq", None),
            P(None, "head"),
            P(None, "head"),
            P(None, "head"),
            P("head", None),
            P("dp", "seq", None),
        ),
        out_specs=(
            P("dp", "seq", "head"),
            P(("seq", "dp"), "head"),
            P(("seq", "dp"), "head"),
            P(("seq", "dp"), "head"),
            P("head", ("seq", "dp")),
        ),
        check_vma=False,
    )
```

```python
import functools

import jax
import jax.numpy as jnp
from jax import lax
from jax.experimental import pallas as pl
from jax.experimental.pallas import tpu as pltpu
from jax.sharding import PartitionSpec as P

HEAD_DIM = 128
BF16 = jnp.bfloat16
F32 = jnp.float32
MIB = 1024 * 1024
PLANNED = (2, 4, 4)
NN = ((1,), (0,))
NT = ((1,), (1,))
TN = ((0,), (0,))
ANYWHERE = pl.BlockSpec(memory_space=pl.ANY)
IN_VMEM = pl.BlockSpec(memory_space=pltpu.VMEM)
IN_SMEM = pl.BlockSpec(memory_space=pltpu.SMEM)


def dot(a, b, dims):
    return lax.dot_general(a, b, (dims, ((), ())), preferred_element_type=F32)


def shaped(shape, dtype):
    return jax.ShapeDtypeStruct(shape, dtype)


def params(mib):
    return pltpu.CompilerParams(vmem_limit_bytes=mib * MIB)


def cost(flops, size):
    return pl.CostEstimate(flops=flops, bytes_accessed=size, transcendentals=0)


class Place:
    def __init__(self, number, sizes):
        _, n_head, n_dp = sizes
        self.dp = lax.rem(number, n_dp)
        self.head = lax.rem(lax.div(number, n_dp), n_head)
        self.seq = lax.div(number, n_head * n_dp)
        self.core = lax.rem(self.dp, 2)


def position_scale(start, rows):
    positions = (start + lax.broadcasted_iota(jnp.int32, (rows, 1), 0)).astype(F32)
    return 1.0 / jnp.sqrt(HEAD_DIM * (positions + 1.0))


def project_part(place, part, xo_ref, wq_ref, wk_ref, wv_ref, wo_ref, out_ref, state_ref, arrived):
    rows, width = xo_ref.shape[1:]
    x_ref, o_ref = xo_ref.at[0], xo_ref.at[1]
    lower, upper = pl.ds(0, width // 2), pl.ds(width // 2, width // 2)

    def first(slot, w_ref):
        arrived(0)
        product = dot(x_ref[:, lower], w_ref[lower, :], NN)
        arrived(1)
        out_ref[slot] = (product + dot(x_ref[:, upper], w_ref[upper, :], NN)).astype(BF16)
        arrived(2)

    def state(slot):
        if state_ref is not None:
            for h in range(state_ref.shape[0]):
                at = pl.ds(h * HEAD_DIM, HEAD_DIM)
                state_ref[h] = dot(out_ref[slot, :, at], out_ref[slot + 1, :, at], TN)

    if part == 0:
        first(0, wk_ref)
        out_ref[1] = dot(x_ref[...], wv_ref[...], NN).astype(BF16)
    else:
        first(2, wq_ref)
        scale = position_scale(place.seq * rows, rows)
        out_ref[3] = (dot(o_ref[...], wo_ref[...], NT) * scale).astype(BF16)
    state(2 * part)


def load_kernel(
    number_ref, x_hbm, o_hbm, wq_hbm, wk_hbm, wv_hbm, wo_hbm,
    out_ref, state_ref, xo_ref, wq_ref, wk_ref, wv_ref, wo_ref, sems, *, sizes, which,
):
    place = Place(number_ref[0], sizes)
    mid = xo_ref.shape[2] // 2
    lower, upper = pl.ds(0, mid), pl.ds(mid, mid)
    x_ref, o_ref = xo_ref.at[0], xo_ref.at[1]

    def run(part):
        w_hbm, w_ref = ((wk_hbm, wk_ref), (wq_hbm, wq_ref))[part]
        v, q, k = (wv_hbm, wv_ref), (wq_hbm, wq_ref), (wk_hbm, wk_ref)
        o, w_o = (o_hbm, o_ref), (wo_hbm, wo_ref)
        pairs = [
            (x_hbm.at[:, lower], x_ref.at[:, lower]),
            (w_hbm.at[lower], w_ref.at[lower]),
            (x_hbm.at[:, upper], x_ref.at[:, upper]),
            (w_hbm.at[upper], w_ref.at[upper]),
            *((v, q, o, w_o) if part == 0 else (o, w_o, k, v)),
        ]
        copies = [pltpu.make_async_copy(a, b, sems.at[i]) for i, (a, b) in enumerate(pairs)]
        needed = (2, 4, 5 if part == 0 else 6)
        for c in copies[:4]:
            c.start()

        def arrived(stage):
            for c in copies[needed[stage - 1] if stage else 0 : needed[stage]]:
                c.wait()
            if stage == 0:
                for c in copies[4:]:
                    c.start()

        project_part(
            place, part, xo_ref, wq_ref, wk_ref, wv_ref, wo_ref, out_ref, state_ref, arrived
        )
        for c in copies[needed[2] :]:
            c.wait()

    chosen = which(place)
    pl.when(chosen == 0)(lambda: run(0))
    pl.when(chosen != 0)(lambda: run(1))


def load(place, which, in_rows, grad_rows, w_query, w_key, w_value, w_out):
    number, sizes = place
    rows, width = in_rows.shape
    hd = w_query.shape[1]
    args = [
        pltpu.with_memory_space_constraint(a, pltpu.HBM)
        for a in (in_rows, grad_rows, w_query, w_key, w_value, w_out)
    ]
    out_shape = [
        pltpu.VMEM((4, rows, hd), BF16),
        pltpu.VMEM((hd // HEAD_DIM, HEAD_DIM, HEAD_DIM), F32),
        pltpu.VMEM((2, rows, width), BF16),
        *[pltpu.VMEM((width, hd), BF16)] * 3,
        pltpu.VMEM((hd, width), BF16),
    ]
    return pl.pallas_call(
        functools.partial(load_kernel, sizes=sizes, which=which),
        out_shape=out_shape,
        in_specs=[IN_SMEM] + [ANYWHERE] * 6,
        out_specs=[IN_VMEM] * len(out_shape),
        scratch_shapes=[pltpu.SemaphoreType.DMA((8,))],
        compiler_params=params(16),
        cost_estimate=cost(4 * rows * width * hd, 14 * MIB),
        name="load",
    )(number, *args)


def project_kernel(place, part_ref, xo_ref, wq_ref, wk_ref, wv_ref, wo_ref, out_ref, *states, which):
    state_ref = states[0] if states else None

    def run(part):
        other = 2 - 2 * part
        out_ref[other : other + 2] = part_ref[other : other + 2]
        project_part(
            place, part, xo_ref, wq_ref, wk_ref, wv_ref, wo_ref, out_ref, state_ref, lambda stage: None
        )

    chosen = which(place)
    pl.when(chosen == 0)(lambda: run(0))
    pl.when(chosen != 0)(lambda: run(1))


def project(place, which, part, xo, weights, w_out, with_state):
    rows, width = xo.shape[1:]
    hd = part.shape[2]
    out = [shaped(part.shape, BF16)]
    if with_state:
        out.append(shaped((hd // HEAD_DIM, HEAD_DIM, HEAD_DIM), F32))
    kernel = functools.partial(project_kernel, which=which)
    args = [part, xo, *weights, w_out]
    return call(kernel, "project", out, args, 4 * rows * width * hd, (), place)


def call(kernel, name, out_shape, args, flops, after=(), place=None):
    n, n_after = len(args), len(after)
    numbers = [] if place is None else [place[0]]

    def body(*refs):
        first = [Place(refs[0][0], place[1])] if numbers else []
        refs = refs[len(numbers) :]
        kernel(*first, *refs[:n], *refs[n + n_after :])

    many = isinstance(out_shape, (list, tuple))
    return pl.pallas_call(
        body,
        out_shape=out_shape,
        in_specs=[IN_SMEM] * len(numbers) + [IN_VMEM] * n + [ANYWHERE] * n_after,
        out_specs=[IN_VMEM] * len(out_shape) if many else IN_VMEM,
        compiler_params=params(16),
        cost_estimate=cost(flops, 2 * MIB),
        name=name,
    )(*numbers, *args, *after)


def attend_kernel(place, in_ref, *rest, which, again):
    if again:
        state_ref, part_ref, scores_ref, out_ref = rest
    else:
        out_ref, scores_ref = rest
    rows, hd = in_ref.shape[1:]
    half = rows // 2
    top, low = slice(0, half), slice(half, rows)

    def causal(h, n, a, b):
        if not again:
            r = lax.broadcasted_iota(jnp.int32, (half, half), 0)
            c = lax.broadcasted_iota(jnp.int32, (half, half), 1)
            diagonal = r >= c
            scores_ref[h, n] = jnp.where(diagonal, dot(a[top], b[top], NT), 0.0).astype(BF16)
            scores_ref[h, n + 1] = dot(a[low], b[top], NT).astype(BF16)
            scores_ref[h, n + 2] = jnp.where(diagonal, dot(a[low], b[low], NT), 0.0).astype(BF16)
        return [scores_ref[h, n + i] for i in range(3)]

    def per_head(body):
        def step(h, carry):
            at = pl.ds(pl.multiple_of(h * HEAD_DIM, HEAD_DIM), HEAD_DIM)
            state = state_ref[h].astype(BF16) if again else None

            def put(slot, halves, cross, dims, scale=None):
                added = dot(cross, state, dims) if again else None
                for rows_at, value in zip((top, low), halves):
                    if again:
                        value = value + added[rows_at]
                    if scale is not None:
                        value = value * scale[rows_at]
                    out_ref[slot, rows_at, at] = value.astype(BF16)

            body(h, [in_ref[slot, :, at] for slot in range(4)], put)
            return carry

        lax.fori_loop(0, hd // HEAD_DIM, step, 0, unroll=2)

    def forward():
        scale = position_scale(place.seq * rows, rows)

        def body(h, heads, put):
            k, v, q, g = heads
            for slot, a, b, c, dims in ((0, q, k, v, NN), (1, g, v, k, NT)):
                s00, s10, s11 = causal(h, 3 * slot, a, b)
                halves = (dot(s00, c[top], NN), dot(s10, c[top], NN) + dot(s11, c[low], NN))
                put(slot, halves, a, dims, scale if slot == 0 else None)

        per_head(body)

    def backward():
        def body(h, heads, put):
            k, v, q, g = heads
            for slot, a, b, c, dims in ((2, q, k, g, NN), (3, g, v, q, NT)):
                s00, s10, s11 = causal(h, 3 * slot - 6, a, b)
                halves = (dot(s00, c[top], TN) + dot(s10, c[low], TN), dot(s11, c[low], TN))
                put(slot, halves, b, dims)

        per_head(body)

    chosen = which(place)
    if again:
        for t in (0, 1):
            out_ref[2 - 2 * chosen + t] = part_ref[2 - 2 * chosen + t]
    pl.when(chosen == 0)(forward)
    pl.when(chosen != 0)(backward)


def attend(place, which, projected, more=(), after=()):
    rows, hd = projected.shape[1:]
    out = shaped((4, rows, hd), BF16)
    scores = shaped((hd // HEAD_DIM, 6, rows // 2, rows // 2), BF16)
    kernel = functools.partial(attend_kernel, which=which, again=bool(more))
    outs = out if more else [out, scores]
    return call(kernel, "attend", outs, [projected, *more], 128 * rows * rows * hd, after, place)


def head_terms_kernel(place, d_ref, wq_ref, wk_ref, wv_ref, out_ref, *, shard):
    width = out_ref.shape[1]
    step = min(width, 256)
    start = shard(place) * width
    for i in range(width // step):
        rows = pl.ds(pl.multiple_of(start + i * step, step), step)
        out_ref[:, pl.ds(i * step, step)] = (
            dot(d_ref[1], wq_ref[rows, :], NT)
            + dot(d_ref[3], wk_ref[rows, :], NT)
            + dot(d_ref[2], wv_ref[rows, :], NT)
        )


def head_terms(place, results, weights, shard, shards, after=()):
    width, hd = weights[0].shape
    rows = results.shape[1]
    return call(
        functools.partial(head_terms_kernel, shard=shard),
        "head_terms",
        shaped((rows, width // shards), F32),
        [results, *weights],
        6 * rows * width // shards * hd,
        after,
        place,
    )


def add_kernel(*refs):
    total = refs[0][...]
    for ref in refs[1:-1]:
        total = total + ref[...]
    refs[-1][...] = total.astype(refs[-1].dtype)


def add(arrays, dtype, after=()):
    return call(add_kernel, "add", shaped(arrays[0].shape, dtype), list(arrays), 0, after)


def column_block(place, i):
    return (place.seq ^ (i // 2 % 2)) * 4 + (place.dp ^ (i % 2 * 2 + i // 4))


def fill_tiles(place, xo_ref, d_ref, pair, side, blocks, scale, added, outs):
    half = d_ref.shape[2] // 2
    block = outs[0].shape[1]
    features = pl.ds(pl.multiple_of(side * half, half), half)
    for i, b in enumerate(blocks):
        columns = pl.ds(pl.multiple_of(column_block(place, b) * block, block), block)
        for t, rows in enumerate((1 - pair, 0)):
            tile = dot(xo_ref[rows, :, columns], d_ref[2 * pair + t, :, features], TN) * scale
            for read in added:
                tile = tile + read(i, t)
            outs[i][t] = tile


def other_core_kernel(place, xo_ref, d_ref, out_ref, *, early, slot, scale):
    outs = [out_ref.at[i] for i in range(4)]
    pair, side = place.seq ^ early, 1 - place.core ^ slot
    fill_tiles(place, xo_ref, d_ref, pair, side, (4, 5, 6, 7), scale, (), outs)


def first_hop_kernel(place, xo_ref, d_ref, far_ref, out_ref, *, early, slot, scale):
    pair, side = place.seq ^ early, place.core ^ slot
    blocks = (2 - side, 3)
    outs = [out_ref.at[i] for i in range(2)]
    added = (lambda i, t: far_ref[blocks[i], t],)
    fill_tiles(place, xo_ref, d_ref, pair, side, blocks, scale, added, outs)


def second_hop_kernel(
    place, xo_ref, d_ref, far0_ref, far1_ref, over0_ref, over1_ref, keep_ref, send_ref,
    *, slot, scale,
):
    over = (over0_ref, over1_ref)
    side = place.core ^ slot
    blocks = (0, 1 + side)

    def far(p, i, t):
        return (far0_ref, far1_ref)[p][blocks[i], t]

    for p in (0, 1):
        added = (
            lambda i, t: jnp.where(side == 0, far(1 - p, i, t), far(p, i, t)),
            lambda i, t: over[p][i, t],
        )
        pair = place.seq ^ p ^ 1 - side
        outs = (keep_ref.at[p], send_ref.at[p])
        fill_tiles(place, xo_ref, d_ref, pair, side, blocks, scale, added, outs)


def settle_kernel(place, kept_ref, moved_ref, out_ref, *, slot):
    side = place.core ^ slot
    for p in (0, 1):
        for t in (0, 1):
            out_ref[p, t] = kept_ref[p ^ 1 - side, t] + moved_ref[1 - p, t]


def finish_kernel(place, *refs):
    line, (sums_ref, kept_ref, moved_ref) = refs[:3], refs[3:6]
    input_ref, out_ref, query_ref, key_ref, value_ref = refs[6:]
    half = query_ref.shape[1] // 2
    input_ref[...] = (line[0][...] + line[1][...] + line[2][...]).astype(BF16)
    for side in (0, 1):
        at = pl.ds(side * half, half)

        def total(pair, t):
            p = place.seq ^ pair
            late = kept_ref[p ^ 1 - side, t] + moved_ref[1 - p, t]
            return jnp.where(place.core == side, sums_ref[p, t], late)

        out_ref[at, :] = total(0, 0).T
        query_ref[:, at] = total(0, 1)
        value_ref[:, at] = total(1, 0)
        key_ref[:, at] = total(1, 1)


def finish(place, line, sums, kept, moved):
    block, half = kept.shape[2:]
    tall, wide = shaped((block, 2 * half), F32), shaped((2 * half, block), F32)
    outs = [shaped(line[0].shape, BF16), wide, tall, tall, tall]
    return call(finish_kernel, "finish", outs, [*line, sums, kept, moved], 0, (), place)


def states_before(x, axis, reverse):
    peers, here = (lax.axis_size(axis), lax.axis_index(axis))
    everything = lax.all_gather(x, axis)
    at = jnp.arange(peers)
    reached = at > here if reverse else at < here
    return jnp.sum(jnp.where(reached[:, None, None, None], everything, 0.0), axis=0)


def swap(x, axis, bit):
    return lax.ppermute(x, axis, [(i, i ^ bit) for i in range(lax.axis_size(axis))])


def local(layer_input, w_query, w_key, w_value, w_out, out_grad):
    num_rows = layer_input.shape[1]
    n_seq, n_head, n_dp = (lax.axis_size(a) for a in ("seq", "head", "dp"))
    scale = float(n_seq * n_dp * num_rows) ** -0.5

    sizes = (n_seq, n_head, n_dp)
    number = (lax.axis_index("seq") * n_head + lax.axis_index("head")) * n_dp + lax.axis_index("dp")
    number = number.astype(jnp.int32).reshape(1)
    place = (number, sizes)
    arrays = (layer_input[0], out_grad[0], w_query, w_key, w_value, w_out)
    planned = sizes == PLANNED
    part = (lambda at: at.seq) if planned else (lambda at: 0)
    projected, state, xo, *weights, wo = load(place, part, *arrays)
    if planned:
        state = swap(state, "seq", 1)
    projected, *more = project(
        place, lambda at: 1 - part(at), projected, xo, weights, wo, not planned
    )

    if not planned:
        prefix = states_before(state, "seq", False)
        suffix = states_before(more[0], "seq", True)
        d, scores = attend(place, lambda at: 0, projected)
        d = attend(place, lambda at: 0, projected, (prefix, d, scores))
        d = attend(place, lambda at: 1, projected, (suffix, d, scores))
        terms = head_terms(place, d, weights, lambda at: 0, 1)

        def reduced(rows, d):
            return lax.psum_scatter(
                dot(rows, d, TN) * scale, ("seq", "dp"), scatter_dimension=0, tiled=True
            )

        return (
            lax.psum_scatter(terms, "head", scatter_dimension=1, tiled=True).astype(BF16)[None],
            reduced(xo[0], d[1]),
            reduced(xo[0], d[3]),
            reduced(xo[0], d[2]),
            reduced(xo[1], d[0]).T,
        )

    def term(flip, after):
        return head_terms(place, d, weights, lambda at: at.head ^ flip, n_head, after)

    def hop(array, slot, second):
        pairs = []
        for i in range(8):
            side = i % 2 ^ slot
            pairs.append((i, i ^ (4 if side == second else 2)))
        return lax.ppermute(array, ("seq", "dp"), pairs)

    block, half = xo.shape[2] // 8, projected.shape[2] // 2
    tile = (2, block, half)
    flops = 4 * num_rows * block * half

    def to_core(d, early, slot, after):
        kernel = functools.partial(other_core_kernel, early=early, slot=slot, scale=scale)
        out = shaped((4, *tile), F32)
        array = call(kernel, "other_core", out, [xo, d], 4 * flops, after, place)
        return array, swap(array, "dp", 1)

    def first_hop(early, slot, after):
        kernel = functools.partial(first_hop_kernel, early=early, slot=slot, scale=scale)
        out = shaped((2, *tile), F32)
        args = [xo, d, far[early][slot]]
        array = call(kernel, "first_hop", out, args, 2 * flops, after, place)
        return array, hop(array, slot, 0)

    def second_hop(slot, over, after):
        kernel = functools.partial(second_hop_kernel, slot=slot, scale=scale)
        outs = [shaped((2, *tile), F32)] * 2
        args = [xo, d, far[0][slot], far[1][slot], *over]
        keep, leave = call(kernel, "second_hop", outs, args, 4 * flops, after, place)
        return keep, hop(leave, slot, 1)

    early, scores = attend(place, lambda at: at.seq, projected)
    far = ([None, None], [None, None])
    at, far[0][0] = to_core(early, 0, 0, [])
    at, far[0][1] = to_core(early, 0, 1, [at])
    d = attend(place, lambda at: 1 - at.seq, projected, (state, early, scores), [at])
    at, far[1][0] = to_core(d, 1, 0, [])
    at, far[1][1] = to_core(d, 1, 1, [at])
    at, over1 = first_hop(0, 0, [at])
    t3 = term(3, [at])
    t3_in = swap(t3, "head", 1)
    at, over2 = first_hop(0, 1, [t3])
    at, over3 = first_hop(1, 0, [at])
    at, over4 = first_hop(1, 1, [at])
    t2 = term(2, [at])
    t0 = term(0, [t2])
    t1 = term(1, [t0, over1])
    t1_in = swap(t1, "head", 1)
    t2 = add([t2, t3_in], F32, [t1])
    t2_in = swap(t2, "head", 2)
    keep0, moved0 = second_hop(0, (over1, over3), [t2, over2])
    keep1, moved1 = second_hop(1, (over2, over4), [keep0])
    settle = functools.partial(settle_kernel, slot=0)
    sums = call(settle, "settle", shaped(keep0.shape, F32), [keep0, moved0], 0, [keep1], place)
    outs = finish(place, (t0, t1_in, t2_in), sums, keep1, moved1)
    input_grad, grad_out, grad_query, grad_key, grad_value = outs
    return (input_grad[None], grad_query, grad_key, grad_value, grad_out)


def solution(mesh):
    return jax.shard_map(
        local,
        mesh=mesh,
        in_specs=(
            P("dp", "seq", None),
            P(None, "head"),
            P(None, "head"),
            P(None, "head"),
            P("head", None),
            P("dp", "seq", None),
        ),
        out_specs=(
            P("dp", "seq", "head"),
            P(("seq", "dp"), "head"),
            P(("seq", "dp"), "head"),
            P(("seq", "dp"), "head"),
            P("head", ("seq", "dp")),
        ),
        check_vma=False,
    )
```

```python
import functools

import jax
import jax.numpy as jnp
from jax import lax
from jax.experimental import pallas as pl
from jax.experimental.pallas import tpu as pltpu
from jax.sharding import PartitionSpec as P

HEAD_DIM = 128
BF16 = jnp.bfloat16
F32 = jnp.float32
MIB = 1024 * 1024
PLANNED = (2, 4, 4)
NN = ((1,), (0,))
NT = ((1,), (1,))
TN = ((0,), (0,))
ANYWHERE = pl.BlockSpec(memory_space=pl.ANY)
IN_VMEM = pl.BlockSpec(memory_space=pltpu.VMEM)
IN_SMEM = pl.BlockSpec(memory_space=pltpu.SMEM)


def dot(a, b, dims):
    return lax.dot_general(a, b, (dims, ((), ())), preferred_element_type=F32)


def shaped(shape, dtype):
    return jax.ShapeDtypeStruct(shape, dtype)


def params(mib):
    return pltpu.CompilerParams(vmem_limit_bytes=mib * MIB)


def cost(flops, size):
    return pl.CostEstimate(flops=flops, bytes_accessed=size, transcendentals=0)


class Place:
    def __init__(self, number, sizes):
        _, n_head, n_dp = sizes
        self.dp = lax.rem(number, n_dp)
        self.head = lax.rem(lax.div(number, n_dp), n_head)
        self.seq = lax.div(number, n_head * n_dp)
        self.core = lax.rem(self.dp, 2)


def position_scale(start, rows):
    positions = (start + lax.broadcasted_iota(jnp.int32, (rows, 1), 0)).astype(F32)
    return 1.0 / jnp.sqrt(HEAD_DIM * (positions + 1.0))


def project_part(place, part, xo_ref, wq_ref, wk_ref, wv_ref, wo_ref, out_ref, state_ref, arrived):
    rows, width = xo_ref.shape[1:]
    x_ref, o_ref = xo_ref.at[0], xo_ref.at[1]
    lower, upper = pl.ds(0, width // 2), pl.ds(width // 2, width // 2)

    def first(slot, w_ref):
        arrived(0)
        product = dot(x_ref[:, lower], w_ref[lower, :], NN)
        arrived(1)
        out_ref[slot] = (product + dot(x_ref[:, upper], w_ref[upper, :], NN)).astype(BF16)
        arrived(2)

    def state(slot):
        if state_ref is not None:
            for h in range(state_ref.shape[0]):
                at = pl.ds(h * HEAD_DIM, HEAD_DIM)
                state_ref[h] = dot(out_ref[slot, :, at], out_ref[slot + 1, :, at], TN)

    if part == 0:
        first(0, wk_ref)
        out_ref[1] = dot(x_ref[...], wv_ref[...], NN).astype(BF16)
    else:
        first(2, wq_ref)
        scale = position_scale(place.seq * rows, rows)
        out_ref[3] = (dot(o_ref[...], wo_ref[...], NT) * scale).astype(BF16)
    state(2 * part)


def load_kernel(
    number_ref, x_hbm, o_hbm, wq_hbm, wk_hbm, wv_hbm, wo_hbm,
    out_ref, state_ref, xo_ref, wq_ref, wk_ref, wv_ref, wo_ref, sems, *, sizes, which,
):
    place = Place(number_ref[0], sizes)
    mid = xo_ref.shape[2] // 2
    lower, upper = pl.ds(0, mid), pl.ds(mid, mid)
    x_ref, o_ref = xo_ref.at[0], xo_ref.at[1]

    def run(part):
        w_hbm, w_ref = ((wk_hbm, wk_ref), (wq_hbm, wq_ref))[part]
        v, q, k = (wv_hbm, wv_ref), (wq_hbm, wq_ref), (wk_hbm, wk_ref)
        o, w_o = (o_hbm, o_ref), (wo_hbm, wo_ref)
        pairs = [
            (x_hbm.at[:, lower], x_ref.at[:, lower]),
            (w_hbm.at[lower], w_ref.at[lower]),
            (x_hbm.at[:, upper], x_ref.at[:, upper]),
            (w_hbm.at[upper], w_ref.at[upper]),
            *((v, q, o, w_o) if part == 0 else (o, w_o, k, v)),
        ]
        copies = [pltpu.make_async_copy(a, b, sems.at[i]) for i, (a, b) in enumerate(pairs)]
        needed = (2, 4, 5 if part == 0 else 6)
        for c in copies[:4]:
            c.start()

        def arrived(stage):
            for c in copies[needed[stage - 1] if stage else 0 : needed[stage]]:
                c.wait()
            if stage == 0:
                for c in copies[4:]:
                    c.start()

        project_part(
            place, part, xo_ref, wq_ref, wk_ref, wv_ref, wo_ref, out_ref, state_ref, arrived
        )
        for c in copies[needed[2] :]:
            c.wait()

    chosen = which(place)
    pl.when(chosen == 0)(lambda: run(0))
    pl.when(chosen != 0)(lambda: run(1))


def load(place, which, in_rows, grad_rows, w_query, w_key, w_value, w_out):
    number, sizes = place
    rows, width = in_rows.shape
    hd = w_query.shape[1]
    args = [
        pltpu.with_memory_space_constraint(a, pltpu.HBM)
        for a in (in_rows, grad_rows, w_query, w_key, w_value, w_out)
    ]
    out_shape = [
        pltpu.VMEM((4, rows, hd), BF16),
        pltpu.VMEM((hd // HEAD_DIM, HEAD_DIM, HEAD_DIM), F32),
        pltpu.VMEM((2, rows, width), BF16),
        *[pltpu.VMEM((width, hd), BF16)] * 3,
        pltpu.VMEM((hd, width), BF16),
    ]
    return pl.pallas_call(
        functools.partial(load_kernel, sizes=sizes, which=which),
        out_shape=out_shape,
        in_specs=[IN_SMEM] + [ANYWHERE] * 6,
        out_specs=[IN_VMEM] * len(out_shape),
        scratch_shapes=[pltpu.SemaphoreType.DMA((8,))],
        compiler_params=params(16),
        cost_estimate=cost(4 * rows * width * hd, 14 * MIB),
        name="load",
    )(number, *args)


def project_kernel(place, part_ref, xo_ref, wq_ref, wk_ref, wv_ref, wo_ref, out_ref, *states, which):
    state_ref = states[0] if states else None

    def run(part):
        other = 2 - 2 * part
        out_ref[other : other + 2] = part_ref[other : other + 2]
        project_part(
            place, part, xo_ref, wq_ref, wk_ref, wv_ref, wo_ref, out_ref, state_ref, lambda stage: None
        )

    chosen = which(place)
    pl.when(chosen == 0)(lambda: run(0))
    pl.when(chosen != 0)(lambda: run(1))


def project(place, which, part, xo, weights, w_out, with_state):
    rows, width = xo.shape[1:]
    hd = part.shape[2]
    out = [shaped(part.shape, BF16)]
    if with_state:
        out.append(shaped((hd // HEAD_DIM, HEAD_DIM, HEAD_DIM), F32))
    kernel = functools.partial(project_kernel, which=which)
    args = [part, xo, *weights, w_out]
    return call(kernel, "project", out, args, 4 * rows * width * hd, (), place)


def call(kernel, name, out_shape, args, flops, after=(), place=None):
    n, n_after = len(args), len(after)
    numbers = [] if place is None else [place[0]]

    def body(*refs):
        first = [Place(refs[0][0], place[1])] if numbers else []
        refs = refs[len(numbers) :]
        kernel(*first, *refs[:n], *refs[n + n_after :])

    many = isinstance(out_shape, (list, tuple))
    return pl.pallas_call(
        body,
        out_shape=out_shape,
        in_specs=[IN_SMEM] * len(numbers) + [IN_VMEM] * n + [ANYWHERE] * n_after,
        out_specs=[IN_VMEM] * len(out_shape) if many else IN_VMEM,
        compiler_params=params(16),
        cost_estimate=cost(flops, 2 * MIB),
        name=name,
    )(*numbers, *args, *after)


def attend_kernel(place, in_ref, *rest, which, again):
    if again:
        state_ref, part_ref, scores_ref, out_ref = rest
    else:
        out_ref, scores_ref = rest
    rows, hd = in_ref.shape[1:]
    half = rows // 2
    top, low = slice(0, half), slice(half, rows)

    def causal(h, n, a, b):
        if not again:
            r = lax.broadcasted_iota(jnp.int32, (half, half), 0)
            c = lax.broadcasted_iota(jnp.int32, (half, half), 1)
            diagonal = r >= c
            scores_ref[h, n] = jnp.where(diagonal, dot(a[top], b[top], NT), 0.0).astype(BF16)
            scores_ref[h, n + 1] = dot(a[low], b[top], NT).astype(BF16)
            scores_ref[h, n + 2] = jnp.where(diagonal, dot(a[low], b[low], NT), 0.0).astype(BF16)
        return [scores_ref[h, n + i] for i in range(3)]

    def per_head(body):
        def step(h, carry):
            at = pl.ds(pl.multiple_of(h * HEAD_DIM, HEAD_DIM), HEAD_DIM)
            state = state_ref[h].astype(BF16) if again else None

            def put(slot, halves, cross, dims, scale=None):
                added = dot(cross, state, dims) if again else None
                for rows_at, value in zip((top, low), halves):
                    if again:
                        value = value + added[rows_at]
                    if scale is not None:
                        value = value * scale[rows_at]
                    out_ref[slot, rows_at, at] = value.astype(BF16)

            body(h, [in_ref[slot, :, at] for slot in range(4)], put)
            return carry

        lax.fori_loop(0, hd // HEAD_DIM, step, 0, unroll=True)

    def forward():
        scale = position_scale(place.seq * rows, rows)

        def body(h, heads, put):
            k, v, q, g = heads
            for slot, a, b, c, dims in ((0, q, k, v, NN), (1, g, v, k, NT)):
                s00, s10, s11 = causal(h, 3 * slot, a, b)
                halves = (dot(s00, c[top], NN), dot(s10, c[top], NN) + dot(s11, c[low], NN))
                put(slot, halves, a, dims, scale if slot == 0 else None)

        per_head(body)

    def backward():
        def body(h, heads, put):
            k, v, q, g = heads
            for slot, a, b, c, dims in ((2, q, k, g, NN), (3, g, v, q, NT)):
                s00, s10, s11 = causal(h, 3 * slot - 6, a, b)
                halves = (dot(s00, c[top], TN) + dot(s10, c[low], TN), dot(s11, c[low], TN))
                put(slot, halves, b, dims)

        per_head(body)

    chosen = which(place)
    if again:
        for t in (0, 1):
            out_ref[2 - 2 * chosen + t] = part_ref[2 - 2 * chosen + t]
    pl.when(chosen == 0)(forward)
    pl.when(chosen != 0)(backward)


def attend(place, which, projected, more=(), after=()):
    rows, hd = projected.shape[1:]
    out = shaped((4, rows, hd), BF16)
    scores = shaped((hd // HEAD_DIM, 6, rows // 2, rows // 2), BF16)
    kernel = functools.partial(attend_kernel, which=which, again=bool(more))
    outs = out if more else [out, scores]
    return call(kernel, "attend", outs, [projected, *more], 128 * rows * rows * hd, after, place)


def head_terms_kernel(place, d_ref, wq_ref, wk_ref, wv_ref, out_ref, *, shard):
    width = out_ref.shape[1]
    step = min(width, 256)
    start = shard(place) * width
    for i in range(width // step):
        rows = pl.ds(pl.multiple_of(start + i * step, step), step)
        out_ref[:, pl.ds(i * step, step)] = (
            dot(d_ref[1], wq_ref[rows, :], NT)
            + dot(d_ref[3], wk_ref[rows, :], NT)
            + dot(d_ref[2], wv_ref[rows, :], NT)
        )


def head_terms(place, results, weights, shard, shards, after=()):
    width, hd = weights[0].shape
    rows = results.shape[1]
    return call(
        functools.partial(head_terms_kernel, shard=shard),
        "head_terms",
        shaped((rows, width // shards), F32),
        [results, *weights],
        6 * rows * width // shards * hd,
        after,
        place,
    )


def add_kernel(*refs):
    total = refs[0][...]
    for ref in refs[1:-1]:
        total = total + ref[...]
    refs[-1][...] = total.astype(refs[-1].dtype)


def add(arrays, dtype, after=()):
    return call(add_kernel, "add", shaped(arrays[0].shape, dtype), list(arrays), 0, after)


def column_block(place, i):
    return (place.seq ^ (i // 2 % 2)) * 4 + (place.dp ^ (i % 2 * 2 + i // 4))


def fill_tiles(place, xo_ref, d_ref, pair, side, blocks, scale, added, outs):
    half = d_ref.shape[2] // 2
    block = outs[0].shape[1]
    features = pl.ds(pl.multiple_of(side * half, half), half)
    for i, b in enumerate(blocks):
        columns = pl.ds(pl.multiple_of(column_block(place, b) * block, block), block)
        for t, rows in enumerate((1 - pair, 0)):
            tile = dot(xo_ref[rows, :, columns], d_ref[2 * pair + t, :, features], TN) * scale
            for read in added:
                tile = tile + read(i, t)
            outs[i][t] = tile


def other_core_kernel(place, xo_ref, d_ref, out_ref, *, early, slot, scale):
    outs = [out_ref.at[i] for i in range(4)]
    pair, side = place.seq ^ early, 1 - place.core ^ slot
    fill_tiles(place, xo_ref, d_ref, pair, side, (4, 5, 6, 7), scale, (), outs)


def other_core_both_kernel(place, xo_ref, d_ref, *out_refs, early, scale):
    pair = place.seq ^ early
    half = d_ref.shape[2] // 2
    block = out_refs[0].shape[2]
    sides = (1 - place.core, place.core)
    for t, rows in enumerate((1 - pair, 0)):
        features = [pl.ds(pl.multiple_of(side * half, half), half) for side in sides]
        d = jnp.concatenate([d_ref[2 * pair + t, :, at] for at in features], axis=1)
        for i in range(4):
            columns = pl.ds(pl.multiple_of(column_block(place, 4 + i) * block, block), block)
            tile = dot(xo_ref[rows, :, columns], d, TN) * scale
            out_refs[0][i, t] = tile[:, :half]
            out_refs[1][i, t] = tile[:, half:]


def first_hop_kernel(place, xo_ref, d_ref, far_ref, out_ref, *, early, slot, scale):
    pair, side = place.seq ^ early, place.core ^ slot
    blocks = (2 - side, 3)
    outs = [out_ref.at[i] for i in range(2)]
    added = (lambda i, t: far_ref[blocks[i], t],)
    fill_tiles(place, xo_ref, d_ref, pair, side, blocks, scale, added, outs)


def second_hop_kernel(
    place, xo_ref, d_ref, far0_ref, far1_ref, over0_ref, over1_ref, keep_ref, send_ref,
    *, slot, scale,
):
    over = (over0_ref, over1_ref)
    side = place.core ^ slot
    blocks = (0, 1 + side)

    def far(p, i, t):
        return (far0_ref, far1_ref)[p][blocks[i], t]

    for p in (0, 1):
        added = (
            lambda i, t: jnp.where(side == 0, far(1 - p, i, t), far(p, i, t)),
            lambda i, t: over[p][i, t],
        )
        pair = place.seq ^ p ^ 1 - side
        outs = (keep_ref.at[p], send_ref.at[p])
        fill_tiles(place, xo_ref, d_ref, pair, side, blocks, scale, added, outs)


def put_side(place, slot, kept_ref, moved_ref, part_ref, out_refs, sems):
    side = place.core ^ slot
    half = part_ref.shape[1]
    at = pl.ds(pl.multiple_of(side * half, half), half)
    copies = []
    for i, (pair, t) in enumerate(((0, 1), (1, 1), (1, 0), (0, 0))):
        p = place.seq ^ pair
        total = kept_ref[p ^ 1 - side, t] + moved_ref[1 - p, t]
        part_ref[i] = total if i < 3 else total.T
        out = out_refs[i].at[:, at] if i < 3 else out_refs[i].at[at]
        copies.append(pltpu.make_async_copy(part_ref.at[i], out, sems.at[i]))
        copies[-1].start()
    return copies


def settle_kernel(number_ref, kept_ref, moved_ref, after_ref, *rest, sizes):
    out_refs, (part_ref, sems) = rest[:4], rest[4:]
    place = Place(number_ref[0], sizes)
    for c in put_side(place, 0, kept_ref, moved_ref, part_ref, out_refs, sems):
        c.wait()


def finish_kernel(number_ref, *refs, sizes):
    line, (kept_ref, moved_ref) = refs[:3], refs[3:5]
    input_out, out_refs, (part_ref, input_ref, sems) = refs[9], refs[10:14], refs[14:]
    place = Place(number_ref[0], sizes)
    input_ref[...] = (line[0][...] + line[1][...] + line[2][...]).astype(BF16)
    last = pltpu.make_async_copy(input_ref, input_out, sems.at[4])
    last.start()
    for c in put_side(place, 1, kept_ref, moved_ref, part_ref, out_refs, sems):
        c.wait()
    last.wait()


def finish(place, line, kept, moved):
    number, sizes = place
    block, half = kept[0].shape[2:]
    tall, wide = pltpu.HBM((block, 2 * half), F32), pltpu.HBM((2 * half, block), F32)
    grads = [tall, tall, tall, wide]
    parts = pltpu.VMEM((4, block, half), F32)
    sides = pl.pallas_call(
        functools.partial(settle_kernel, sizes=sizes),
        out_shape=grads,
        in_specs=[IN_SMEM, IN_VMEM, IN_VMEM, ANYWHERE],
        out_specs=[ANYWHERE] * 4,
        scratch_shapes=[parts, pltpu.SemaphoreType.DMA((4,))],
        compiler_params=params(16),
        cost_estimate=cost(0, 2 * MIB),
        name="settle",
    )(number, kept[0], moved[0], kept[1])
    return pl.pallas_call(
        functools.partial(finish_kernel, sizes=sizes),
        out_shape=[pltpu.HBM(line[0].shape, BF16), *grads],
        in_specs=[IN_SMEM] + [IN_VMEM] * 5 + [ANYWHERE] * 4,
        out_specs=[ANYWHERE] * 5,
        input_output_aliases={6 + i: 1 + i for i in range(4)},
        scratch_shapes=[parts, pltpu.VMEM(line[0].shape, BF16), pltpu.SemaphoreType.DMA((5,))],
        compiler_params=params(16),
        cost_estimate=cost(0, 2 * MIB),
        name="finish",
    )(number, *line, kept[1], moved[1], *sides)


def states_before(x, axis, reverse):
    peers, here = (lax.axis_size(axis), lax.axis_index(axis))
    everything = lax.all_gather(x, axis)
    at = jnp.arange(peers)
    reached = at > here if reverse else at < here
    return jnp.sum(jnp.where(reached[:, None, None, None], everything, 0.0), axis=0)


def swap(x, axis, bit):
    return lax.ppermute(x, axis, [(i, i ^ bit) for i in range(lax.axis_size(axis))])


def local(layer_input, w_query, w_key, w_value, w_out, out_grad):
    num_rows = layer_input.shape[1]
    n_seq, n_head, n_dp = (lax.axis_size(a) for a in ("seq", "head", "dp"))
    scale = float(n_seq * n_dp * num_rows) ** -0.5

    sizes = (n_seq, n_head, n_dp)
    number = (lax.axis_index("seq") * n_head + lax.axis_index("head")) * n_dp + lax.axis_index("dp")
    number = number.astype(jnp.int32).reshape(1)
    place = (number, sizes)
    arrays = (layer_input[0], out_grad[0], w_query, w_key, w_value, w_out)
    planned = sizes == PLANNED
    part = (lambda at: at.seq) if planned else (lambda at: 0)
    projected, state, xo, *weights, wo = load(place, part, *arrays)
    if planned:
        state = swap(state, "seq", 1)
    projected, *more = project(
        place, lambda at: 1 - part(at), projected, xo, weights, wo, not planned
    )

    if not planned:
        prefix = states_before(state, "seq", False)
        suffix = states_before(more[0], "seq", True)
        d, scores = attend(place, lambda at: 0, projected)
        d = attend(place, lambda at: 0, projected, (prefix, d, scores))
        d = attend(place, lambda at: 1, projected, (suffix, d, scores))
        terms = head_terms(place, d, weights, lambda at: 0, 1)

        def reduced(rows, d):
            return lax.psum_scatter(
                dot(rows, d, TN) * scale, ("seq", "dp"), scatter_dimension=0, tiled=True
            )

        return (
            lax.psum_scatter(terms, "head", scatter_dimension=1, tiled=True).astype(BF16)[None],
            reduced(xo[0], d[1]),
            reduced(xo[0], d[3]),
            reduced(xo[0], d[2]),
            reduced(xo[1], d[0]).T,
        )

    def term(flip, after):
        return head_terms(place, d, weights, lambda at: at.head ^ flip, n_head, after)

    def hop(array, slot, second):
        pairs = []
        for i in range(8):
            side = i % 2 ^ slot
            pairs.append((i, i ^ (4 if side == second else 2)))
        return lax.ppermute(array, ("seq", "dp"), pairs)

    block, half = xo.shape[2] // 8, projected.shape[2] // 2
    tile = (2, block, half)
    flops = 4 * num_rows * block * half

    def to_core(d, early, slot, after):
        kernel = functools.partial(other_core_kernel, early=early, slot=slot, scale=scale)
        out = shaped((4, *tile), F32)
        array = call(kernel, "other_core", out, [xo, d], 4 * flops, after, place)
        return array, swap(array, "dp", 1)

    def both_to_core(d, early, after):
        kernel = functools.partial(other_core_both_kernel, early=early, scale=scale)
        outs = [shaped((4, *tile), F32)] * 2
        arrays = call(kernel, "other_core_both", outs, [xo, d], 8 * flops, after, place)
        return arrays[0], [swap(array, "dp", 1) for array in arrays]

    def first_hop(early, slot, after):
        kernel = functools.partial(first_hop_kernel, early=early, slot=slot, scale=scale)
        out = shaped((2, *tile), F32)
        args = [xo, d, far[early][slot]]
        array = call(kernel, "first_hop", out, args, 2 * flops, after, place)
        return array, hop(array, slot, 0)

    def second_hop(slot, over, after):
        kernel = functools.partial(second_hop_kernel, slot=slot, scale=scale)
        outs = [shaped((2, *tile), F32)] * 2
        args = [xo, d, far[0][slot], far[1][slot], *over]
        keep, leave = call(kernel, "second_hop", outs, args, 4 * flops, after, place)
        return keep, hop(leave, slot, 1)

    early, scores = attend(place, lambda at: at.seq, projected)
    far = ([None, None], [None, None])
    at, far[0][0] = to_core(early, 0, 0, [])
    at, far[0][1] = to_core(early, 0, 1, [at])
    d = attend(place, lambda at: 1 - at.seq, projected, (state, early, scores), [at])
    at, far[1][:] = both_to_core(d, 1, [])
    at, over1 = first_hop(0, 0, [at])
    t3 = term(3, [at])
    t3_in = swap(t3, "head", 1)
    at, over2 = first_hop(0, 1, [t3])
    at, over3 = first_hop(1, 0, [at])
    at, over4 = first_hop(1, 1, [at])
    t2 = term(2, [at])
    t0 = term(0, [t2])
    t1 = term(1, [t0, over1])
    t1_in = swap(t1, "head", 1)
    t2 = add([t2, t3_in], F32, [t1])
    t2_in = swap(t2, "head", 2)
    keep0, moved0 = second_hop(0, (over1, over3), [t2, over2])
    keep1, moved1 = second_hop(1, (over2, over4), [keep0])
    outs = finish(place, (t0, t1_in, t2_in), (keep0, keep1), (moved0, moved1))
    input_grad, grad_query, grad_key, grad_value, grad_out = outs
    return (input_grad[None], grad_query, grad_key, grad_value, grad_out)


def solution(mesh):
    return jax.shard_map(
        local,
        mesh=mesh,
        in_specs=(
            P("dp", "seq", None),
            P(None, "head"),
            P(None, "head"),
            P(None, "head"),
            P("head", None),
            P("dp", "seq", None),
        ),
        out_specs=(
            P("dp", "seq", "head"),
            P(("seq", "dp"), "head"),
            P(("seq", "dp"), "head"),
            P(("seq", "dp"), "head"),
            P("head", ("seq", "dp")),
        ),
        check_vma=False,
    )
```

```python
import functools

import jax
import jax.numpy as jnp
from jax import lax
from jax.experimental import pallas as pl
from jax.experimental.pallas import tpu as pltpu
from jax.sharding import PartitionSpec as P

HEAD_DIM = 128
BF16 = jnp.bfloat16
F32 = jnp.float32
MIB = 1024 * 1024
PLANNED = (2, 4, 4)
NN = ((1,), (0,))
NT = ((1,), (1,))
TN = ((0,), (0,))
ANYWHERE = pl.BlockSpec(memory_space=pl.ANY)
IN_VMEM = pl.BlockSpec(memory_space=pltpu.VMEM)
IN_SMEM = pl.BlockSpec(memory_space=pltpu.SMEM)


def dot(a, b, dims):
    return lax.dot_general(a, b, (dims, ((), ())), preferred_element_type=F32)


def shaped(shape, dtype):
    return jax.ShapeDtypeStruct(shape, dtype)


def params(mib):
    return pltpu.CompilerParams(vmem_limit_bytes=mib * MIB)


def cost(flops, size):
    return pl.CostEstimate(flops=flops, bytes_accessed=size, transcendentals=0)


class Place:
    def __init__(self, number, sizes):
        _, n_head, n_dp = sizes
        self.dp = lax.rem(number, n_dp)
        self.head = lax.rem(lax.div(number, n_dp), n_head)
        self.seq = lax.div(number, n_head * n_dp)
        self.core = lax.rem(self.dp, 2)


def position_scale(start, rows):
    positions = (start + lax.broadcasted_iota(jnp.int32, (rows, 1), 0)).astype(F32)
    return 1.0 / jnp.sqrt(HEAD_DIM * (positions + 1.0))


def project_part(place, part, xo_ref, wq_ref, wk_ref, wv_ref, wo_ref, out_ref, state_ref, arrived):
    rows, width = xo_ref.shape[1:]
    x_ref, o_ref = xo_ref.at[0], xo_ref.at[1]
    lower, upper = pl.ds(0, width // 2), pl.ds(width // 2, width // 2)

    def first(w_ref):
        arrived(0)
        product = dot(x_ref[:, lower], w_ref[lower, :], NN)
        arrived(1)
        out_ref[0] = (product + dot(x_ref[:, upper], w_ref[upper, :], NN)).astype(BF16)
        arrived(2)

    def state():
        if state_ref is not None:
            for h in range(state_ref.shape[0]):
                at = pl.ds(h * HEAD_DIM, HEAD_DIM)
                state_ref[h] = dot(out_ref[0, :, at], out_ref[1, :, at], TN)

    if part == 0:
        first(wk_ref)
        out_ref[1] = dot(x_ref[...], wv_ref[...], NN).astype(BF16)
    else:
        first(wq_ref)
        scale = position_scale(place.seq * rows, rows)
        out_ref[1] = (dot(o_ref[...], wo_ref[...], NT) * scale).astype(BF16)
    state()


def load_kernel(
    number_ref, x_hbm, o_hbm, wq_hbm, wk_hbm, wv_hbm, wo_hbm,
    out_ref, state_ref, xo_ref, wq_ref, wk_ref, wv_ref, wo_ref, sems, *, sizes, which,
):
    place = Place(number_ref[0], sizes)
    mid = xo_ref.shape[2] // 2
    lower, upper = pl.ds(0, mid), pl.ds(mid, mid)
    x_ref, o_ref = xo_ref.at[0], xo_ref.at[1]

    def run(part):
        w_hbm, w_ref = ((wk_hbm, wk_ref), (wq_hbm, wq_ref))[part]
        v, q, k = (wv_hbm, wv_ref), (wq_hbm, wq_ref), (wk_hbm, wk_ref)
        o, w_o = (o_hbm, o_ref), (wo_hbm, wo_ref)
        pairs = [
            (x_hbm.at[:, lower], x_ref.at[:, lower]),
            (w_hbm.at[lower], w_ref.at[lower]),
            (x_hbm.at[:, upper], x_ref.at[:, upper]),
            (w_hbm.at[upper], w_ref.at[upper]),
            *((v, q, o, w_o) if part == 0 else (o, w_o, k, v)),
        ]
        copies = [pltpu.make_async_copy(a, b, sems.at[i]) for i, (a, b) in enumerate(pairs)]
        needed = (2, 4, 5 if part == 0 else 6)
        for c in copies[:4]:
            c.start()

        def arrived(stage):
            for c in copies[needed[stage - 1] if stage else 0 : needed[stage]]:
                c.wait()
            if stage == 0:
                for c in copies[4:]:
                    c.start()

        project_part(
            place, part, xo_ref, wq_ref, wk_ref, wv_ref, wo_ref, out_ref, state_ref, arrived
        )
        for c in copies[needed[2] :]:
            c.wait()

    chosen = which(place)
    pl.when(chosen == 0)(lambda: run(0))
    pl.when(chosen != 0)(lambda: run(1))


def load(place, which, in_rows, grad_rows, w_query, w_key, w_value, w_out):
    number, sizes = place
    rows, width = in_rows.shape
    hd = w_query.shape[1]
    args = [
        pltpu.with_memory_space_constraint(a, pltpu.HBM)
        for a in (in_rows, grad_rows, w_query, w_key, w_value, w_out)
    ]
    out_shape = [
        pltpu.VMEM((2, rows, hd), BF16),
        pltpu.VMEM((hd // HEAD_DIM, HEAD_DIM, HEAD_DIM), F32),
        pltpu.VMEM((2, rows, width), BF16),
        *[pltpu.VMEM((width, hd), BF16)] * 3,
        pltpu.VMEM((hd, width), BF16),
    ]
    return pl.pallas_call(
        functools.partial(load_kernel, sizes=sizes, which=which),
        out_shape=out_shape,
        in_specs=[IN_SMEM] + [ANYWHERE] * 6,
        out_specs=[IN_VMEM] * len(out_shape),
        scratch_shapes=[pltpu.SemaphoreType.DMA((8,))],
        compiler_params=params(16),
        cost_estimate=cost(4 * rows * width * hd, 14 * MIB),
        name="load",
    )(number, *args)


def project_kernel(place, xo_ref, wq_ref, wk_ref, wv_ref, wo_ref, out_ref, *states, which):
    state_ref = states[0] if states else None

    def run(part):
        project_part(
            place, part, xo_ref, wq_ref, wk_ref, wv_ref, wo_ref, out_ref, state_ref, lambda stage: None
        )

    chosen = which(place)
    pl.when(chosen == 0)(lambda: run(0))
    pl.when(chosen != 0)(lambda: run(1))


def project(place, which, xo, weights, w_out, with_state):
    rows, width = xo.shape[1:]
    hd = w_out.shape[0]
    out = [shaped((2, rows, hd), BF16)]
    if with_state:
        out.append(shaped((hd // HEAD_DIM, HEAD_DIM, HEAD_DIM), F32))
    kernel = functools.partial(project_kernel, which=which)
    args = [xo, *weights, w_out]
    return call(kernel, "project", out, args, 4 * rows * width * hd, (), place)


def call(kernel, name, out_shape, args, flops, after=(), place=None):
    n, n_after = len(args), len(after)
    numbers = [] if place is None else [place[0]]

    def body(*refs):
        first = [Place(refs[0][0], place[1])] if numbers else []
        refs = refs[len(numbers) :]
        kernel(*first, *refs[:n], *refs[n + n_after :])

    many = isinstance(out_shape, (list, tuple))
    return pl.pallas_call(
        body,
        out_shape=out_shape,
        in_specs=[IN_SMEM] * len(numbers) + [IN_VMEM] * n + [ANYWHERE] * n_after,
        out_specs=[IN_VMEM] * len(out_shape) if many else IN_VMEM,
        compiler_params=params(16),
        cost_estimate=cost(flops, 2 * MIB),
        name=name,
    )(*numbers, *args, *after)


def attend_kernel(place, *refs, which, part_of, again):
    in_refs, rest = refs[:2], refs[2:]
    if again:
        state_ref, part_ref, scores_ref, out_ref = rest
    else:
        out_ref, scores_ref = rest
    rows, hd = out_ref.shape[1:]
    half = rows // 2
    top, low = slice(0, half), slice(half, rows)

    def causal(h, n, a, b):
        if not again:
            r = lax.broadcasted_iota(jnp.int32, (half, half), 0)
            c = lax.broadcasted_iota(jnp.int32, (half, half), 1)
            diagonal = r >= c
            scores_ref[h, n] = jnp.where(diagonal, dot(a[top], b[top], NT), 0.0).astype(BF16)
            scores_ref[h, n + 1] = dot(a[low], b[top], NT).astype(BF16)
            scores_ref[h, n + 2] = jnp.where(diagonal, dot(a[low], b[low], NT), 0.0).astype(BF16)
        return [scores_ref[h, n + i] for i in range(3)]

    def per_head(body, part):
        k_v, q_g = in_refs[part], in_refs[1 - part]

        def step(h, carry):
            at = pl.ds(pl.multiple_of(h * HEAD_DIM, HEAD_DIM), HEAD_DIM)
            state = state_ref[h].astype(BF16) if again else None

            def put(slot, halves, cross, dims, scale=None):
                added = dot(cross, state, dims) if again else None
                for rows_at, value in zip((top, low), halves):
                    if again:
                        value = value + added[rows_at]
                    if scale is not None:
                        value = value * scale[rows_at]
                    out_ref[slot, rows_at, at] = value.astype(BF16)

            body(h, [ref[i, :, at] for ref in (k_v, q_g) for i in (0, 1)], put)
            return carry

        lax.fori_loop(0, hd // HEAD_DIM, step, 0, unroll=True)

    def forward():
        scale = position_scale(place.seq * rows, rows)

        def body(h, heads, put):
            k, v, q, g = heads
            for slot, a, b, c, dims in ((0, q, k, v, NN), (1, g, v, k, NT)):
                s00, s10, s11 = causal(h, 3 * slot, a, b)
                halves = (dot(s00, c[top], NN), dot(s10, c[top], NN) + dot(s11, c[low], NN))
                put(slot, halves, a, dims, scale if slot == 0 else None)

        per_head(body, part_of(0))

    def backward():
        def body(h, heads, put):
            k, v, q, g = heads
            for slot, a, b, c, dims in ((2, q, k, g, NN), (3, g, v, q, NT)):
                s00, s10, s11 = causal(h, 3 * slot - 6, a, b)
                halves = (dot(s00, c[top], TN) + dot(s10, c[low], TN), dot(s11, c[low], TN))
                put(slot, halves, b, dims)

        per_head(body, part_of(1))

    chosen = which(place)
    if again:
        for t in (0, 1):
            out_ref[2 - 2 * chosen + t] = part_ref[2 - 2 * chosen + t]
    pl.when(chosen == 0)(forward)
    pl.when(chosen != 0)(backward)


def attend(place, which, part_of, projected, more=(), after=()):
    rows, hd = projected[0].shape[1:]
    out = shaped((4, rows, hd), BF16)
    scores = shaped((hd // HEAD_DIM, 6, rows // 2, rows // 2), BF16)
    kernel = functools.partial(attend_kernel, which=which, part_of=part_of, again=bool(more))
    outs = out if more else [out, scores]
    return call(kernel, "attend", outs, [*projected, *more], 128 * rows * rows * hd, after, place)


def head_terms_kernel(place, d_ref, wq_ref, wk_ref, wv_ref, out_ref, *, shard):
    width = out_ref.shape[1]
    step = min(width, 256)
    start = shard(place) * width
    for i in range(width // step):
        rows = pl.ds(pl.multiple_of(start + i * step, step), step)
        out_ref[:, pl.ds(i * step, step)] = (
            dot(d_ref[1], wq_ref[rows, :], NT)
            + dot(d_ref[3], wk_ref[rows, :], NT)
            + dot(d_ref[2], wv_ref[rows, :], NT)
        )


def head_terms(place, results, weights, shard, shards, after=()):
    width, hd = weights[0].shape
    rows = results.shape[1]
    return call(
        functools.partial(head_terms_kernel, shard=shard),
        "head_terms",
        shaped((rows, width // shards), F32),
        [results, *weights],
        6 * rows * width // shards * hd,
        after,
        place,
    )


def add_kernel(*refs):
    total = refs[0][...]
    for ref in refs[1:-1]:
        total = total + ref[...]
    refs[-1][...] = total.astype(refs[-1].dtype)


def add(arrays, dtype, after=()):
    return call(add_kernel, "add", shaped(arrays[0].shape, dtype), list(arrays), 0, after)


def column_block(place, i):
    return (place.seq ^ (i // 2 % 2)) * 4 + (place.dp ^ (i % 2 * 2 + i // 4))


def fill_tiles(place, xo_ref, d_ref, pair, side, blocks, scale, added, outs):
    half = d_ref.shape[2] // 2
    block = outs[0].shape[1]
    features = pl.ds(pl.multiple_of(side * half, half), half)
    for i, b in enumerate(blocks):
        columns = pl.ds(pl.multiple_of(column_block(place, b) * block, block), block)
        for t, rows in enumerate((1 - pair, 0)):
            tile = dot(xo_ref[rows, :, columns], d_ref[2 * pair + t, :, features], TN) * scale
            for read in added:
                tile = tile + read(i, t)
            outs[i][t] = tile


def other_core_kernel(place, xo_ref, d_ref, out_ref, *, early, slot, scale):
    outs = [out_ref.at[i] for i in range(4)]
    pair, side = place.seq ^ early, 1 - place.core ^ slot
    fill_tiles(place, xo_ref, d_ref, pair, side, (4, 5, 6, 7), scale, (), outs)


def other_core_both_kernel(place, xo_ref, d_ref, *out_refs, early, scale):
    pair = place.seq ^ early
    half = d_ref.shape[2] // 2
    block = out_refs[0].shape[2]
    sides = (1 - place.core, place.core)
    for t, rows in enumerate((1 - pair, 0)):
        features = [pl.ds(pl.multiple_of(side * half, half), half) for side in sides]
        d = jnp.concatenate([d_ref[2 * pair + t, :, at] for at in features], axis=1)
        for i in range(4):
            columns = pl.ds(pl.multiple_of(column_block(place, 4 + i) * block, block), block)
            tile = dot(xo_ref[rows, :, columns], d, TN) * scale
            out_refs[0][i, t] = tile[:, :half]
            out_refs[1][i, t] = tile[:, half:]


def first_hop_kernel(place, xo_ref, d_ref, far_ref, out_ref, *, early, slot, scale):
    pair, side = place.seq ^ early, place.core ^ slot
    blocks = (2 - side, 3)
    outs = [out_ref.at[i] for i in range(2)]
    added = (lambda i, t: far_ref[blocks[i], t],)
    fill_tiles(place, xo_ref, d_ref, pair, side, blocks, scale, added, outs)


def second_hop_kernel(
    place, xo_ref, d_ref, far0_ref, far1_ref, over0_ref, over1_ref, keep_ref, send_ref,
    *, slot, scale,
):
    over = (over0_ref, over1_ref)
    side = place.core ^ slot
    blocks = (0, 1 + side)

    def far(p, i, t):
        return (far0_ref, far1_ref)[p][blocks[i], t]

    for p in (0, 1):
        added = (
            lambda i, t: jnp.where(side == 0, far(1 - p, i, t), far(p, i, t)),
            lambda i, t: over[p][i, t],
        )
        pair = place.seq ^ p ^ 1 - side
        outs = (keep_ref.at[p], send_ref.at[p])
        fill_tiles(place, xo_ref, d_ref, pair, side, blocks, scale, added, outs)


def put_side(place, slot, kept_ref, moved_ref, part_ref, out_refs, sems):
    side = place.core ^ slot
    half = part_ref.shape[1]
    at = pl.ds(pl.multiple_of(side * half, half), half)
    copies = []
    for i, (pair, t) in enumerate(((0, 1), (1, 1), (1, 0), (0, 0))):
        p = place.seq ^ pair
        total = kept_ref[p ^ 1 - side, t] + moved_ref[1 - p, t]
        part_ref[i] = total if i < 3 else total.T
        out = out_refs[i].at[:, at] if i < 3 else out_refs[i].at[at]
        copies.append(pltpu.make_async_copy(part_ref.at[i], out, sems.at[i]))
        copies[-1].start()
    return copies


def settle_kernel(number_ref, kept_ref, moved_ref, after_ref, *rest, sizes):
    out_refs, (part_ref, sems) = rest[:4], rest[4:]
    place = Place(number_ref[0], sizes)
    for c in put_side(place, 0, kept_ref, moved_ref, part_ref, out_refs, sems):
        c.wait()


def finish_kernel(number_ref, *refs, sizes):
    line, (kept_ref, moved_ref) = refs[:3], refs[3:5]
    input_out, out_refs, (part_ref, input_ref, sems) = refs[9], refs[10:14], refs[14:]
    place = Place(number_ref[0], sizes)
    input_ref[...] = (line[0][...] + line[1][...] + line[2][...]).astype(BF16)
    last = pltpu.make_async_copy(input_ref, input_out, sems.at[4])
    last.start()
    for c in put_side(place, 1, kept_ref, moved_ref, part_ref, out_refs, sems):
        c.wait()
    last.wait()


def finish(place, line, kept, moved):
    number, sizes = place
    block, half = kept[0].shape[2:]
    tall, wide = pltpu.HBM((block, 2 * half), F32), pltpu.HBM((2 * half, block), F32)
    grads = [tall, tall, tall, wide]
    parts = pltpu.VMEM((4, block, half), F32)
    sides = pl.pallas_call(
        functools.partial(settle_kernel, sizes=sizes),
        out_shape=grads,
        in_specs=[IN_SMEM, IN_VMEM, IN_VMEM, ANYWHERE],
        out_specs=[ANYWHERE] * 4,
        scratch_shapes=[parts, pltpu.SemaphoreType.DMA((4,))],
        compiler_params=params(16),
        cost_estimate=cost(0, 2 * MIB),
        name="settle",
    )(number, kept[0], moved[0], kept[1])
    return pl.pallas_call(
        functools.partial(finish_kernel, sizes=sizes),
        out_shape=[pltpu.HBM(line[0].shape, BF16), *grads],
        in_specs=[IN_SMEM] + [IN_VMEM] * 5 + [ANYWHERE] * 4,
        out_specs=[ANYWHERE] * 5,
        input_output_aliases={6 + i: 1 + i for i in range(4)},
        scratch_shapes=[parts, pltpu.VMEM(line[0].shape, BF16), pltpu.SemaphoreType.DMA((5,))],
        compiler_params=params(16),
        cost_estimate=cost(0, 2 * MIB),
        name="finish",
    )(number, *line, kept[1], moved[1], *sides)


def states_before(x, axis, reverse):
    peers, here = (lax.axis_size(axis), lax.axis_index(axis))
    everything = lax.all_gather(x, axis)
    at = jnp.arange(peers)
    reached = at > here if reverse else at < here
    return jnp.sum(jnp.where(reached[:, None, None, None], everything, 0.0), axis=0)


def swap(x, axis, bit):
    return lax.ppermute(x, axis, [(i, i ^ bit) for i in range(lax.axis_size(axis))])


def local(layer_input, w_query, w_key, w_value, w_out, out_grad):
    num_rows = layer_input.shape[1]
    n_seq, n_head, n_dp = (lax.axis_size(a) for a in ("seq", "head", "dp"))
    scale = float(n_seq * n_dp * num_rows) ** -0.5

    sizes = (n_seq, n_head, n_dp)
    number = (lax.axis_index("seq") * n_head + lax.axis_index("head")) * n_dp + lax.axis_index("dp")
    number = number.astype(jnp.int32).reshape(1)
    place = (number, sizes)
    arrays = (layer_input[0], out_grad[0], w_query, w_key, w_value, w_out)
    planned = sizes == PLANNED
    part = (lambda at: at.seq) if planned else (lambda at: 0)
    projected, state, xo, *weights, wo = load(place, part, *arrays)
    if planned:
        state = swap(state, "seq", 1)
    other, *more = project(place, lambda at: 1 - part(at), xo, weights, wo, not planned)
    projected = (projected, other)

    if not planned:
        prefix = states_before(state, "seq", False)
        suffix = states_before(more[0], "seq", True)
        d, scores = attend(place, lambda at: 0, lambda which: 0, projected)
        d = attend(place, lambda at: 0, lambda which: 0, projected, (prefix, d, scores))
        d = attend(place, lambda at: 1, lambda which: 0, projected, (suffix, d, scores))
        terms = head_terms(place, d, weights, lambda at: 0, 1)

        def reduced(rows, d):
            return lax.psum_scatter(
                dot(rows, d, TN) * scale, ("seq", "dp"), scatter_dimension=0, tiled=True
            )

        return (
            lax.psum_scatter(terms, "head", scatter_dimension=1, tiled=True).astype(BF16)[None],
            reduced(xo[0], d[1]),
            reduced(xo[0], d[3]),
            reduced(xo[0], d[2]),
            reduced(xo[1], d[0]).T,
        )

    def term(flip, after):
        return head_terms(place, d, weights, lambda at: at.head ^ flip, n_head, after)

    def hop(array, slot, second):
        pairs = []
        for i in range(8):
            side = i % 2 ^ slot
            pairs.append((i, i ^ (4 if side == second else 2)))
        return lax.ppermute(array, ("seq", "dp"), pairs)

    block, half = xo.shape[2] // 8, projected[0].shape[2] // 2
    tile = (2, block, half)
    flops = 4 * num_rows * block * half

    def to_core(d, early, slot, after):
        kernel = functools.partial(other_core_kernel, early=early, slot=slot, scale=scale)
        out = shaped((4, *tile), F32)
        array = call(kernel, "other_core", out, [xo, d], 4 * flops, after, place)
        return array, swap(array, "dp", 1)

    def both_to_core(d, early, after):
        kernel = functools.partial(other_core_both_kernel, early=early, scale=scale)
        outs = [shaped((4, *tile), F32)] * 2
        arrays = call(kernel, "other_core_both", outs, [xo, d], 8 * flops, after, place)
        return arrays[0], [swap(array, "dp", 1) for array in arrays]

    def first_hop(early, slot, after):
        kernel = functools.partial(first_hop_kernel, early=early, slot=slot, scale=scale)
        out = shaped((2, *tile), F32)
        args = [xo, d, far[early][slot]]
        array = call(kernel, "first_hop", out, args, 2 * flops, after, place)
        return array, hop(array, slot, 0)

    def second_hop(slot, over, after):
        kernel = functools.partial(second_hop_kernel, slot=slot, scale=scale)
        outs = [shaped((2, *tile), F32)] * 2
        args = [xo, d, far[0][slot], far[1][slot], *over]
        keep, leave = call(kernel, "second_hop", outs, args, 4 * flops, after, place)
        return keep, hop(leave, slot, 1)

    early, scores = attend(place, lambda at: at.seq, lambda which: which, projected)
    far = ([None, None], [None, None])
    at, far[0][0] = to_core(early, 0, 0, [])
    at, far[0][1] = to_core(early, 0, 1, [at])
    d = attend(place, lambda at: 1 - at.seq, lambda which: 1 - which, projected, (state, early, scores), [at])
    at, far[1][:] = both_to_core(d, 1, [])
    at, over1 = first_hop(0, 0, [at])
    t3 = term(3, [at])
    t3_in = swap(t3, "head", 1)
    at, over2 = first_hop(0, 1, [t3])
    at, over3 = first_hop(1, 0, [at])
    at, over4 = first_hop(1, 1, [at])
    t2 = term(2, [at])
    t0 = term(0, [t2])
    t1 = term(1, [t0, over1])
    t1_in = swap(t1, "head", 1)
    t2 = add([t2, t3_in], F32, [t1])
    t2_in = swap(t2, "head", 2)
    keep0, moved0 = second_hop(0, (over1, over3), [t2, over2])
    keep1, moved1 = second_hop(1, (over2, over4), [keep0])
    outs = finish(place, (t0, t1_in, t2_in), (keep0, keep1), (moved0, moved1))
    input_grad, grad_query, grad_key, grad_value, grad_out = outs
    return (input_grad[None], grad_query, grad_key, grad_value, grad_out)


def solution(mesh):
    return jax.shard_map(
        local,
        mesh=mesh,
        in_specs=(
            P("dp", "seq", None),
            P(None, "head"),
            P(None, "head"),
            P(None, "head"),
            P("head", None),
            P("dp", "seq", None),
        ),
        out_specs=(
            P("dp", "seq", "head"),
            P(("seq", "dp"), "head"),
            P(("seq", "dp"), "head"),
            P(("seq", "dp"), "head"),
            P("head", ("seq", "dp")),
        ),
        check_vma=False,
    )
```

```python
import functools

import jax
import jax.numpy as jnp
from jax import lax
from jax.experimental import pallas as pl
from jax.experimental.pallas import tpu as pltpu
from jax.sharding import PartitionSpec as P

HEAD_DIM = 128
BF16 = jnp.bfloat16
F32 = jnp.float32
MIB = 1024 * 1024
PLANNED = (2, 4, 4)
NN = ((1,), (0,))
NT = ((1,), (1,))
TN = ((0,), (0,))
ANYWHERE = pl.BlockSpec(memory_space=pl.ANY)
IN_VMEM = pl.BlockSpec(memory_space=pltpu.VMEM)
IN_SMEM = pl.BlockSpec(memory_space=pltpu.SMEM)


def dot(a, b, dims):
    return lax.dot_general(a, b, (dims, ((), ())), preferred_element_type=F32)


def shaped(shape, dtype):
    return jax.ShapeDtypeStruct(shape, dtype)


def params(mib):
    return pltpu.CompilerParams(vmem_limit_bytes=mib * MIB)


def cost(flops, size):
    return pl.CostEstimate(flops=flops, bytes_accessed=size, transcendentals=0)


class Place:
    def __init__(self, number, sizes):
        _, n_head, n_dp = sizes
        self.dp = lax.rem(number, n_dp)
        self.head = lax.rem(lax.div(number, n_dp), n_head)
        self.seq = lax.div(number, n_head * n_dp)
        self.core = lax.rem(self.dp, 2)


def position_scale(start, rows):
    positions = (start + lax.broadcasted_iota(jnp.int32, (rows, 1), 0)).astype(F32)
    return 1.0 / jnp.sqrt(HEAD_DIM * (positions + 1.0))


def project_part(place, part, xo_ref, wq_ref, wk_ref, wv_ref, wo_ref, out_ref, state_ref, arrived):
    rows, width = xo_ref.shape[1:]
    x_ref, o_ref = xo_ref.at[0], xo_ref.at[1]
    lower, upper = pl.ds(0, width // 2), pl.ds(width // 2, width // 2)

    def first(w_ref):
        arrived(0)
        product = dot(x_ref[:, lower], w_ref[lower, :], NN)
        arrived(1)
        out_ref[0] = (product + dot(x_ref[:, upper], w_ref[upper, :], NN)).astype(BF16)
        arrived(2)

    def state():
        if state_ref is not None:
            for h in range(state_ref.shape[0]):
                at = pl.ds(h * HEAD_DIM, HEAD_DIM)
                state_ref[h] = dot(out_ref[0, :, at], out_ref[1, :, at], TN)

    if part == 0:
        first(wk_ref)
        out_ref[1] = dot(x_ref[...], wv_ref[...], NN).astype(BF16)
    else:
        first(wq_ref)
        scale = position_scale(place.seq * rows, rows)
        out_ref[1] = (dot(o_ref[...], wo_ref[...], NT) * scale).astype(BF16)
    state()


def load_kernel(
    number_ref, x_hbm, o_hbm, wq_hbm, wk_hbm, wv_hbm, wo_hbm,
    out_ref, state_ref, xo_ref, wq_ref, wk_ref, wv_ref, wo_ref, sems, *, sizes, which,
):
    place = Place(number_ref[0], sizes)
    mid = xo_ref.shape[2] // 2
    lower, upper = pl.ds(0, mid), pl.ds(mid, mid)
    x_ref, o_ref = xo_ref.at[0], xo_ref.at[1]

    def run(part):
        w_hbm, w_ref = ((wk_hbm, wk_ref), (wq_hbm, wq_ref))[part]
        v, q, k = (wv_hbm, wv_ref), (wq_hbm, wq_ref), (wk_hbm, wk_ref)
        o, w_o = (o_hbm, o_ref), (wo_hbm, wo_ref)
        pairs = [
            (x_hbm.at[:, lower], x_ref.at[:, lower]),
            (w_hbm.at[lower], w_ref.at[lower]),
            (x_hbm.at[:, upper], x_ref.at[:, upper]),
            (w_hbm.at[upper], w_ref.at[upper]),
            *((v, q, o, w_o) if part == 0 else (o, w_o, k, v)),
        ]
        copies = [pltpu.make_async_copy(a, b, sems.at[i]) for i, (a, b) in enumerate(pairs)]
        needed = (2, 4, 5 if part == 0 else 6)
        for c in copies[:4]:
            c.start()

        def arrived(stage):
            for c in copies[needed[stage - 1] if stage else 0 : needed[stage]]:
                c.wait()
            if stage == 0:
                for c in copies[4:]:
                    c.start()

        project_part(
            place, part, xo_ref, wq_ref, wk_ref, wv_ref, wo_ref, out_ref, state_ref, arrived
        )
        for c in copies[needed[2] :]:
            c.wait()

    chosen = which(place)
    pl.when(chosen == 0)(lambda: run(0))
    pl.when(chosen != 0)(lambda: run(1))


def load(place, which, in_rows, grad_rows, w_query, w_key, w_value, w_out):
    number, sizes = place
    rows, width = in_rows.shape
    hd = w_query.shape[1]
    args = [
        pltpu.with_memory_space_constraint(a, pltpu.HBM)
        for a in (in_rows, grad_rows, w_query, w_key, w_value, w_out)
    ]
    out_shape = [
        pltpu.VMEM((2, rows, hd), BF16),
        pltpu.VMEM((hd // HEAD_DIM, HEAD_DIM, HEAD_DIM), F32),
        pltpu.VMEM((2, rows, width), BF16),
        *[pltpu.VMEM((width, hd), BF16)] * 3,
        pltpu.VMEM((hd, width), BF16),
    ]
    return pl.pallas_call(
        functools.partial(load_kernel, sizes=sizes, which=which),
        out_shape=out_shape,
        in_specs=[IN_SMEM] + [ANYWHERE] * 6,
        out_specs=[IN_VMEM] * len(out_shape),
        scratch_shapes=[pltpu.SemaphoreType.DMA((8,))],
        compiler_params=params(16),
        cost_estimate=cost(4 * rows * width * hd, 14 * MIB),
        name="load",
    )(number, *args)


def project_kernel(place, xo_ref, wq_ref, wk_ref, wv_ref, wo_ref, out_ref, *states, which):
    state_ref = states[0] if states else None

    def run(part):
        project_part(
            place, part, xo_ref, wq_ref, wk_ref, wv_ref, wo_ref, out_ref, state_ref, lambda stage: None
        )

    chosen = which(place)
    pl.when(chosen == 0)(lambda: run(0))
    pl.when(chosen != 0)(lambda: run(1))


def project(place, which, xo, weights, w_out, with_state):
    rows, width = xo.shape[1:]
    hd = w_out.shape[0]
    out = [shaped((2, rows, hd), BF16)]
    if with_state:
        out.append(shaped((hd // HEAD_DIM, HEAD_DIM, HEAD_DIM), F32))
    kernel = functools.partial(project_kernel, which=which)
    args = [xo, *weights, w_out]
    return call(kernel, "project", out, args, 4 * rows * width * hd, (), place)


def call(kernel, name, out_shape, args, flops, after=(), place=None):
    n, n_after = len(args), len(after)
    numbers = [] if place is None else [place[0]]

    def body(*refs):
        first = [Place(refs[0][0], place[1])] if numbers else []
        refs = refs[len(numbers) :]
        kernel(*first, *refs[:n], *refs[n + n_after :])

    many = isinstance(out_shape, (list, tuple))
    return pl.pallas_call(
        body,
        out_shape=out_shape,
        in_specs=[IN_SMEM] * len(numbers) + [IN_VMEM] * n + [ANYWHERE] * n_after,
        out_specs=[IN_VMEM] * len(out_shape) if many else IN_VMEM,
        compiler_params=params(16),
        cost_estimate=cost(flops, 2 * MIB),
        name=name,
    )(*numbers, *args, *after)


def attend_kernel(place, *refs, which, part_of, again):
    in_refs, rest = refs[:2], refs[2:]
    if again:
        state_ref, scores_ref, out_ref = rest
    else:
        out_ref, scores_ref = rest
    rows, hd = out_ref.shape[1:]
    half = rows // 2
    top, low = slice(0, half), slice(half, rows)

    def causal(h, n, a, b):
        if not again:
            r = lax.broadcasted_iota(jnp.int32, (half, half), 0)
            c = lax.broadcasted_iota(jnp.int32, (half, half), 1)
            diagonal = r >= c
            scores_ref[h, n] = jnp.where(diagonal, dot(a[top], b[top], NT), 0.0).astype(BF16)
            scores_ref[h, n + 1] = dot(a[low], b[top], NT).astype(BF16)
            scores_ref[h, n + 2] = jnp.where(diagonal, dot(a[low], b[low], NT), 0.0).astype(BF16)
        return [scores_ref[h, n + i] for i in range(3)]

    def per_head(body, part):
        k_v, q_g = in_refs[part], in_refs[1 - part]

        def step(h, carry):
            at = pl.ds(pl.multiple_of(h * HEAD_DIM, HEAD_DIM), HEAD_DIM)
            state = state_ref[h].astype(BF16) if again else None

            def put(slot, halves, cross, dims, scale=None):
                added = dot(cross, state, dims) if again else None
                for rows_at, value in zip((top, low), halves):
                    if again:
                        value = value + added[rows_at]
                    if scale is not None:
                        value = value * scale[rows_at]
                    out_ref[slot, rows_at, at] = value.astype(BF16)

            body(h, [ref[i, :, at] for ref in (k_v, q_g) for i in (0, 1)], put)
            return carry

        lax.fori_loop(0, hd // HEAD_DIM, step, 0, unroll=True)

    def forward():
        scale = position_scale(place.seq * rows, rows)

        def body(h, heads, put):
            k, v, q, g = heads
            for slot, a, b, c, dims in ((0, q, k, v, NN), (1, g, v, k, NT)):
                s00, s10, s11 = causal(h, 3 * slot, a, b)
                halves = (dot(s00, c[top], NN), dot(s10, c[top], NN) + dot(s11, c[low], NN))
                put(slot, halves, a, dims, scale if slot == 0 else None)

        per_head(body, part_of(0))

    def backward():
        def body(h, heads, put):
            k, v, q, g = heads
            for slot, a, b, c, dims in ((0, q, k, g, NN), (1, g, v, q, NT)):
                s00, s10, s11 = causal(h, 3 * slot, a, b)
                halves = (dot(s00, c[top], TN) + dot(s10, c[low], TN), dot(s11, c[low], TN))
                put(slot, halves, b, dims)

        per_head(body, part_of(1))

    chosen = which(place)
    pl.when(chosen == 0)(forward)
    pl.when(chosen != 0)(backward)


def attend(place, which, part_of, projected, more=(), after=()):
    rows, hd = projected[0].shape[1:]
    out = shaped((2, rows, hd), BF16)
    scores = shaped((hd // HEAD_DIM, 6, rows // 2, rows // 2), BF16)
    kernel = functools.partial(attend_kernel, which=which, part_of=part_of, again=bool(more))
    outs = out if more else [out, scores]
    return call(kernel, "attend", outs, [*projected, *more], 128 * rows * rows * hd, after, place)


def head_terms_kernel(place, d0_ref, d1_ref, wq_ref, wk_ref, wv_ref, out_ref, *, which, shard):
    width = out_ref.shape[1]
    step = min(width, 256)
    start = shard(place) * width

    def fill(forward_ref, backward_ref):
        for i in range(width // step):
            rows = pl.ds(pl.multiple_of(start + i * step, step), step)
            out_ref[:, pl.ds(i * step, step)] = (
                dot(forward_ref[1], wq_ref[rows, :], NT)
                + dot(backward_ref[1], wk_ref[rows, :], NT)
                + dot(backward_ref[0], wv_ref[rows, :], NT)
            )

    chosen = which(place)
    pl.when(chosen == 0)(lambda: fill(d0_ref, d1_ref))
    pl.when(chosen != 0)(lambda: fill(d1_ref, d0_ref))


def head_terms(place, which, first, second, weights, shard, shards, after=()):
    width, hd = weights[0].shape
    rows = first.shape[1]
    return call(
        functools.partial(head_terms_kernel, which=which, shard=shard),
        "head_terms",
        shaped((rows, width // shards), F32),
        [first, second, *weights],
        6 * rows * width // shards * hd,
        after,
        place,
    )


def add_kernel(*refs):
    total = refs[0][...]
    for ref in refs[1:-1]:
        total = total + ref[...]
    refs[-1][...] = total.astype(refs[-1].dtype)


def add(arrays, dtype, after=()):
    return call(add_kernel, "add", shaped(arrays[0].shape, dtype), list(arrays), 0, after)


def column_block(place, i):
    return (place.seq ^ (i // 2 % 2)) * 4 + (place.dp ^ (i % 2 * 2 + i // 4))


def fill_tiles(place, xo_ref, read, half, pair, side, blocks, scale, added, outs):
    block = outs[0].shape[1]
    features = pl.ds(pl.multiple_of(side * half, half), half)
    for i, b in enumerate(blocks):
        columns = pl.ds(pl.multiple_of(column_block(place, b) * block, block), block)
        for t, rows in enumerate((1 - pair, 0)):
            tile = dot(xo_ref[rows, :, columns], read(t, features), TN) * scale
            for more in added:
                tile = tile + more(i, t)
            outs[i][t] = tile


def reader(d_ref):
    return (lambda t, features: d_ref[t, :, features]), d_ref.shape[2] // 2


def other_core_kernel(place, xo_ref, d_ref, out_ref, *, early, slot, scale):
    outs = [out_ref.at[i] for i in range(4)]
    pair, side = place.seq ^ early, 1 - place.core ^ slot
    fill_tiles(place, xo_ref, *reader(d_ref), pair, side, (4, 5, 6, 7), scale, (), outs)


def other_core_both_kernel(place, xo_ref, d_ref, *out_refs, early, scale):
    pair = place.seq ^ early
    half = d_ref.shape[2] // 2
    block = out_refs[0].shape[2]
    sides = (1 - place.core, place.core)
    for t, rows in enumerate((1 - pair, 0)):
        features = [pl.ds(pl.multiple_of(side * half, half), half) for side in sides]
        d = jnp.concatenate([d_ref[t, :, at] for at in features], axis=1)
        for i in range(4):
            columns = pl.ds(pl.multiple_of(column_block(place, 4 + i) * block, block), block)
            tile = dot(xo_ref[rows, :, columns], d, TN) * scale
            out_refs[0][i, t] = tile[:, :half]
            out_refs[1][i, t] = tile[:, half:]


def first_hop_kernel(place, xo_ref, d_ref, far_ref, out_ref, *, early, slot, scale):
    pair, side = place.seq ^ early, place.core ^ slot
    blocks = (2 - side, 3)
    outs = [out_ref.at[i] for i in range(2)]
    added = (lambda i, t: far_ref[blocks[i], t],)
    fill_tiles(place, xo_ref, *reader(d_ref), pair, side, blocks, scale, added, outs)


def second_hop_kernel(
    place, xo_ref, d0_ref, d1_ref, far0_ref, far1_ref, over0_ref, over1_ref, keep_ref, send_ref,
    *, slot, scale,
):
    over = (over0_ref, over1_ref)
    side = place.core ^ slot
    blocks = (0, 1 + side)

    def far(p, i, t):
        return (far0_ref, far1_ref)[p][blocks[i], t]

    for p in (0, 1):
        added = (
            lambda i, t: jnp.where(side == 0, far(1 - p, i, t), far(p, i, t)),
            lambda i, t: over[p][i, t],
        )
        late = p ^ 1 - side

        def read(t, features):
            return jnp.where(late == 0, d0_ref[t, :, features], d1_ref[t, :, features])

        pair = place.seq ^ p ^ 1 - side
        outs = (keep_ref.at[p], send_ref.at[p])
        fill_tiles(place, xo_ref, read, d0_ref.shape[2] // 2, pair, side, blocks, scale, added, outs)


def put_side(place, slot, kept_ref, moved_ref, part_ref, out_refs, sems):
    side = place.core ^ slot
    half = part_ref.shape[1]
    at = pl.ds(pl.multiple_of(side * half, half), half)
    copies = []
    for i, (pair, t) in enumerate(((0, 1), (1, 1), (1, 0), (0, 0))):
        p = place.seq ^ pair
        total = kept_ref[p ^ 1 - side, t] + moved_ref[1 - p, t]
        part_ref[i] = total if i < 3 else total.T
        out = out_refs[i].at[:, at] if i < 3 else out_refs[i].at[at]
        copies.append(pltpu.make_async_copy(part_ref.at[i], out, sems.at[i]))
        copies[-1].start()
    return copies


def settle_kernel(number_ref, kept_ref, moved_ref, after_ref, *rest, sizes):
    out_refs, (part_ref, sems) = rest[:4], rest[4:]
    place = Place(number_ref[0], sizes)
    for c in put_side(place, 0, kept_ref, moved_ref, part_ref, out_refs, sems):
        c.wait()


def finish_kernel(number_ref, *refs, sizes):
    line, (kept_ref, moved_ref) = refs[:3], refs[3:5]
    input_out, out_refs, (part_ref, input_ref, sems) = refs[9], refs[10:14], refs[14:]
    place = Place(number_ref[0], sizes)
    input_ref[...] = (line[0][...] + line[1][...] + line[2][...]).astype(BF16)
    last = pltpu.make_async_copy(input_ref, input_out, sems.at[4])
    last.start()
    for c in put_side(place, 1, kept_ref, moved_ref, part_ref, out_refs, sems):
        c.wait()
    last.wait()


def finish(place, line, kept, moved):
    number, sizes = place
    block, half = kept[0].shape[2:]
    tall, wide = pltpu.HBM((block, 2 * half), F32), pltpu.HBM((2 * half, block), F32)
    grads = [tall, tall, tall, wide]
    parts = pltpu.VMEM((4, block, half), F32)
    sides = pl.pallas_call(
        functools.partial(settle_kernel, sizes=sizes),
        out_shape=grads,
        in_specs=[IN_SMEM, IN_VMEM, IN_VMEM, ANYWHERE],
        out_specs=[ANYWHERE] * 4,
        scratch_shapes=[parts, pltpu.SemaphoreType.DMA((4,))],
        compiler_params=params(16),
        cost_estimate=cost(0, 2 * MIB),
        name="settle",
    )(number, kept[0], moved[0], kept[1])
    return pl.pallas_call(
        functools.partial(finish_kernel, sizes=sizes),
        out_shape=[pltpu.HBM(line[0].shape, BF16), *grads],
        in_specs=[IN_SMEM] + [IN_VMEM] * 5 + [ANYWHERE] * 4,
        out_specs=[ANYWHERE] * 5,
        input_output_aliases={6 + i: 1 + i for i in range(4)},
        scratch_shapes=[parts, pltpu.VMEM(line[0].shape, BF16), pltpu.SemaphoreType.DMA((5,))],
        compiler_params=params(16),
        cost_estimate=cost(0, 2 * MIB),
        name="finish",
    )(number, *line, kept[1], moved[1], *sides)


def states_before(x, axis, reverse):
    peers, here = (lax.axis_size(axis), lax.axis_index(axis))
    everything = lax.all_gather(x, axis)
    at = jnp.arange(peers)
    reached = at > here if reverse else at < here
    return jnp.sum(jnp.where(reached[:, None, None, None], everything, 0.0), axis=0)


def swap(x, axis, bit):
    return lax.ppermute(x, axis, [(i, i ^ bit) for i in range(lax.axis_size(axis))])


def local(layer_input, w_query, w_key, w_value, w_out, out_grad):
    num_rows = layer_input.shape[1]
    n_seq, n_head, n_dp = (lax.axis_size(a) for a in ("seq", "head", "dp"))
    scale = float(n_seq * n_dp * num_rows) ** -0.5

    sizes = (n_seq, n_head, n_dp)
    number = (lax.axis_index("seq") * n_head + lax.axis_index("head")) * n_dp + lax.axis_index("dp")
    number = number.astype(jnp.int32).reshape(1)
    place = (number, sizes)
    arrays = (layer_input[0], out_grad[0], w_query, w_key, w_value, w_out)
    planned = sizes == PLANNED
    part = (lambda at: at.seq) if planned else (lambda at: 0)
    projected, state, xo, *weights, wo = load(place, part, *arrays)
    if planned:
        state = swap(state, "seq", 1)
    other, *more = project(place, lambda at: 1 - part(at), xo, weights, wo, not planned)
    projected = (projected, other)

    if not planned:
        prefix = states_before(state, "seq", False)
        suffix = states_before(more[0], "seq", True)
        _, scores = attend(place, lambda at: 0, lambda which: 0, projected)
        first = attend(place, lambda at: 0, lambda which: 0, projected, (prefix, scores))
        second = attend(place, lambda at: 1, lambda which: 0, projected, (suffix, scores))
        terms = head_terms(place, lambda at: 0, first, second, weights, lambda at: 0, 1)

        def reduced(rows, d):
            return lax.psum_scatter(
                dot(rows, d, TN) * scale, ("seq", "dp"), scatter_dimension=0, tiled=True
            )

        return (
            lax.psum_scatter(terms, "head", scatter_dimension=1, tiled=True).astype(BF16)[None],
            reduced(xo[0], first[1]),
            reduced(xo[0], second[1]),
            reduced(xo[0], second[0]),
            reduced(xo[1], first[0]).T,
        )

    def term(flip, after):
        return head_terms(
            place, lambda at: at.seq, early, late, weights, lambda at: at.head ^ flip, n_head, after
        )

    def hop(array, slot, second):
        pairs = []
        for i in range(8):
            side = i % 2 ^ slot
            pairs.append((i, i ^ (4 if side == second else 2)))
        return lax.ppermute(array, ("seq", "dp"), pairs)

    block, half = xo.shape[2] // 8, projected[0].shape[2] // 2
    tile = (2, block, half)
    flops = 4 * num_rows * block * half

    def to_core(d, early, slot, after):
        kernel = functools.partial(other_core_kernel, early=early, slot=slot, scale=scale)
        out = shaped((4, *tile), F32)
        array = call(kernel, "other_core", out, [xo, d], 4 * flops, after, place)
        return array, swap(array, "dp", 1)

    def both_to_core(d, early, after):
        kernel = functools.partial(other_core_both_kernel, early=early, scale=scale)
        outs = [shaped((4, *tile), F32)] * 2
        arrays = call(kernel, "other_core_both", outs, [xo, d], 8 * flops, after, place)
        return arrays[0], [swap(array, "dp", 1) for array in arrays]

    def first_hop(early, slot, after):
        kernel = functools.partial(first_hop_kernel, early=early, slot=slot, scale=scale)
        out = shaped((2, *tile), F32)
        args = [xo, results[early], far[early][slot]]
        array = call(kernel, "first_hop", out, args, 2 * flops, after, place)
        return array, hop(array, slot, 0)

    def second_hop(slot, over, after):
        kernel = functools.partial(second_hop_kernel, slot=slot, scale=scale)
        outs = [shaped((2, *tile), F32)] * 2
        args = [xo, *results, far[0][slot], far[1][slot], *over]
        keep, leave = call(kernel, "second_hop", outs, args, 4 * flops, after, place)
        return keep, hop(leave, slot, 1)

    early, scores = attend(place, lambda at: at.seq, lambda which: which, projected)
    far = ([None, None], [None, None])
    at, far[0][0] = to_core(early, 0, 0, [])
    at, far[0][1] = to_core(early, 0, 1, [at])
    late = attend(
        place, lambda at: 1 - at.seq, lambda which: 1 - which, projected, (state, scores), [at]
    )
    results = (early, late)
    at, far[1][:] = both_to_core(late, 1, [])
    at, over1 = first_hop(0, 0, [at])
    t3 = term(3, [at])
    t3_in = swap(t3, "head", 1)
    at, over2 = first_hop(0, 1, [t3])
    at, over3 = first_hop(1, 0, [at])
    at, over4 = first_hop(1, 1, [at])
    t2 = term(2, [at])
    t0 = term(0, [t2])
    t1 = term(1, [t0, over1])
    t1_in = swap(t1, "head", 1)
    t2 = add([t2, t3_in], F32, [t1])
    t2_in = swap(t2, "head", 2)
    keep0, moved0 = second_hop(0, (over1, over3), [t2, over2])
    keep1, moved1 = second_hop(1, (over2, over4), [keep0])
    outs = finish(place, (t0, t1_in, t2_in), (keep0, keep1), (moved0, moved1))
    input_grad, grad_query, grad_key, grad_value, grad_out = outs
    return (input_grad[None], grad_query, grad_key, grad_value, grad_out)


def solution(mesh):
    return jax.shard_map(
        local,
        mesh=mesh,
        in_specs=(
            P("dp", "seq", None),
            P(None, "head"),
            P(None, "head"),
            P(None, "head"),
            P("head", None),
            P("dp", "seq", None),
        ),
        out_specs=(
            P("dp", "seq", "head"),
            P(("seq", "dp"), "head"),
            P(("seq", "dp"), "head"),
            P(("seq", "dp"), "head"),
            P("head", ("seq", "dp")),
        ),
        check_vma=False,
    )
```

```python
import functools

import jax
import jax.numpy as jnp
from jax import lax
from jax.experimental import pallas as pl
from jax.experimental.pallas import tpu as pltpu
from jax.sharding import PartitionSpec as P

HEAD_DIM = 128
BF16 = jnp.bfloat16
F32 = jnp.float32
MIB = 1024 * 1024
PLANNED = (2, 4, 4)
NN = ((1,), (0,))
NT = ((1,), (1,))
TN = ((0,), (0,))
ANYWHERE = pl.BlockSpec(memory_space=pl.ANY)
IN_VMEM = pl.BlockSpec(memory_space=pltpu.VMEM)
IN_SMEM = pl.BlockSpec(memory_space=pltpu.SMEM)


def dot(a, b, dims):
    return lax.dot_general(a, b, (dims, ((), ())), preferred_element_type=F32)


def shaped(shape, dtype):
    return jax.ShapeDtypeStruct(shape, dtype)


def params(mib):
    return pltpu.CompilerParams(vmem_limit_bytes=mib * MIB)


def cost(flops, size):
    return pl.CostEstimate(flops=flops, bytes_accessed=size, transcendentals=0)


class Place:
    def __init__(self, number, sizes):
        _, n_head, n_dp = sizes
        self.dp = lax.rem(number, n_dp)
        self.head = lax.rem(lax.div(number, n_dp), n_head)
        self.seq = lax.div(number, n_head * n_dp)
        self.core = lax.rem(self.dp, 2)


def position_scale(start, rows):
    positions = (start + lax.broadcasted_iota(jnp.int32, (rows, 1), 0)).astype(F32)
    return 1.0 / jnp.sqrt(HEAD_DIM * (positions + 1.0))


def project_part(place, part, xo_ref, wq_ref, wk_ref, wv_ref, wo_ref, out_ref, state_ref, arrived):
    rows, width = xo_ref.shape[1:]
    x_ref, o_ref = xo_ref.at[0], xo_ref.at[1]
    lower, upper = pl.ds(0, width // 2), pl.ds(width // 2, width // 2)

    def first(w_ref):
        arrived(0)
        product = dot(x_ref[:, lower], w_ref[lower, :], NN)
        arrived(1)
        out_ref[0] = (product + dot(x_ref[:, upper], w_ref[upper, :], NN)).astype(BF16)
        arrived(2)

    def state():
        if state_ref is not None:
            for h in range(state_ref.shape[0]):
                at = pl.ds(h * HEAD_DIM, HEAD_DIM)
                state_ref[h] = dot(out_ref[0, :, at], out_ref[1, :, at], TN)

    if part == 0:
        first(wk_ref)
        out_ref[1] = dot(x_ref[...], wv_ref[...], NN).astype(BF16)
    else:
        first(wq_ref)
        scale = position_scale(place.seq * rows, rows)
        out_ref[1] = (dot(o_ref[...], wo_ref[...], NT) * scale).astype(BF16)
    state()


def load_kernel(
    number_ref, x_hbm, o_hbm, wq_hbm, wk_hbm, wv_hbm, wo_hbm,
    out_ref, state_ref, xo_ref, wq_ref, wk_ref, wv_ref, wo_ref, sems, *, sizes, which,
):
    place = Place(number_ref[0], sizes)
    mid = xo_ref.shape[2] // 2
    lower, upper = pl.ds(0, mid), pl.ds(mid, mid)
    x_ref, o_ref = xo_ref.at[0], xo_ref.at[1]

    def run(part):
        w_hbm, w_ref = ((wk_hbm, wk_ref), (wq_hbm, wq_ref))[part]
        v, q, k = (wv_hbm, wv_ref), (wq_hbm, wq_ref), (wk_hbm, wk_ref)
        o, w_o = (o_hbm, o_ref), (wo_hbm, wo_ref)
        pairs = [
            (x_hbm.at[:, lower], x_ref.at[:, lower]),
            (w_hbm.at[lower], w_ref.at[lower]),
            (x_hbm.at[:, upper], x_ref.at[:, upper]),
            (w_hbm.at[upper], w_ref.at[upper]),
            *((v, q, o, w_o) if part == 0 else (o, w_o, k, v)),
        ]
        copies = [pltpu.make_async_copy(a, b, sems.at[i]) for i, (a, b) in enumerate(pairs)]
        needed = (2, 4, 5 if part == 0 else 6)
        for c in copies[:4]:
            c.start()

        def arrived(stage):
            for c in copies[needed[stage - 1] if stage else 0 : needed[stage]]:
                c.wait()
            if stage == 0:
                for c in copies[4:]:
                    c.start()

        project_part(
            place, part, xo_ref, wq_ref, wk_ref, wv_ref, wo_ref, out_ref, state_ref, arrived
        )
        for c in copies[needed[2] :]:
            c.wait()

    chosen = which(place)
    pl.when(chosen == 0)(lambda: run(0))
    pl.when(chosen != 0)(lambda: run(1))


def load(place, which, in_rows, grad_rows, w_query, w_key, w_value, w_out):
    number, sizes = place
    rows, width = in_rows.shape
    hd = w_query.shape[1]
    args = [
        pltpu.with_memory_space_constraint(a, pltpu.HBM)
        for a in (in_rows, grad_rows, w_query, w_key, w_value, w_out)
    ]
    out_shape = [
        pltpu.VMEM((2, rows, hd), BF16),
        pltpu.VMEM((hd // HEAD_DIM, HEAD_DIM, HEAD_DIM), F32),
        pltpu.VMEM((2, rows, width), BF16),
        *[pltpu.VMEM((width, hd), BF16)] * 3,
        pltpu.VMEM((hd, width), BF16),
    ]
    return pl.pallas_call(
        functools.partial(load_kernel, sizes=sizes, which=which),
        out_shape=out_shape,
        in_specs=[IN_SMEM] + [ANYWHERE] * 6,
        out_specs=[IN_VMEM] * len(out_shape),
        scratch_shapes=[pltpu.SemaphoreType.DMA((8,))],
        compiler_params=params(16),
        cost_estimate=cost(4 * rows * width * hd, 14 * MIB),
        name="load",
    )(number, *args)


def project_kernel(place, xo_ref, wq_ref, wk_ref, wv_ref, wo_ref, out_ref, *states, which):
    state_ref = states[0] if states else None

    def run(part):
        project_part(
            place, part, xo_ref, wq_ref, wk_ref, wv_ref, wo_ref, out_ref, state_ref, lambda stage: None
        )

    chosen = which(place)
    pl.when(chosen == 0)(lambda: run(0))
    pl.when(chosen != 0)(lambda: run(1))


def project(place, which, xo, weights, w_out, with_state):
    rows, width = xo.shape[1:]
    hd = w_out.shape[0]
    out = [shaped((2, rows, hd), BF16)]
    if with_state:
        out.append(shaped((hd // HEAD_DIM, HEAD_DIM, HEAD_DIM), F32))
    kernel = functools.partial(project_kernel, which=which)
    args = [xo, *weights, w_out]
    return call(kernel, "project", out, args, 4 * rows * width * hd, (), place)


def call(kernel, name, out_shape, args, flops, after=(), place=None):
    n, n_after = len(args), len(after)
    numbers = [] if place is None else [place[0]]

    def body(*refs):
        first = [Place(refs[0][0], place[1])] if numbers else []
        refs = refs[len(numbers) :]
        kernel(*first, *refs[:n], *refs[n + n_after :])

    many = isinstance(out_shape, (list, tuple))
    return pl.pallas_call(
        body,
        out_shape=out_shape,
        in_specs=[IN_SMEM] * len(numbers) + [IN_VMEM] * n + [ANYWHERE] * n_after,
        out_specs=[IN_VMEM] * len(out_shape) if many else IN_VMEM,
        compiler_params=params(16),
        cost_estimate=cost(flops, 2 * MIB),
        name=name,
    )(*numbers, *args, *after)


def attend_kernel(place, *refs, which, part_of, again):
    in_refs, rest = refs[:2], refs[2:]
    if again:
        state_ref, part_ref, scores_ref, out_ref = rest
    else:
        out_ref, scores_ref = rest
    rows, hd = out_ref.shape[1:]
    half = rows // 2
    top, low = slice(0, half), slice(half, rows)

    def causal(h, n, a, b):
        if not again:
            r = lax.broadcasted_iota(jnp.int32, (half, half), 0)
            c = lax.broadcasted_iota(jnp.int32, (half, half), 1)
            diagonal = r >= c
            scores_ref[h, n] = jnp.where(diagonal, dot(a[top], b[top], NT), 0.0).astype(BF16)
            scores_ref[h, n + 1] = dot(a[low], b[top], NT).astype(BF16)
            scores_ref[h, n + 2] = jnp.where(diagonal, dot(a[low], b[low], NT), 0.0).astype(BF16)
        return [scores_ref[h, n + i] for i in range(3)]

    def per_head(body, part):
        k_v, q_g = in_refs[part], in_refs[1 - part]

        def step(h, carry):
            at = pl.ds(pl.multiple_of(h * HEAD_DIM, HEAD_DIM), HEAD_DIM)
            state = state_ref[h].astype(BF16) if again else None

            def put(slot, halves, cross, dims, scale=None):
                added = dot(cross, state, dims) if again else None
                for rows_at, value in zip((top, low), halves):
                    if again:
                        value = value + added[rows_at]
                    if scale is not None:
                        value = value * scale[rows_at]
                    out_ref[slot, rows_at, at] = value.astype(BF16)

            body(h, [ref[i, :, at] for ref in (k_v, q_g) for i in (0, 1)], put)
            return carry

        lax.fori_loop(0, hd // HEAD_DIM, step, 0, unroll=True)

    def forward():
        scale = position_scale(place.seq * rows, rows)

        def body(h, heads, put):
            k, v, q, g = heads
            for slot, a, b, c, dims in ((0, q, k, v, NN), (1, g, v, k, NT)):
                s00, s10, s11 = causal(h, 3 * slot, a, b)
                halves = (dot(s00, c[top], NN), dot(s10, c[top], NN) + dot(s11, c[low], NN))
                put(slot, halves, a, dims, scale if slot == 0 else None)

        per_head(body, part_of(0))

    def backward():
        def body(h, heads, put):
            k, v, q, g = heads
            for slot, a, b, c, dims in ((2, q, k, g, NN), (3, g, v, q, NT)):
                s00, s10, s11 = causal(h, 3 * slot - 6, a, b)
                halves = (dot(s00, c[top], TN) + dot(s10, c[low], TN), dot(s11, c[low], TN))
                put(slot, halves, b, dims)

        per_head(body, part_of(1))

    chosen = which(place)
    if again:
        for t in (0, 1):
            out_ref[2 - 2 * chosen + t] = part_ref[2 - 2 * chosen + t]
    pl.when(chosen == 0)(forward)
    pl.when(chosen != 0)(backward)


def attend(place, which, part_of, projected, more=(), after=()):
    rows, hd = projected[0].shape[1:]
    out = shaped((4, rows, hd), BF16)
    scores = shaped((hd // HEAD_DIM, 6, rows // 2, rows // 2), BF16)
    kernel = functools.partial(attend_kernel, which=which, part_of=part_of, again=bool(more))
    outs = out if more else [out, scores]
    return call(kernel, "attend", outs, [*projected, *more], 128 * rows * rows * hd, after, place)


def head_terms_kernel(place, d_ref, wq_ref, wk_ref, wv_ref, out_ref, *, shard):
    width = out_ref.shape[1]
    step = min(width, 256)
    start = shard(place) * width
    for i in range(width // step):
        rows = pl.ds(pl.multiple_of(start + i * step, step), step)
        out_ref[:, pl.ds(i * step, step)] = (
            dot(d_ref[1], wq_ref[rows, :], NT)
            + dot(d_ref[3], wk_ref[rows, :], NT)
            + dot(d_ref[2], wv_ref[rows, :], NT)
        )


def head_terms(place, results, weights, shard, shards, after=()):
    width, hd = weights[0].shape
    rows = results.shape[1]
    return call(
        functools.partial(head_terms_kernel, shard=shard),
        "head_terms",
        shaped((rows, width // shards), F32),
        [results, *weights],
        6 * rows * width // shards * hd,
        after,
        place,
    )


def add_kernel(*refs):
    total = refs[0][...]
    for ref in refs[1:-1]:
        total = total + ref[...]
    refs[-1][...] = total.astype(refs[-1].dtype)


def add(arrays, dtype, after=()):
    return call(add_kernel, "add", shaped(arrays[0].shape, dtype), list(arrays), 0, after)


def column_block(place, i):
    return (place.seq ^ (i // 2 % 2)) * 4 + (place.dp ^ (i % 2 * 2 + i // 4))


def fill_tiles(place, xo_ref, d_ref, pair, side, blocks, scale, added, outs):
    half = d_ref.shape[2] // 2
    block = outs[0].shape[1]
    features = pl.ds(pl.multiple_of(side * half, half), half)
    for i, b in enumerate(blocks):
        columns = pl.ds(pl.multiple_of(column_block(place, b) * block, block), block)
        for t, rows in enumerate((1 - pair, 0)):
            tile = dot(xo_ref[rows, :, columns], d_ref[2 * pair + t, :, features], TN) * scale
            for read in added:
                tile = tile + read(i, t)
            outs[i][t] = tile


def other_core_kernel(place, xo_ref, d_ref, out_ref, *, early, slot, scale):
    outs = [out_ref.at[i] for i in range(4)]
    pair, side = place.seq ^ early, 1 - place.core ^ slot
    fill_tiles(place, xo_ref, d_ref, pair, side, (4, 5, 6, 7), scale, (), outs)


def other_core_both_kernel(place, xo_ref, d_ref, *out_refs, early, scale):
    pair = place.seq ^ early
    half = d_ref.shape[2] // 2
    block = out_refs[0].shape[2]
    sides = (1 - place.core, place.core)
    for t, rows in enumerate((1 - pair, 0)):
        features = [pl.ds(pl.multiple_of(side * half, half), half) for side in sides]
        d = jnp.concatenate([d_ref[2 * pair + t, :, at] for at in features], axis=1)
        for i in range(4):
            columns = pl.ds(pl.multiple_of(column_block(place, 4 + i) * block, block), block)
            tile = dot(xo_ref[rows, :, columns], d, TN) * scale
            out_refs[0][i, t] = tile[:, :half]
            out_refs[1][i, t] = tile[:, half:]


def first_hop_kernel(place, xo_ref, d_ref, far_ref, out_ref, *, early, slot, scale):
    pair, side = place.seq ^ early, place.core ^ slot
    blocks = (2 - side, 3)
    outs = [out_ref.at[i] for i in range(2)]
    added = (lambda i, t: far_ref[blocks[i], t],)
    fill_tiles(place, xo_ref, d_ref, pair, side, blocks, scale, added, outs)


def second_hop_kernel(
    place, xo_ref, d_ref, far0_ref, far1_ref, over0_ref, over1_ref, keep_ref, send_ref,
    *, slot, scale,
):
    over = (over0_ref, over1_ref)
    side = place.core ^ slot
    blocks = (0, 1 + side)

    def far(p, i, t):
        return (far0_ref, far1_ref)[p][blocks[i], t]

    for p in (0, 1):
        added = (
            lambda i, t: jnp.where(side == 0, far(1 - p, i, t), far(p, i, t)),
            lambda i, t: over[p][i, t],
        )
        pair = place.seq ^ p ^ 1 - side
        outs = (keep_ref.at[p], send_ref.at[p])
        fill_tiles(place, xo_ref, d_ref, pair, side, blocks, scale, added, outs)


def put_side(place, slot, kept_ref, moved_ref, part_ref, out_refs, sems):
    side = place.core ^ slot
    half = part_ref.shape[1]
    at = pl.ds(pl.multiple_of(side * half, half), half)
    copies = []
    for i, (pair, t) in enumerate(((0, 1), (1, 1), (1, 0), (0, 0))):
        p = place.seq ^ pair
        total = kept_ref[p ^ 1 - side, t] + moved_ref[1 - p, t]
        part_ref[i] = total if i < 3 else total.T
        out = out_refs[i].at[:, at] if i < 3 else out_refs[i].at[at]
        copies.append(pltpu.make_async_copy(part_ref.at[i], out, sems.at[i]))
        copies[-1].start()
    return copies


def settle_kernel(number_ref, kept_ref, moved_ref, after_ref, *rest, sizes):
    out_refs, (part_ref, sems) = rest[:4], rest[4:]
    place = Place(number_ref[0], sizes)
    for c in put_side(place, 0, kept_ref, moved_ref, part_ref, out_refs, sems):
        c.wait()


def finish_kernel(number_ref, *refs, sizes):
    line, (kept_ref, moved_ref) = refs[:3], refs[3:5]
    input_out, out_refs, (part_ref, input_ref, sems) = refs[9], refs[10:14], refs[14:]
    place = Place(number_ref[0], sizes)
    copies = put_side(place, 1, kept_ref, moved_ref, part_ref, out_refs, sems)
    rows = input_ref.shape[0] // 2
    for i in (0, 1):
        at = pl.ds(i * rows, rows)
        input_ref[at] = (line[0][at] + line[1][at] + line[2][at]).astype(BF16)
        copies.append(pltpu.make_async_copy(input_ref.at[at], input_out.at[at], sems.at[4 + i]))
        copies[-1].start()
    for c in copies:
        c.wait()


def finish(place, line, kept, moved):
    number, sizes = place
    block, half = kept[0].shape[2:]
    tall, wide = pltpu.HBM((block, 2 * half), F32), pltpu.HBM((2 * half, block), F32)
    grads = [tall, tall, tall, wide]
    parts = pltpu.VMEM((4, block, half), F32)
    sides = pl.pallas_call(
        functools.partial(settle_kernel, sizes=sizes),
        out_shape=grads,
        in_specs=[IN_SMEM, IN_VMEM, IN_VMEM, ANYWHERE],
        out_specs=[ANYWHERE] * 4,
        scratch_shapes=[parts, pltpu.SemaphoreType.DMA((4,))],
        compiler_params=params(16),
        cost_estimate=cost(0, 2 * MIB),
        name="settle",
    )(number, kept[0], moved[0], kept[1])
    return pl.pallas_call(
        functools.partial(finish_kernel, sizes=sizes),
        out_shape=[pltpu.HBM(line[0].shape, BF16), *grads],
        in_specs=[IN_SMEM] + [IN_VMEM] * 5 + [ANYWHERE] * 4,
        out_specs=[ANYWHERE] * 5,
        input_output_aliases={6 + i: 1 + i for i in range(4)},
        scratch_shapes=[parts, pltpu.VMEM(line[0].shape, BF16), pltpu.SemaphoreType.DMA((6,))],
        compiler_params=params(16),
        cost_estimate=cost(0, 2 * MIB),
        name="finish",
    )(number, *line, kept[1], moved[1], *sides)


def states_before(x, axis, reverse):
    peers, here = (lax.axis_size(axis), lax.axis_index(axis))
    everything = lax.all_gather(x, axis)
    at = jnp.arange(peers)
    reached = at > here if reverse else at < here
    return jnp.sum(jnp.where(reached[:, None, None, None], everything, 0.0), axis=0)


def swap(x, axis, bit):
    return lax.ppermute(x, axis, [(i, i ^ bit) for i in range(lax.axis_size(axis))])


def local(layer_input, w_query, w_key, w_value, w_out, out_grad):
    num_rows = layer_input.shape[1]
    n_seq, n_head, n_dp = (lax.axis_size(a) for a in ("seq", "head", "dp"))
    scale = float(n_seq * n_dp * num_rows) ** -0.5

    sizes = (n_seq, n_head, n_dp)
    number = (lax.axis_index("seq") * n_head + lax.axis_index("head")) * n_dp + lax.axis_index("dp")
    number = number.astype(jnp.int32).reshape(1)
    place = (number, sizes)
    arrays = (layer_input[0], out_grad[0], w_query, w_key, w_value, w_out)
    planned = sizes == PLANNED
    part = (lambda at: at.seq) if planned else (lambda at: 0)
    projected, state, xo, *weights, wo = load(place, part, *arrays)
    if planned:
        state = swap(state, "seq", 1)
    other, *more = project(place, lambda at: 1 - part(at), xo, weights, wo, not planned)
    projected = (projected, other)

    if not planned:
        prefix = states_before(state, "seq", False)
        suffix = states_before(more[0], "seq", True)
        d, scores = attend(place, lambda at: 0, lambda which: 0, projected)
        d = attend(place, lambda at: 0, lambda which: 0, projected, (prefix, d, scores))
        d = attend(place, lambda at: 1, lambda which: 0, projected, (suffix, d, scores))
        terms = head_terms(place, d, weights, lambda at: 0, 1)

        def reduced(rows, d):
            return lax.psum_scatter(
                dot(rows, d, TN) * scale, ("seq", "dp"), scatter_dimension=0, tiled=True
            )

        return (
            lax.psum_scatter(terms, "head", scatter_dimension=1, tiled=True).astype(BF16)[None],
            reduced(xo[0], d[1]),
            reduced(xo[0], d[3]),
            reduced(xo[0], d[2]),
            reduced(xo[1], d[0]).T,
        )

    def term(flip, after):
        return head_terms(place, d, weights, lambda at: at.head ^ flip, n_head, after)

    def hop(array, slot, second):
        pairs = []
        for i in range(8):
            side = i % 2 ^ slot
            pairs.append((i, i ^ (4 if side == second else 2)))
        return lax.ppermute(array, ("seq", "dp"), pairs)

    block, half = xo.shape[2] // 8, projected[0].shape[2] // 2
    tile = (2, block, half)
    flops = 4 * num_rows * block * half

    def to_core(d, early, slot, after):
        kernel = functools.partial(other_core_kernel, early=early, slot=slot, scale=scale)
        out = shaped((4, *tile), F32)
        array = call(kernel, "other_core", out, [xo, d], 4 * flops, after, place)
        return array, swap(array, "dp", 1)

    def both_to_core(d, early, after):
        kernel = functools.partial(other_core_both_kernel, early=early, scale=scale)
        outs = [shaped((4, *tile), F32)] * 2
        arrays = call(kernel, "other_core_both", outs, [xo, d], 8 * flops, after, place)
        return arrays[0], [swap(array, "dp", 1) for array in arrays]

    def first_hop(early, slot, after):
        kernel = functools.partial(first_hop_kernel, early=early, slot=slot, scale=scale)
        out = shaped((2, *tile), F32)
        args = [xo, d, far[early][slot]]
        array = call(kernel, "first_hop", out, args, 2 * flops, after, place)
        return array, hop(array, slot, 0)

    def second_hop(slot, over, after):
        kernel = functools.partial(second_hop_kernel, slot=slot, scale=scale)
        outs = [shaped((2, *tile), F32)] * 2
        args = [xo, d, far[0][slot], far[1][slot], *over]
        keep, leave = call(kernel, "second_hop", outs, args, 4 * flops, after, place)
        return keep, hop(leave, slot, 1)

    early, scores = attend(place, lambda at: at.seq, lambda which: which, projected)
    far = ([None, None], [None, None])
    at, far[0][0] = to_core(early, 0, 0, [])
    at, far[0][1] = to_core(early, 0, 1, [at])
    d = attend(place, lambda at: 1 - at.seq, lambda which: 1 - which, projected, (state, early, scores), [at])
    at, far[1][:] = both_to_core(d, 1, [])
    at, over1 = first_hop(0, 0, [at])
    t3 = term(3, [at])
    t3_in = swap(t3, "head", 1)
    at, over2 = first_hop(0, 1, [t3])
    at, over3 = first_hop(1, 0, [at])
    at, over4 = first_hop(1, 1, [at])
    t2 = term(2, [at])
    t0 = term(0, [t2])
    t1 = term(1, [t0, over1])
    t1_in = swap(t1, "head", 1)
    t2 = add([t2, t3_in], F32, [t1])
    t2_in = swap(t2, "head", 2)
    keep0, moved0 = second_hop(0, (over1, over3), [t2, over2])
    keep1, moved1 = second_hop(1, (over2, over4), [keep0])
    outs = finish(place, (t0, t1_in, t2_in), (keep0, keep1), (moved0, moved1))
    input_grad, grad_query, grad_key, grad_value, grad_out = outs
    return (input_grad[None], grad_query, grad_key, grad_value, grad_out)


def solution(mesh):
    return jax.shard_map(
        local,
        mesh=mesh,
        in_specs=(
            P("dp", "seq", None),
            P(None, "head"),
            P(None, "head"),
            P(None, "head"),
            P("head", None),
            P("dp", "seq", None),
        ),
        out_specs=(
            P("dp", "seq", "head"),
            P(("seq", "dp"), "head"),
            P(("seq", "dp"), "head"),
            P(("seq", "dp"), "head"),
            P("head", ("seq", "dp")),
        ),
        check_vma=False,
    )
```

```python
import functools

import jax
import jax.numpy as jnp
from jax import lax
from jax.experimental import pallas as pl
from jax.experimental.pallas import tpu as pltpu
from jax.sharding import PartitionSpec as P

HEAD_DIM = 128
BF16 = jnp.bfloat16
F32 = jnp.float32
MIB = 1024 * 1024
PLANNED = (2, 4, 4)
NN = ((1,), (0,))
NT = ((1,), (1,))
TN = ((0,), (0,))
ANYWHERE = pl.BlockSpec(memory_space=pl.ANY)
IN_VMEM = pl.BlockSpec(memory_space=pltpu.VMEM)
IN_SMEM = pl.BlockSpec(memory_space=pltpu.SMEM)


def dot(a, b, dims):
    return lax.dot_general(a, b, (dims, ((), ())), preferred_element_type=F32)


def shaped(shape, dtype):
    return jax.ShapeDtypeStruct(shape, dtype)


def params(mib):
    return pltpu.CompilerParams(vmem_limit_bytes=mib * MIB)


def cost(flops, size):
    return pl.CostEstimate(flops=flops, bytes_accessed=size, transcendentals=0)


class Place:
    def __init__(self, number, sizes):
        _, n_head, n_dp = sizes
        self.dp = lax.rem(number, n_dp)
        self.head = lax.rem(lax.div(number, n_dp), n_head)
        self.seq = lax.div(number, n_head * n_dp)
        self.core = lax.rem(self.dp, 2)


def position_scale(start, rows):
    positions = (start + lax.broadcasted_iota(jnp.int32, (rows, 1), 0)).astype(F32)
    return 1.0 / jnp.sqrt(HEAD_DIM * (positions + 1.0))


def project_part(place, part, xo_ref, wq_ref, wk_ref, wv_ref, wo_ref, out_ref, state_ref, arrived):
    rows, width = xo_ref.shape[1:]
    x_ref, o_ref = xo_ref.at[0], xo_ref.at[1]
    lower, upper = pl.ds(0, width // 2), pl.ds(width // 2, width // 2)

    def first(w_ref):
        arrived(0)
        product = dot(x_ref[:, lower], w_ref[lower, :], NN)
        arrived(1)
        out_ref[0] = (product + dot(x_ref[:, upper], w_ref[upper, :], NN)).astype(BF16)
        arrived(2)

    def state():
        if state_ref is not None:
            for h in range(state_ref.shape[0]):
                at = pl.ds(h * HEAD_DIM, HEAD_DIM)
                state_ref[h] = dot(out_ref[0, :, at], out_ref[1, :, at], TN)

    if part == 0:
        first(wk_ref)
        out_ref[1] = dot(x_ref[...], wv_ref[...], NN).astype(BF16)
    else:
        first(wq_ref)
        scale = position_scale(place.seq * rows, rows)
        out_ref[1] = (dot(o_ref[...], wo_ref[...], NT) * scale).astype(BF16)
    state()


def load_kernel(
    number_ref, x_hbm, o_hbm, wq_hbm, wk_hbm, wv_hbm, wo_hbm,
    out_ref, state_ref, xo_ref, wq_ref, wk_ref, wv_ref, wo_ref, sems, *, sizes, which,
):
    place = Place(number_ref[0], sizes)
    mid = xo_ref.shape[2] // 2
    lower, upper = pl.ds(0, mid), pl.ds(mid, mid)
    x_ref, o_ref = xo_ref.at[0], xo_ref.at[1]

    def run(part):
        w_hbm, w_ref = ((wk_hbm, wk_ref), (wq_hbm, wq_ref))[part]
        v, q, k = (wv_hbm, wv_ref), (wq_hbm, wq_ref), (wk_hbm, wk_ref)
        o, w_o = (o_hbm, o_ref), (wo_hbm, wo_ref)
        pairs = [
            (x_hbm.at[:, lower], x_ref.at[:, lower]),
            (w_hbm.at[lower], w_ref.at[lower]),
            (x_hbm.at[:, upper], x_ref.at[:, upper]),
            (w_hbm.at[upper], w_ref.at[upper]),
            *((v, q, o, w_o) if part == 0 else (o, w_o, k, v)),
        ]
        copies = [pltpu.make_async_copy(a, b, sems.at[i]) for i, (a, b) in enumerate(pairs)]
        needed = (2, 4, 5 if part == 0 else 6)
        for c in copies[:4]:
            c.start()

        def arrived(stage):
            for c in copies[needed[stage - 1] if stage else 0 : needed[stage]]:
                c.wait()
            if stage == 0:
                for c in copies[4:]:
                    c.start()

        project_part(
            place, part, xo_ref, wq_ref, wk_ref, wv_ref, wo_ref, out_ref, state_ref, arrived
        )
        for c in copies[needed[2] :]:
            c.wait()

    chosen = which(place)
    pl.when(chosen == 0)(lambda: run(0))
    pl.when(chosen != 0)(lambda: run(1))


def load(place, which, in_rows, grad_rows, w_query, w_key, w_value, w_out):
    number, sizes = place
    rows, width = in_rows.shape
    hd = w_query.shape[1]
    args = [
        pltpu.with_memory_space_constraint(a, pltpu.HBM)
        for a in (in_rows, grad_rows, w_query, w_key, w_value, w_out)
    ]
    out_shape = [
        pltpu.VMEM((2, rows, hd), BF16),
        pltpu.VMEM((hd // HEAD_DIM, HEAD_DIM, HEAD_DIM), F32),
        pltpu.VMEM((2, rows, width), BF16),
        *[pltpu.VMEM((width, hd), BF16)] * 3,
        pltpu.VMEM((hd, width), BF16),
    ]
    return pl.pallas_call(
        functools.partial(load_kernel, sizes=sizes, which=which),
        out_shape=out_shape,
        in_specs=[IN_SMEM] + [ANYWHERE] * 6,
        out_specs=[IN_VMEM] * len(out_shape),
        scratch_shapes=[pltpu.SemaphoreType.DMA((8,))],
        compiler_params=params(16),
        cost_estimate=cost(4 * rows * width * hd, 14 * MIB),
        name="load",
    )(number, *args)


def project_kernel(place, xo_ref, wq_ref, wk_ref, wv_ref, wo_ref, out_ref, *states, which):
    state_ref = states[0] if states else None

    def run(part):
        project_part(
            place, part, xo_ref, wq_ref, wk_ref, wv_ref, wo_ref, out_ref, state_ref, lambda stage: None
        )

    chosen = which(place)
    pl.when(chosen == 0)(lambda: run(0))
    pl.when(chosen != 0)(lambda: run(1))


def project(place, which, xo, weights, w_out, with_state):
    rows, width = xo.shape[1:]
    hd = w_out.shape[0]
    out = [shaped((2, rows, hd), BF16)]
    if with_state:
        out.append(shaped((hd // HEAD_DIM, HEAD_DIM, HEAD_DIM), F32))
    kernel = functools.partial(project_kernel, which=which)
    args = [xo, *weights, w_out]
    return call(kernel, "project", out, args, 4 * rows * width * hd, (), place)


def call(kernel, name, out_shape, args, flops, after=(), place=None):
    n, n_after = len(args), len(after)
    numbers = [] if place is None else [place[0]]

    def body(*refs):
        first = [Place(refs[0][0], place[1])] if numbers else []
        refs = refs[len(numbers) :]
        kernel(*first, *refs[:n], *refs[n + n_after :])

    many = isinstance(out_shape, (list, tuple))
    return pl.pallas_call(
        body,
        out_shape=out_shape,
        in_specs=[IN_SMEM] * len(numbers) + [IN_VMEM] * n + [ANYWHERE] * n_after,
        out_specs=[IN_VMEM] * len(out_shape) if many else IN_VMEM,
        compiler_params=params(16),
        cost_estimate=cost(flops, 2 * MIB),
        name=name,
    )(*numbers, *args, *after)


def attend_kernel(place, *refs, which, part_of, again):
    in_refs, rest = refs[:2], refs[2:]
    if again:
        state_ref, part_ref, scores_ref, out_ref = rest
    else:
        out_ref, scores_ref = rest
    rows, hd = out_ref.shape[1:]
    half = rows // 2
    top, low = slice(0, half), slice(half, rows)

    def causal(h, n, a, b):
        if not again:
            r = lax.broadcasted_iota(jnp.int32, (half, half), 0)
            c = lax.broadcasted_iota(jnp.int32, (half, half), 1)
            diagonal = r >= c
            scores_ref[h, n] = jnp.where(diagonal, dot(a[top], b[top], NT), 0.0).astype(BF16)
            scores_ref[h, n + 1] = dot(a[low], b[top], NT).astype(BF16)
            scores_ref[h, n + 2] = jnp.where(diagonal, dot(a[low], b[low], NT), 0.0).astype(BF16)
        return [scores_ref[h, n + i] for i in range(3)]

    def per_head(body, part):
        k_v, q_g = in_refs[part], in_refs[1 - part]

        def step(h, carry):
            at = pl.ds(pl.multiple_of(h * HEAD_DIM, HEAD_DIM), HEAD_DIM)
            state = state_ref[h].astype(BF16) if again else None

            def put(slot, halves, cross, dims, scale=None):
                added = dot(cross, state, dims) if again else None
                for rows_at, value in zip((top, low), halves):
                    if again:
                        value = value + added[rows_at]
                    if scale is not None:
                        value = value * scale[rows_at]
                    out_ref[slot, rows_at, at] = value.astype(BF16)

            body(h, [ref[i, :, at] for ref in (k_v, q_g) for i in (0, 1)], put)
            return carry

        lax.fori_loop(0, hd // HEAD_DIM, step, 0, unroll=True)

    def forward():
        scale = position_scale(place.seq * rows, rows)

        def body(h, heads, put):
            k, v, q, g = heads
            for slot, a, b, c, dims in ((0, q, k, v, NN), (1, g, v, k, NT)):
                s00, s10, s11 = causal(h, 3 * slot, a, b)
                halves = (dot(s00, c[top], NN), dot(s10, c[top], NN) + dot(s11, c[low], NN))
                put(slot, halves, a, dims, scale if slot == 0 else None)

        per_head(body, part_of(0))

    def backward():
        def body(h, heads, put):
            k, v, q, g = heads
            for slot, a, b, c, dims in ((2, q, k, g, NN), (3, g, v, q, NT)):
                s00, s10, s11 = causal(h, 3 * slot - 6, a, b)
                halves = (dot(s00, c[top], TN) + dot(s10, c[low], TN), dot(s11, c[low], TN))
                put(slot, halves, b, dims)

        per_head(body, part_of(1))

    chosen = which(place)
    if again:
        for t in (0, 1):
            out_ref[2 - 2 * chosen + t] = part_ref[2 - 2 * chosen + t]
    pl.when(chosen == 0)(forward)
    pl.when(chosen != 0)(backward)


def attend(place, which, part_of, projected, more=(), after=()):
    rows, hd = projected[0].shape[1:]
    out = shaped((4, rows, hd), BF16)
    scores = shaped((hd // HEAD_DIM, 6, rows // 2, rows // 2), BF16)
    kernel = functools.partial(attend_kernel, which=which, part_of=part_of, again=bool(more))
    outs = out if more else [out, scores]
    return call(kernel, "attend", outs, [*projected, *more], 128 * rows * rows * hd, after, place)


def head_terms_kernel(place, d_ref, wq_ref, wk_ref, wv_ref, out_ref, *, shard):
    width = out_ref.shape[1]
    step = min(width, 256)
    start = shard(place) * width
    for i in range(width // step):
        rows = pl.ds(pl.multiple_of(start + i * step, step), step)
        out_ref[:, pl.ds(i * step, step)] = (
            dot(d_ref[1], wq_ref[rows, :], NT)
            + dot(d_ref[3], wk_ref[rows, :], NT)
            + dot(d_ref[2], wv_ref[rows, :], NT)
        )


def head_terms(place, results, weights, shard, shards, after=()):
    width, hd = weights[0].shape
    rows = results.shape[1]
    return call(
        functools.partial(head_terms_kernel, shard=shard),
        "head_terms",
        shaped((rows, width // shards), F32),
        [results, *weights],
        6 * rows * width // shards * hd,
        after,
        place,
    )


def add_kernel(*refs):
    total = refs[0][...]
    for ref in refs[1:-1]:
        total = total + ref[...]
    refs[-1][...] = total.astype(refs[-1].dtype)


def add(arrays, dtype, after=()):
    return call(add_kernel, "add", shaped(arrays[0].shape, dtype), list(arrays), 0, after)


def column_block(place, i):
    return (place.seq ^ (i // 2 % 2)) * 4 + (place.dp ^ (i % 2 * 2 + i // 4))


def fill_tiles(place, xo_ref, d_ref, pair, side, blocks, scale, added, outs):
    half = d_ref.shape[2] // 2
    block = outs[0].shape[1]
    features = pl.ds(pl.multiple_of(side * half, half), half)
    for i, b in enumerate(blocks):
        columns = pl.ds(pl.multiple_of(column_block(place, b) * block, block), block)
        for t, rows in enumerate((1 - pair, 0)):
            tile = dot(xo_ref[rows, :, columns], d_ref[2 * pair + t, :, features], TN) * scale
            for read in added:
                tile = tile + read(i, t)
            outs[i][t] = tile


def other_core_kernel(place, xo_ref, d_ref, out_ref, *, early, slot, scale):
    outs = [out_ref.at[i] for i in range(4)]
    pair, side = place.seq ^ early, 1 - place.core ^ slot
    fill_tiles(place, xo_ref, d_ref, pair, side, (4, 5, 6, 7), scale, (), outs)


def other_core_both_kernel(place, xo_ref, d_ref, *out_refs, early, scale):
    pair = place.seq ^ early
    half = d_ref.shape[2] // 2
    block = out_refs[0].shape[2]
    sides = (1 - place.core, place.core)
    for t, rows in enumerate((1 - pair, 0)):
        features = [pl.ds(pl.multiple_of(side * half, half), half) for side in sides]
        d = jnp.concatenate([d_ref[2 * pair + t, :, at] for at in features], axis=1)
        for i in range(4):
            columns = pl.ds(pl.multiple_of(column_block(place, 4 + i) * block, block), block)
            tile = dot(xo_ref[rows, :, columns], d, TN) * scale
            out_refs[0][i, t] = tile[:, :half]
            out_refs[1][i, t] = tile[:, half:]


def first_hop_kernel(place, xo_ref, d_ref, far_ref, out_ref, *, early, slot, scale):
    pair, side = place.seq ^ early, place.core ^ slot
    blocks = (2 - side, 3)
    outs = [out_ref.at[i] for i in range(2)]
    added = (lambda i, t: far_ref[blocks[i], t],)
    fill_tiles(place, xo_ref, d_ref, pair, side, blocks, scale, added, outs)


def second_hop_kernel(
    place, xo_ref, d_ref, far0_ref, far1_ref, over0_ref, over1_ref, keep_ref, send_ref,
    *, slot, scale,
):
    over = (over0_ref, over1_ref)
    side = place.core ^ slot
    blocks = (0, 1 + side)

    def far(p, i, t):
        return (far0_ref, far1_ref)[p][blocks[i], t]

    for p in (0, 1):
        added = (
            lambda i, t: jnp.where(side == 0, far(1 - p, i, t), far(p, i, t)),
            lambda i, t: over[p][i, t],
        )
        pair = place.seq ^ p ^ 1 - side
        outs = (keep_ref.at[p], send_ref.at[p])
        fill_tiles(place, xo_ref, d_ref, pair, side, blocks, scale, added, outs)


def put_side(place, slot, kept_ref, moved_ref, part_ref, out_refs, sems):
    side = place.core ^ slot
    half = part_ref.shape[1]
    at = pl.ds(pl.multiple_of(side * half, half), half)
    copies = []
    for i, (pair, t) in enumerate(((0, 1), (1, 1), (1, 0), (0, 0))):
        p = place.seq ^ pair
        total = kept_ref[p ^ 1 - side, t] + moved_ref[1 - p, t]
        part_ref[i] = total if i < 3 else total.T
        out = out_refs[i].at[:, at] if i < 3 else out_refs[i].at[at]
        copies.append(pltpu.make_async_copy(part_ref.at[i], out, sems.at[i]))
        copies[-1].start()
    return copies


def settle_kernel(number_ref, kept_ref, moved_ref, after_ref, *rest, sizes):
    out_refs, (part_ref, sems) = rest[:4], rest[4:]
    place = Place(number_ref[0], sizes)
    for c in put_side(place, 0, kept_ref, moved_ref, part_ref, out_refs, sems):
        c.wait()


def finish_kernel(number_ref, *refs, sizes):
    line, (kept_ref, moved_ref) = refs[:3], refs[3:5]
    input_out, out_refs, (part_ref, input_ref, sems) = refs[9], refs[10:14], refs[14:]
    place = Place(number_ref[0], sizes)
    copies = put_side(place, 1, kept_ref, moved_ref, part_ref, out_refs, sems)
    rows = input_ref.shape[0] // 2
    for i in (0, 1):
        at = pl.ds(i * rows, rows)
        input_ref[at] = (line[0][at] + line[1][at] + line[2][at]).astype(BF16)
        copies.append(pltpu.make_async_copy(input_ref.at[at], input_out.at[at], sems.at[4 + i]))
        copies[-1].start()
    for c in copies:
        c.wait()


def finish(place, line, kept, moved):
    number, sizes = place
    block, half = kept[0].shape[2:]
    tall, wide = pltpu.HBM((block, 2 * half), F32), pltpu.HBM((2 * half, block), F32)
    grads = [tall, tall, tall, wide]
    parts = pltpu.VMEM((4, block, half), F32)
    sides = pl.pallas_call(
        functools.partial(settle_kernel, sizes=sizes),
        out_shape=grads,
        in_specs=[IN_SMEM, IN_VMEM, IN_VMEM, ANYWHERE],
        out_specs=[ANYWHERE] * 4,
        scratch_shapes=[parts, pltpu.SemaphoreType.DMA((4,))],
        compiler_params=params(16),
        cost_estimate=cost(0, 2 * MIB),
        name="settle",
    )(number, kept[0], moved[0], kept[1])
    return pl.pallas_call(
        functools.partial(finish_kernel, sizes=sizes),
        out_shape=[pltpu.HBM(line[0].shape, BF16), *grads],
        in_specs=[IN_SMEM] + [IN_VMEM] * 5 + [ANYWHERE] * 4,
        out_specs=[ANYWHERE] * 5,
        input_output_aliases={6 + i: 1 + i for i in range(4)},
        scratch_shapes=[parts, pltpu.VMEM(line[0].shape, BF16), pltpu.SemaphoreType.DMA((6,))],
        compiler_params=params(16),
        cost_estimate=cost(0, 2 * MIB),
        name="finish",
    )(number, *line, kept[1], moved[1], *sides)


def states_before(x, axis, reverse):
    peers, here = (lax.axis_size(axis), lax.axis_index(axis))
    everything = lax.all_gather(x, axis)
    at = jnp.arange(peers)
    reached = at > here if reverse else at < here
    return jnp.sum(jnp.where(reached[:, None, None, None], everything, 0.0), axis=0)


def swap(x, axis, bit):
    return lax.ppermute(x, axis, [(i, i ^ bit) for i in range(lax.axis_size(axis))])


def local(layer_input, w_query, w_key, w_value, w_out, out_grad):
    num_rows = layer_input.shape[1]
    n_seq, n_head, n_dp = (lax.axis_size(a) for a in ("seq", "head", "dp"))
    scale = float(n_seq * n_dp * num_rows) ** -0.5

    sizes = (n_seq, n_head, n_dp)
    number = (lax.axis_index("seq") * n_head + lax.axis_index("head")) * n_dp + lax.axis_index("dp")
    number = number.astype(jnp.int32).reshape(1)
    place = (number, sizes)
    arrays = (layer_input[0], out_grad[0], w_query, w_key, w_value, w_out)
    planned = sizes == PLANNED
    part = (lambda at: at.seq) if planned else (lambda at: 0)
    projected, state, xo, *weights, wo = load(place, part, *arrays)
    if planned:
        state = swap(state, "seq", 1)
    other, *more = project(place, lambda at: 1 - part(at), xo, weights, wo, not planned)
    projected = (projected, other)

    if not planned:
        prefix = states_before(state, "seq", False)
        suffix = states_before(more[0], "seq", True)
        d, scores = attend(place, lambda at: 0, lambda which: 0, projected)
        d = attend(place, lambda at: 0, lambda which: 0, projected, (prefix, d, scores))
        d = attend(place, lambda at: 1, lambda which: 0, projected, (suffix, d, scores))
        terms = head_terms(place, d, weights, lambda at: 0, 1)

        def reduced(rows, d):
            return lax.psum_scatter(
                dot(rows, d, TN) * scale, ("seq", "dp"), scatter_dimension=0, tiled=True
            )

        return (
            lax.psum_scatter(terms, "head", scatter_dimension=1, tiled=True).astype(BF16)[None],
            reduced(xo[0], d[1]),
            reduced(xo[0], d[3]),
            reduced(xo[0], d[2]),
            reduced(xo[1], d[0]).T,
        )

    def term(flip, after):
        return head_terms(place, d, weights, lambda at: at.head ^ flip, n_head, after)

    def hop(array, slot, second):
        pairs = []
        for i in range(8):
            side = i % 2 ^ slot
            pairs.append((i, i ^ (4 if side == second else 2)))
        return lax.ppermute(array, ("seq", "dp"), pairs)

    block, half = xo.shape[2] // 8, projected[0].shape[2] // 2
    tile = (2, block, half)
    flops = 4 * num_rows * block * half

    def to_core(d, early, slot, after):
        kernel = functools.partial(other_core_kernel, early=early, slot=slot, scale=scale)
        out = shaped((4, *tile), F32)
        array = call(kernel, "other_core", out, [xo, d], 4 * flops, after, place)
        return array, swap(array, "dp", 1)

    def both_to_core(d, early, after):
        kernel = functools.partial(other_core_both_kernel, early=early, scale=scale)
        outs = [shaped((4, *tile), F32)] * 2
        arrays = call(kernel, "other_core_both", outs, [xo, d], 8 * flops, after, place)
        return arrays[0], [swap(array, "dp", 1) for array in arrays]

    def first_hop(early, slot, after):
        kernel = functools.partial(first_hop_kernel, early=early, slot=slot, scale=scale)
        out = shaped((2, *tile), F32)
        args = [xo, d, far[early][slot]]
        array = call(kernel, "first_hop", out, args, 2 * flops, after, place)
        return array, hop(array, slot, 0)

    def second_hop(slot, over, after):
        kernel = functools.partial(second_hop_kernel, slot=slot, scale=scale)
        outs = [shaped((2, *tile), F32)] * 2
        args = [xo, d, far[0][slot], far[1][slot], *over]
        keep, leave = call(kernel, "second_hop", outs, args, 4 * flops, after, place)
        return keep, hop(leave, slot, 1)

    early, scores = attend(place, lambda at: at.seq, lambda which: which, projected)
    far = ([None, None], [None, None])
    at, far[0][0] = to_core(early, 0, 0, [])
    at, far[0][1] = to_core(early, 0, 1, [at])
    d = attend(place, lambda at: 1 - at.seq, lambda which: 1 - which, projected, (state, early, scores), [at])
    at, far[1][:] = both_to_core(d, 1, [])
    t3 = term(3, [at])
    t3_in = swap(t3, "head", 1)
    at, over1 = first_hop(0, 0, [t3])
    at, over2 = first_hop(0, 1, [at])
    at, over3 = first_hop(1, 0, [at])
    at, over4 = first_hop(1, 1, [at])
    t2 = term(2, [at])
    t0 = term(0, [t2])
    t1 = term(1, [t0, over1])
    t1_in = swap(t1, "head", 1)
    t2 = add([t2, t3_in], F32, [t1])
    t2_in = swap(t2, "head", 2)
    keep0, moved0 = second_hop(0, (over1, over3), [t2, over2])
    keep1, moved1 = second_hop(1, (over2, over4), [keep0])
    outs = finish(place, (t0, t1_in, t2_in), (keep0, keep1), (moved0, moved1))
    input_grad, grad_query, grad_key, grad_value, grad_out = outs
    return (input_grad[None], grad_query, grad_key, grad_value, grad_out)


def solution(mesh):
    return jax.shard_map(
        local,
        mesh=mesh,
        in_specs=(
            P("dp", "seq", None),
            P(None, "head"),
            P(None, "head"),
            P(None, "head"),
            P("head", None),
            P("dp", "seq", None),
        ),
        out_specs=(
            P("dp", "seq", "head"),
            P(("seq", "dp"), "head"),
            P(("seq", "dp"), "head"),
            P(("seq", "dp"), "head"),
            P("head", ("seq", "dp")),
        ),
        check_vma=False,
    )
```
